32 devices in a mesh: grp: 8 (over z, y), head: 4 (over x, core).
Axes of the slice: x: 2, y: 2, z: 4, core: 2. Of those that a mesh axis runs over, the one named last changes fastest.
Arguments:
- tokens: bfloat16 [4096, 1024], P(('grp', 'head')), may hold values from -6 to 6
- norm_gain: float32 [1024], replicated, may hold values from 0.5 to 1.5
- w_qkv: bfloat16 [1024, 3072], replicated, may hold values from -0.1875 to 0.1875
- w_gates: bfloat16 [1024, 16], replicated, may hold values from -0.1875 to 0.1875
- conv_weight: float32 [4, 3072], replicated, may hold values from -3 to 3
- conv_state: bfloat16 [8, 3, 3072], P('grp'), may hold values from -6 to 6
- decay_rate: float32 [8], replicated, may hold values from 0.0005 to 0.1
- ridge: float32 [8], P('head'), may hold values from 0.25 to 2
- w_out: bfloat16 [1024, 1024], replicated, may hold values from -0.1875 to 0.1875
- cache_keys: bfloat16 [512, 128, 8, 128], P('grp', None, 'head'), may hold values from -0.59765625 to 0.59765625
- cache_values: bfloat16 [512, 128, 8, 128], P('grp', None, 'head'), may hold values from -6 to 6
- page_table: int32 [8, 64], replicated, may hold values from 0 to 511, as said below
- cache_lengths: int32 [8], replicated, may hold values from 1 to 8192, 32768 in all
- group_prompt: int32 [8], replicated, may hold values from 0 to 7
- prompt_state: float32 [8, 8, 2, 128, 128], P('grp', 'head'), may hold values from -8 to 16
Outputs:
- layer_out: bfloat16 [4096, 1024], P(('grp', 'head'))
The draws below stay inside these ranges and needn't reach their ends.
Inputs may be any that keep to these rules, and one draw needn't show every extreme that they name: `page_table`: every pool page is named exactly once in the table; each pool shard of 64 consecutive pages holds exactly 8 pages of every group's requests. `cache_lengths`: some request has exactly 8192 cached tokens.
All inputs are finite; a program needn't handle non-finite values.
Results may differ from the reference program's by a relative error of at most 0.0045.
Values may be sent and summed in bfloat16 or wider, within the bound.
No kernel may reach another device: no remote copies, remote signals or barrier semaphores. Data moves between devices by JAX's collectives and lax.ppermute only.
A program may use at most 128 MiB of HBM per device.

```python
import math
import jax
import jax.numpy as jnp
import numpy as np
from jax import lax

D = 1024
HEADS = 8
HDIM = 128
CONV = 4
NEW = 512
CG_STEPS = 8
PAGE = 128
REQ_GRP = 1
PAGES_MAX = 64
GROUPS = 8
PROMPTS = 8
REQS = 8
TOKENS = 4096
POOL = 512


def draw_page_table(key, part):
    shard_pages = REQ_GRP * PAGES_MAX
    per_group = shard_pages // GROUPS
    key_place, key_local = jax.random.split(key)
    place_keys = jax.random.split(key_place, GROUPS)
    placed = jax.vmap(lambda k: jax.random.permutation(k, shard_pages))(place_keys)
    local_keys = jax.random.split(key_local, GROUPS)
    local_perm = jax.vmap(lambda k: jax.random.permutation(k, shard_pages))(local_keys)
    shard_of = placed // per_group
    group_ids = jnp.arange(GROUPS)[:, None]
    before_perm = group_ids * per_group + placed % per_group
    page_ids = shard_of * shard_pages + local_perm[shard_of, before_perm]
    return page_ids.reshape(REQS, PAGES_MAX).astype(jnp.int32)


def draw_group_prompt(key, part):
    key_pick, key_far = jax.random.split(jax.random.fold_in(key, 71))
    picks = jax.random.randint(key_pick, (GROUPS,), 0, PROMPTS)
    far_group = jax.random.randint(key_far, (), 0, GROUPS)
    group_ids = jnp.arange(GROUPS)
    far_prompt = (group_ids + GROUPS // 2) % PROMPTS
    return jnp.where(group_ids == far_group, far_prompt, picks).astype(jnp.int32)


def draw_prompt_state(key, part):
    key_diag, key_off, key_cross = jax.random.split(key, 3)
    diag_vals = jnp.exp(jax.random.uniform(key_diag, (PROMPTS, HEADS, HDIM), jnp.float32, math.log(5.2), math.log(16.0)))
    off_vals = jax.random.uniform(key_off, (PROMPTS, HEADS, HDIM, HDIM), jnp.float32, -0.04, 0.04)
    off_vals = 0.5 * (off_vals + jnp.swapaxes(off_vals, -1, -2))
    eye_mat = jnp.eye(HDIM, dtype=jnp.float32)
    gram_part = off_vals * (1.0 - eye_mat) + diag_vals[..., None] * eye_mat
    cross_part = jnp.clip(1.5 * jax.random.normal(key_cross, (PROMPTS, HEADS, HDIM, HDIM), jnp.float32), -8.0, 8.0)
    return jnp.stack([gram_part, cross_part], axis=2)


def shard_levels(own_key, shape, pieces, low, high):
    factor_of, own = 1.0, jax.random.fold_in(own_key, 6)
    for dim, blocks in pieces:
        heights = jnp.exp(jax.random.uniform(jax.random.fold_in(own, dim), (blocks,), jnp.float32, low / len(pieces), high / len(pieces)))
        factor_of = factor_of * jnp.repeat(heights, shape[dim] // blocks).reshape([-1 if axis == dim else 1 for axis in range(len(shape))])
    return factor_of


def split_up(number_of, total, bound, skew):
    weights = [(1 << 20) // math.isqrt(rank ** skew) + 1 for rank in range(2, number_of + 1)]
    rest, holding = total - bound - (number_of - 1), [1] * (number_of - 1)
    while rest > 0:
        free = [i for i in range(number_of - 1) if holding[i] < bound]
        mass, budget = sum([weights[i] for i in free]), rest
        for i in free:
            more = min(bound - holding[i], max(1, budget * weights[i] // mass), rest)
            holding[i] = holding[i] + more
            rest = rest - more
    return np.array([bound] + holding)


def ragged(rng, amount, total, limit, slope):
    if amount == 2:
        one = jax.random.randint(rng, (), max(1, total - limit), min(limit, total - 1) + 1)
        return jnp.stack([one, total - one])
    lengths = jnp.asarray(split_up(amount, total, limit, slope), jnp.int32)
    couples = (amount - 1) // 2
    giver, taker = lengths[1:1 + 2 * couples:2], lengths[2:2 + 2 * couples:2]
    room = jnp.minimum(giver - 1, limit - taker)
    moved = jax.random.randint(jax.random.fold_in(rng, 1), (couples,), 0, 1 << 20) % (room + 1)
    lengths = lengths.at[1:1 + 2 * couples:2].set(giver - moved).at[2:2 + 2 * couples:2].set(taker + moved)
    return lengths[jax.random.permutation(jax.random.fold_in(rng, 2), amount)]


def noise(stream_key, shape, scale, limit, cuts=(), held_as=jnp.bfloat16):
    array = scale * jax.random.normal(stream_key, shape, jnp.float32)
    if cuts:
        array = array * shard_levels(stream_key, shape, cuts, -0.22, 0.18)
    return jnp.clip(array, -limit, limit).astype(held_as)


def setup_inputs(seed: int = 0) -> dict:
    key_of = jax.random.split(jax.random.key(seed), 16)
    tokens = noise(key_of[0], (TOKENS, D), 1.0, 6.0, ((0, 32),))
    norm_gain = jnp.clip(1.0 + 0.1 * jax.random.normal(key_of[1], (D,), jnp.float32), 0.5, 1.5)
    w_qkv = noise(key_of[2], (D, 3 * HEADS * HDIM), D ** -0.5, 0.1875)
    w_gates = noise(key_of[3], (D, 2 * HEADS), D ** -0.5, 0.1875)
    conv_weight = noise(key_of[4], (CONV, 3 * HEADS * HDIM), 0.5, 3.0, (), jnp.float32)
    conv_state = noise(key_of[5], (REQS, CONV - 1, 3 * HEADS * HDIM), 1.0, 6.0, ((0, 8),))
    decay_rate = jnp.clip(jnp.exp(jax.random.uniform(key_of[6], (HEADS,), jnp.float32, math.log(0.0005), math.log(0.1))), 0.0005, 0.1)
    ridge = jnp.clip(jnp.exp(math.log(2.0) - 2.0794415 * jax.random.uniform(key_of[7], (HEADS,), jnp.float32) ** shard_levels(key_of[7], (HEADS,), ((0, 4),), -0.2, 0.2)), 0.25, 2.0)
    w_out = noise(key_of[8], (HEADS * HDIM, D), (HEADS * HDIM) ** -0.5, 0.1875)
    cache_keys = noise(key_of[9], (POOL, PAGE, HEADS, HDIM), 0.0884, 0.59765625, ((0, 8), (2, 4)))
    cache_values = noise(key_of[10], (POOL, PAGE, HEADS, HDIM), 1.0, 6.0, ((0, 8), (2, 4)))
    page_table = draw_page_table(jax.random.fold_in(key_of[15], 71), 0)
    cache_lengths = ragged(key_of[12], REQS, REQS * PAGES_MAX * PAGE // 2, PAGES_MAX * PAGE, 2).astype(jnp.int32)
    group_prompt = draw_group_prompt(jax.random.fold_in(key_of[15], 71), 0)
    prompt_state = draw_prompt_state(jax.random.fold_in(key_of[15], 71), 0)
    return {"tokens": tokens, "norm_gain": norm_gain, "w_qkv": w_qkv, "w_gates": w_gates, "conv_weight": conv_weight, "conv_state": conv_state, "decay_rate": decay_rate, "ridge": ridge, "w_out": w_out, "cache_keys": cache_keys, "cache_values": cache_values, "page_table": page_table, "cache_lengths": cache_lengths, "group_prompt": group_prompt, "prompt_state": prompt_state}


PRECISE = lax.Precision.HIGHEST
EPS_NORM = 1e-06

def unit_rows(block):
    return block * lax.rsqrt(lax.optimization_barrier(jnp.sum(block * block, axis=-1, keepdims=True)) + EPS_NORM)

def ridge_read(query, key_rows, value_rows, write_gate, log_gamma, start_gram, start_cross, ridge_add, steps):
    length = query.shape[2]
    positions = jnp.arange(length)
    causal = positions[:, None] >= positions[None, :]
    lower_tri = causal.astype(jnp.float32)
    cumul = jnp.einsum('ts,rhs->rht', lower_tri, log_gamma, precision=PRECISE)
    spread = jnp.where(causal, cumul[..., :, None] - cumul[..., None, :], -jnp.inf)
    weights = jnp.exp(spread) * write_gate[..., None, :]
    carry_scale = jnp.exp(cumul)[..., None]
    ridge_term = ridge_add[None, :, None, None]

    def apply_op(vectors):
        from_start = jnp.einsum('rhte,rhfe->rhtf', vectors, start_gram, precision=PRECISE)
        scores = jnp.einsum('rhte,rhse->rhts', vectors, key_rows, precision=PRECISE) * weights
        return carry_scale * from_start + ridge_term * vectors + jnp.einsum('rhts,rhse->rhte', scores, key_rows, precision=PRECISE)
    solved = jnp.zeros_like(query)
    residue = query
    direction = query
    norm_now = lax.optimization_barrier(jnp.sum(residue * residue, axis=-1, keepdims=True))
    for cg_step in range(steps):
        image = apply_op(direction)
        alpha = norm_now / lax.optimization_barrier(jnp.sum(direction * image, axis=-1, keepdims=True))
        solved = solved + alpha * direction
        residue = residue - alpha * image
        norm_next = lax.optimization_barrier(jnp.sum(residue * residue, axis=-1, keepdims=True))
        direction = residue + norm_next / norm_now * direction
        norm_now = norm_next
    from_start = carry_scale * jnp.einsum('rhte,rhfe->rhtf', solved, start_cross, precision=PRECISE)
    scores = jnp.einsum('rhte,rhse->rhts', solved, key_rows, precision=PRECISE) * weights
    return from_start + jnp.einsum('rhts,rhsf->rhtf', scores, value_rows, precision=PRECISE)

def reference(tokens, norm_gain, w_qkv, w_gates, conv_weight, conv_state, decay_rate, ridge, w_out, cache_keys, cache_values, page_table, cache_lengths, group_prompt, prompt_state):
    tok_total = tokens.shape[0]
    requests = tok_total // NEW
    widened = tokens.astype(jnp.float32)
    normed = (widened * lax.rsqrt(lax.optimization_barrier(jnp.mean(widened * widened, axis=-1, keepdims=True)) + EPS_NORM) * norm_gain).astype(jnp.bfloat16)
    mixed_in = jnp.dot(normed, w_qkv, preferred_element_type=jnp.float32).astype(jnp.bfloat16)
    mixed_in = lax.optimization_barrier(mixed_in)
    gate_logits = jnp.dot(normed, w_gates, preferred_element_type=jnp.float32).reshape(tok_total, HEADS, 2)
    write_gate = jax.nn.sigmoid(gate_logits[..., 0]).astype(jnp.bfloat16)
    log_gamma = (-decay_rate * jax.nn.softplus(gate_logits[..., 1])).astype(jnp.bfloat16)
    write_gate, log_gamma = lax.optimization_barrier((write_gate, log_gamma))
    per_request = mixed_in.reshape(requests, NEW, -1)
    padded = jnp.concatenate([conv_state, per_request], axis=1).astype(jnp.float32)
    conv_sum = conv_weight[CONV - 1] * padded[:, CONV - 1:]
    for lag_step in range(1, CONV):
        conv_sum = conv_sum + conv_weight[CONV - 1 - lag_step] * padded[:, CONV - 1 - lag_step:CONV - 1 - lag_step + NEW]
    conv_sum = conv_sum.reshape(requests, NEW, HEADS, 3, HDIM)
    query = unit_rows(jax.nn.silu(conv_sum[:, :, :, 0]))
    key_vec = unit_rows(jax.nn.silu(conv_sum[:, :, :, 1]))
    value_vec = conv_sum[:, :, :, 2]
    stacked = jnp.stack([query, key_vec, value_vec], axis=3).astype(jnp.bfloat16)
    stacked = lax.optimization_barrier(stacked).astype(jnp.float32)
    stacked = jnp.transpose(stacked, (0, 2, 1, 3, 4))
    gate_pair = jnp.stack([write_gate, log_gamma], axis=-1).astype(jnp.float32).reshape(requests, NEW, HEADS, 2)
    gate_pair = jnp.transpose(gate_pair, (0, 2, 1, 3))
    token_index = jnp.arange(PAGES_MAX * PAGE)

    def one_request(pair):
        pages, length = pair
        key_pages = cache_keys[pages].reshape(PAGES_MAX * PAGE, HEADS, HDIM).astype(jnp.float32)
        value_pages = cache_values[pages].reshape(PAGES_MAX * PAGE, HEADS, HDIM).astype(jnp.float32)
        live = (token_index < length).astype(jnp.float32)[:, None, None]
        key_pages = key_pages * live
        gram = jnp.einsum('the,thf->hef', key_pages, key_pages, precision=PRECISE)
        cross = jnp.einsum('thf,the->hfe', value_pages, key_pages, precision=PRECISE)
        return jnp.stack([gram, cross], axis=1)
    cache_sums = lax.map(one_request, (page_table, cache_lengths))
    group_of = jnp.arange(requests) // REQ_GRP

    def one_read(pair):
        index, block = pair
        state = cache_sums[index] + prompt_state[group_prompt[group_of[index]]]
        gates = gate_pair[index]
        result = ridge_read(block[None, :, :, 0], block[None, :, :, 1], block[None, :, :, 2], gates[None, :, :, 0], gates[None, :, :, 1], state[None, :, 0], state[None, :, 1], ridge, CG_STEPS)
        return result[0].astype(jnp.bfloat16)
    read_out = lax.map(one_read, (jnp.arange(requests), stacked))
    read_out = jnp.transpose(read_out, (0, 2, 1, 3)).reshape(tok_total, HEADS * HDIM)
    attended = jnp.dot(read_out, w_out, preferred_element_type=jnp.float32)
    return (widened + attended).astype(jnp.bfloat16)
```

```python
import functools

import jax
import jax.numpy as jnp
from jax import lax
from jax.experimental import pallas as pl
from jax.experimental.pallas import tpu as pltpu
from jax.sharding import PartitionSpec as P

HEADS = 8
HDIM = 128
CONV = 4
CG_STEPS = 8
PAGE = 128
CHUNK = 128
PAIR = 2 * CHUNK
EPS_NORM = 1e-06
F32 = jnp.float32
BF16 = jnp.bfloat16


def swap(block, axis, distance):
    size = lax.axis_size(axis)
    return lax.ppermute(block, axis, [(i, i ^ distance) for i in range(size)])


def dot(a, b):
    return jnp.dot(a, b, preferred_element_type=F32)


def silu(a):
    return a * jax.nn.sigmoid(a)


def unit_rows(a):
    return a * lax.rsqrt(jnp.sum(a * a, axis=-1, keepdims=True) + EPS_NORM)


def block_diag(a):
    first = lax.broadcasted_iota(jnp.int32, a.shape, 1) < CHUNK
    zero = jnp.zeros_like(a)
    return jnp.concatenate([jnp.where(first, a, zero), jnp.where(first, zero, a)], axis=0)


def gram_kernel(heads, owners, code_ref, meta_ref, pick_ref, keys_ref, values_ref, prompt_ref,
                send_ref, keep_ref, acc_ref):
    step = pl.program_id(0)
    pages, rows = keys_ref.shape[0], keys_ref.shape[1]

    @pl.when(step == 0)
    def _():
        acc_ref[...] = jnp.zeros_like(acc_ref)

    lane = lax.broadcasted_iota(jnp.int32, (HDIM, rows), 1)
    for page in range(pages):
        code = code_ref[step * pages + page]
        owner, live = code // 256, code % 256
        keys = keys_ref[page]
        turned = keys.T
        zero = jnp.zeros_like(turned)
        left = jnp.concatenate(
            [
                jnp.where((lane % heads == head) & (lane < live * heads), turned, zero)
                for head in range(heads)
            ],
            axis=0,
        )
        right = jnp.concatenate([keys, values_ref[page]], axis=1)
        acc_ref[owner] += dot(left, right)

    @pl.when(step == pl.num_programs(0) - 1)
    def _():
        mine, bit = meta_ref[0], meta_ref[1]
        stored = prompt_ref.shape[0]

        def add_prompt(owner, carry):
            for slot in range(stored):

                @pl.when(pick_ref[owner] == mine * stored + slot)
                def _():
                    for head in range(heads):
                        rows_here = slice(head * HDIM, (head + 1) * HDIM)
                        acc_ref[owner, rows_here, :HDIM] += prompt_ref[slot, head, 0].T
                        acc_ref[owner, rows_here, HDIM:] += prompt_ref[slot, head, 1].T

            return carry

        lax.fori_loop(0, owners, add_prompt, 0)
        for pair in range(owners // 2):
            send_ref[pair] = acc_ref[2 * pair + 1 - bit].astype(BF16)
            keep_ref[pair] = acc_ref[2 * pair + bit].astype(BF16)


def page_sums(code, meta, group_prompt, keys, values, prompt_state, owners):
    pool, rows, _ = keys.shape
    heads = prompt_state.shape[1]
    pages = 8
    half = (owners // 2, heads * HDIM, 2 * HDIM)
    page_spec = pl.BlockSpec((pages, rows, HDIM), lambda i, *_: (i, 0, 0))
    out_spec = pl.BlockSpec(half, lambda i, *_: (0, 0, 0))
    return pl.pallas_call(
        functools.partial(gram_kernel, heads, owners),
        grid_spec=pltpu.PrefetchScalarGridSpec(
            num_scalar_prefetch=3,
            grid=(pool // pages,),
            in_specs=[
                page_spec,
                page_spec,
                pl.BlockSpec(prompt_state.shape, lambda i, *_: (0, 0, 0, 0, 0)),
            ],
            out_specs=[out_spec, out_spec],
            scratch_shapes=[pltpu.VMEM((owners, heads * HDIM, 2 * HDIM), F32)],
        ),
        out_shape=[jax.ShapeDtypeStruct(half, BF16)] * 2,
        compiler_params=pltpu.CompilerParams(vmem_limit_bytes=32 * 2**20),
        cost_estimate=pl.CostEstimate(
            flops=2 * pool * rows * heads * HDIM * 2 * HDIM,
            bytes_accessed=4 * pool * rows * HDIM,
            transcendentals=0,
        ),
        name="page_sums",
    )(code, meta, group_prompt, keys, values, prompt_state)


def halve_kernel(meta_ref, keep_ref, got_ref, *outs):
    for distance, out_ref in enumerate(outs):
        row = meta_ref[2] ^ distance
        total = keep_ref[row].astype(F32) + got_ref[row].astype(F32)
        out_ref[...] = total.astype(out_ref.dtype)


def halve_sums(meta, keep, got):
    count, rows, cols = keep.shape
    outs = [jax.ShapeDtypeStruct((rows, cols), F32 if i == 0 else BF16) for i in range(count)]
    whole = pl.BlockSpec(memory_space=pltpu.VMEM)
    return pl.pallas_call(
        halve_kernel,
        in_specs=[pl.BlockSpec(memory_space=pltpu.SMEM), whole, whole],
        out_specs=[whole] * count,
        out_shape=outs,
        compiler_params=pltpu.CompilerParams(vmem_limit_bytes=32 * 2**20),
        cost_estimate=pl.CostEstimate(
            flops=count * rows * cols, bytes_accessed=6 * count * rows * cols, transcendentals=0
        ),
        name="halve_sums",
    )(meta, keep, got)


def token_kernel(heads, place_ref, rate_ref, *refs):
    head_count = HEADS // heads
    blocks = refs[:head_count]
    (gain_ref, w_ref, wg_ref, taps_ref, state_ref) = refs[head_count : head_count + 5]
    (q_ref, k_ref, kt_ref, vt_ref, weight_ref, prefix_ref, rows_ref) = refs[head_count + 5 : -2]
    ext_ref, gate_ref = refs[-2:]
    me = place_ref[0]
    tok_rows = blocks[0].shape[0]
    length = tok_rows * head_count
    chunks = length // CHUNK
    base = 8
    ext_ref[base - (CONV - 1) : base, :] = state_ref[0].astype(F32)
    gate_ref[...] = jnp.zeros_like(gate_ref)
    for distance, block in enumerate(blocks):
        first = pl.multiple_of((me ^ distance) * tok_rows, tok_rows)
        wide = block[...].astype(F32)
        scale = lax.rsqrt(jnp.mean(wide * wide, axis=-1, keepdims=True) + EPS_NORM)
        normed = (wide * scale * gain_ref[...]).astype(BF16)
        mixed = dot(normed, w_ref[...]).astype(BF16)
        ext_ref[pl.ds(pl.multiple_of(base + first, 8), tok_rows), :] = mixed.astype(F32)
        gate_ref[pl.ds(first, tok_rows), : 2 * HEADS] = dot(normed, wg_ref[...])

    shift = lax.rem(HDIM - 2 * heads * me, HDIM)
    logits = pltpu.roll(gate_ref[...], shift, 1)
    lane = lax.broadcasted_iota(jnp.int32, (1, HDIM), 1)
    rate = jnp.zeros((1, HDIM), F32)
    for head in range(heads):
        rate = jnp.where(lane == 2 * head + 1, rate_ref[me * heads + head], rate)
    write = jax.nn.sigmoid(logits).astype(BF16).astype(F32)
    soft = jnp.maximum(logits, 0.0) + jnp.log1p(jnp.exp(-jnp.abs(logits)))
    decay = (-rate * soft).astype(BF16)
    here = lax.broadcasted_iota(jnp.int32, (CHUNK, CHUNK), 0)
    there = lax.broadcasted_iota(jnp.int32, (CHUNK, CHUNK), 1)
    lower = (here >= there).astype(F32).astype(BF16)
    cumul = [dot(lower, decay[c * CHUNK : (c + 1) * CHUNK]) for c in range(chunks)]
    turned = [block.T for block in cumul]

    for head in range(heads):
        parts = []
        for part in range(3):
            cols = slice((3 * head + part) * HDIM, (3 * head + part + 1) * HDIM)
            total = taps_ref[CONV - 1 : CONV, cols] * ext_ref[base : base + length, cols]
            for lag in range(1, CONV):
                total = total + taps_ref[CONV - 1 - lag : CONV - lag, cols] * (
                    ext_ref[base - lag : base - lag + length, cols]
                )
            parts.append(total)
        query = unit_rows(silu(parts[0])).astype(BF16)
        key = unit_rows(silu(parts[1])).astype(BF16)
        value = parts[2].astype(BF16)
        q_ref[head] = query.T
        k_ref[head] = key
        kt_ref[head] = key.T
        vt_ref[head] = value.T
        prefix = jnp.zeros((HDIM, 2 * HDIM), F32)
        so_far = jnp.zeros((1, 1), F32)
        for c in range(chunks):
            rows = slice(c * CHUNK, (c + 1) * CHUNK)
            col = cumul[c][:, 2 * head + 1 : 2 * head + 2]
            row = turned[c][2 * head + 1 : 2 * head + 2, :]
            gate = write[rows, 2 * head : 2 * head + 1]
            spread = jnp.exp(jnp.minimum(row - col, 0.0)) * gate
            half = slice((c % 2) * CHUNK, (c % 2 + 1) * CHUNK)
            weight_ref[head, c // 2, :, half] = jnp.where(here <= there, spread, 0.0)
            rows_ref[head, c // 2, 0:1, half] = jnp.exp(row)
            rows_ref[head, c // 2, 1:2, half] = jnp.broadcast_to(jnp.exp(so_far), (1, CHUNK))
            prefix_ref[head, c, :HDIM] = prefix[:, :HDIM]
            prefix_ref[head, c, HDIM:] = prefix[:, HDIM:].T
            if c + 1 < chunks:
                whole = cumul[c][CHUNK - 1 :, 2 * head + 1 : 2 * head + 2]
                carry = jnp.exp(whole - col) * gate
                both = jnp.concatenate([key[rows], value[rows]], axis=1).astype(F32)
                prefix = prefix * jnp.exp(whole) + dot(
                    kt_ref[head, :, rows], (both * carry).astype(BF16)
                )
                so_far = so_far + whole


def token_vectors(place, decay_rate, blocks, norm_gain, w_qkv, w_gates, conv_weight, conv_state):
    head_count = len(blocks)
    heads = HEADS // head_count
    width = heads * 3 * HDIM
    tok_rows, model = blocks[0].shape
    length = head_count * tok_rows
    chunks = length // CHUNK

    def full(shape):
        return pl.BlockSpec(shape, lambda i, *_: (0,) * len(shape))

    outs = [
        jax.ShapeDtypeStruct((heads, HDIM, length), BF16),
        jax.ShapeDtypeStruct((heads, length, HDIM), BF16),
        jax.ShapeDtypeStruct((heads, HDIM, length), BF16),
        jax.ShapeDtypeStruct((heads, HDIM, length), BF16),
        jax.ShapeDtypeStruct((heads, chunks // 2, CHUNK, PAIR), F32),
        jax.ShapeDtypeStruct((heads, chunks, 2 * HDIM, HDIM), F32),
        jax.ShapeDtypeStruct((heads, chunks // 2, 8, PAIR), F32),
    ]
    return pl.pallas_call(
        functools.partial(token_kernel, heads),
        grid_spec=pltpu.PrefetchScalarGridSpec(
            num_scalar_prefetch=2,
            grid=(1,),
            in_specs=[full(b.shape) for b in blocks]
            + [
                full((1, model)),
                pl.BlockSpec((model, width), lambda i, place, rate: (0, place[0])),
                full(w_gates.shape),
                pl.BlockSpec((CONV, width), lambda i, place, rate: (0, place[0])),
                pl.BlockSpec((1, CONV - 1, width), lambda i, place, rate: (0, 0, place[0])),
            ],
            out_specs=[full(o.shape) for o in outs],
            scratch_shapes=[pltpu.VMEM((8 + length, width), F32), pltpu.VMEM((length, HDIM), F32)],
        ),
        out_shape=outs,
        compiler_params=pltpu.CompilerParams(vmem_limit_bytes=40 * 2**20),
        cost_estimate=pl.CostEstimate(
            flops=2 * length * model * width,
            bytes_accessed=2 * model * (length + width) + 4 * 2**20,
            transcendentals=length * width,
        ),
        name="token_vectors",
    )(place, decay_rate, *blocks, norm_gain.reshape(1, model), w_qkv, w_gates, conv_weight, conv_state)


def read_kernel(heads, terms, place_ref, ridge_ref, *refs):
    head_count = HEADS // heads
    sums = refs[:terms]
    (q_ref, k_ref, kt_ref, vt_ref, weight_ref, prefix_ref, rows_ref) = refs[terms : terms + 7]
    outs = refs[terms + 7 : terms + 7 + head_count]
    left_ref, cross_ref, x_ref, r_ref, d_ref, o_ref = refs[terms + 7 + head_count :]
    me = place_ref[0]
    pairs = q_ref.shape[2] // PAIR
    groups = [(head, pair) for head in range(heads) for pair in range(pairs)]
    norms = []
    for head in range(heads):
        rows = slice(head * HDIM, (head + 1) * HDIM)
        total = sums[0][rows, :].astype(F32)
        for term in sums[1:]:
            total = total + term[rows, :].astype(F32)
        gram, cross = total[:, :HDIM].T, total[:, HDIM:].T
        for pair in range(pairs):
            for side in range(2):
                c = 2 * pair + side
                half = slice(side * CHUNK, (side + 1) * CHUNK)
                scale = rows_ref[head, pair, 1:2, half]
                left_ref[head, pair, :HDIM, half] = (
                    gram * scale + prefix_ref[head, c, :HDIM]
                ).astype(BF16)
                left_ref[head, pair, HDIM:, half] = k_ref[head, c * CHUNK : (c + 1) * CHUNK]
                cross_ref[head, pair, :, half] = (
                    cross * scale + prefix_ref[head, c, HDIM:]
                ).astype(BF16)
            query = q_ref[head, :, pair * PAIR : (pair + 1) * PAIR].astype(F32)
            x_ref[head, pair] = jnp.zeros_like(query)
            r_ref[head, pair] = query
            d_ref[head, pair] = query
            norms.append(jnp.sum(query * query, axis=0, keepdims=True))

    def one_step(_, norms):
        firsts = [dot(left_ref[g], block_diag(d_ref[g].astype(BF16))) for g in groups]
        seconds = []
        for (head, pair), first in zip(groups, firsts):
            scores = (first[HDIM:] * weight_ref[head, pair]).astype(BF16)
            seconds.append(
                dot(kt_ref[head, :, pair * PAIR : (pair + 1) * PAIR], block_diag(scores))
            )
        later = []
        for (head, pair), first, second, norm in zip(groups, firsts, seconds, norms):
            direction = d_ref[head, pair]
            image = (
                rows_ref[head, pair, 0:1] * first[:HDIM] + ridge_ref[head] * direction + second
            )
            alpha = norm / jnp.sum(direction * image, axis=0, keepdims=True)
            x_ref[head, pair] += alpha * direction
            residue = r_ref[head, pair] - alpha * image
            r_ref[head, pair] = residue
            norm_next = jnp.sum(residue * residue, axis=0, keepdims=True)
            d_ref[head, pair] = residue + norm_next / norm * direction
            later.append(norm_next)
        return tuple(later)

    lax.fori_loop(0, CG_STEPS, one_step, tuple(norms))
    for head, pair in groups:
        left_ref[head, pair, :HDIM] = cross_ref[head, pair]
        first = dot(left_ref[head, pair], block_diag(x_ref[head, pair].astype(BF16)))
        scores = (first[HDIM:] * weight_ref[head, pair]).astype(BF16)
        span = slice(pair * PAIR, (pair + 1) * PAIR)
        read = rows_ref[head, pair, 0:1] * first[:HDIM] + dot(
            vt_ref[head, :, span], block_diag(scores)
        )
        o_ref[span, head * HDIM : (head + 1) * HDIM] = read.T.astype(BF16)
    tok_rows = outs[0].shape[0]
    for distance, out_ref in enumerate(outs):
        first_row = pl.multiple_of((me ^ distance) * tok_rows, tok_rows)
        out_ref[...] = o_ref[pl.ds(first_row, tok_rows), :]


def ridge_reads(place, ridge, sums, vectors, head_count):
    heads = HEADS // head_count
    length = vectors[0].shape[2]
    pairs = length // PAIR
    tok_rows = length // head_count
    whole = pl.BlockSpec(memory_space=pltpu.VMEM)
    small = pl.BlockSpec(memory_space=pltpu.SMEM)
    state = pltpu.VMEM((heads, pairs, HDIM, PAIR), F32)
    return pl.pallas_call(
        functools.partial(read_kernel, heads, len(sums)),
        in_specs=[small, small] + [whole] * (len(sums) + len(vectors)),
        out_specs=[whole] * head_count,
        out_shape=[jax.ShapeDtypeStruct((tok_rows, heads * HDIM), BF16)] * head_count,
        scratch_shapes=[
            pltpu.VMEM((heads, pairs, 2 * HDIM, PAIR), BF16),
            pltpu.VMEM((heads, pairs, HDIM, PAIR), BF16),
            state,
            state,
            state,
            pltpu.VMEM((length, heads * HDIM), BF16),
        ],
        compiler_params=pltpu.CompilerParams(vmem_limit_bytes=32 * 2**20),
        cost_estimate=pl.CostEstimate(
            flops=CG_STEPS * heads * pairs * 6 * CHUNK**3 * 4,
            bytes_accessed=4 * 2**20,
            transcendentals=0,
        ),
        name="ridge_reads",
    )(place, ridge, *sums, *vectors)


def output_kernel(place_ref, tokens_ref, w_ref, *refs):
    out_ref = refs[-1]
    me = place_ref[0]
    total = tokens_ref[...].astype(F32)
    for distance, part in enumerate(refs[:-1]):
        width = part.shape[1]
        first = pl.multiple_of((me ^ distance) * width, width)
        total = total + dot(part[...], w_ref[pl.ds(first, width), :])
    out_ref[...] = total.astype(BF16)


def output_rows(place, tokens, w_out, reads):
    whole = pl.BlockSpec(memory_space=pltpu.VMEM)
    return pl.pallas_call(
        output_kernel,
        in_specs=[pl.BlockSpec(memory_space=pltpu.SMEM)] + [whole] * (2 + len(reads)),
        out_specs=whole,
        out_shape=jax.ShapeDtypeStruct(tokens.shape, BF16),
        compiler_params=pltpu.CompilerParams(vmem_limit_bytes=24 * 2**20),
        cost_estimate=pl.CostEstimate(
            flops=2 * tokens.shape[0] * w_out.shape[0] * w_out.shape[1],
            bytes_accessed=2 * w_out.size + 6 * tokens.size,
            transcendentals=0,
        ),
        name="output_rows",
    )(place, tokens, w_out, *reads)


def shards(
    tokens,
    norm_gain,
    w_qkv,
    w_gates,
    conv_weight,
    conv_state,
    decay_rate,
    ridge,
    w_out,
    cache_keys,
    cache_values,
    page_table,
    cache_lengths,
    group_prompt,
    prompt_state,
):
    head_count = lax.axis_size("head")
    owners = lax.axis_size("grp")
    me = lax.axis_index("head").astype(jnp.int32)
    group = lax.axis_index("grp").astype(jnp.int32)
    place = me.reshape(1)
    meta = jnp.stack([group, group % 2, group // 2])

    blocks = {0: tokens}
    bit = head_count // 2
    while bit:
        for held in list(blocks):
            blocks[held ^ bit] = swap(blocks[held], "head", bit)
        bit //= 2
    blocks = [blocks[i] for i in range(head_count)]

    pool, page, heads, _ = cache_keys.shape
    ids = group * pool + jnp.arange(pool, dtype=jnp.int32)
    slots = page_table.shape[1]
    live = jnp.clip(cache_lengths[:, None] - jnp.arange(slots, dtype=jnp.int32) * PAGE, 0, PAGE)
    tag = jnp.arange(owners, dtype=jnp.int32)[:, None] * 256 + live
    code = jnp.sum(
        jnp.where(page_table[:, :, None] == ids, tag[:, :, None], 0), axis=(0, 1), dtype=jnp.int32
    )
    send, keep = page_sums(
        code,
        meta,
        group_prompt,
        cache_keys.reshape(pool, page * heads, HDIM),
        cache_values.reshape(pool, page * heads, HDIM),
        prompt_state,
        owners,
    )
    got = swap(send, "grp", 1)
    vectors = token_vectors(
        place, decay_rate, blocks, norm_gain, w_qkv, w_gates, conv_weight, conv_state
    )
    sums = halve_sums(meta, keep, got)
    sums = [sums[0]] + [swap(sums[i], "grp", 2 * i) for i in range(1, owners // 2)]
    reads = ridge_reads(place, ridge, sums, vectors, head_count)
    reads = [reads[0]] + [swap(reads[i], "head", i) for i in range(1, head_count)]
    return output_rows(place, tokens, w_out, reads)


def solution(mesh):
    placed = (
        P(("grp", "head"), None),
        P(),
        P(),
        P(),
        P(),
        P("grp", None, None),
        P(),
        P("head"),
        P(),
        P("grp", None, "head", None),
        P("grp", None, "head", None),
        P(),
        P(),
        P(),
        P("grp", "head", None, None, None),
    )
    return jax.shard_map(
        shards, mesh=mesh, in_specs=placed, out_specs=P(("grp", "head"), None), check_vma=False
    )
```

```python
import functools

import jax
import jax.numpy as jnp
from jax import lax
from jax.experimental import pallas as pl
from jax.experimental.pallas import tpu as pltpu
from jax.sharding import PartitionSpec as P

HEADS = 8
HDIM = 128
CONV = 4
CG_STEPS = 8
PAGE = 128
CHUNK = 128
PAIR = 2 * CHUNK
EPS_NORM = 1e-06
PAGE_VMEM = 50
TOKEN_VMEM = 48
F32 = jnp.float32
BF16 = jnp.bfloat16


def swap(block, axis, distance):
    size = lax.axis_size(axis)
    return lax.ppermute(block, axis, [(i, i ^ distance) for i in range(size)])


def dot(a, b):
    return jnp.dot(a, b, preferred_element_type=F32)


def silu(a):
    return a * jax.nn.sigmoid(a)


def unit_rows(a):
    return a * lax.rsqrt(jnp.sum(a * a, axis=-1, keepdims=True) + EPS_NORM)


def block_diag(a):
    zero = jnp.zeros((a.shape[0], CHUNK), a.dtype)
    return jnp.concatenate(
        [
            jnp.concatenate([a[:, :CHUNK], zero], axis=1),
            jnp.concatenate([zero, a[:, CHUNK:]], axis=1),
        ],
        axis=0,
    )


def sums_kernel(heads, owners, slots, cross, code_ref, meta_ref, *refs):
    keys_ref, right_ref, prompt_ref = refs[0], refs[1 if cross else 0], refs[2 if cross else 1]
    send_ref, keep_ref, acc_ref = refs[-3:]
    step = pl.program_id(0)
    pages, rows = keys_ref.shape[0], keys_ref.shape[1]

    @pl.when(step == 0)
    def _():
        acc_ref[...] = jnp.zeros_like(acc_ref)

    lane = lax.broadcasted_iota(jnp.int32, (1, rows), 1)
    for page in range(pages):
        code = code_ref[step * pages + page]
        owner, slot = code // slots, code % slots
        live = jnp.clip(meta_ref[3 + owners + owner] - slot * PAGE, 0, PAGE)
        turned = keys_ref[page].T
        left = []
        for head in range(heads):
            mask = (lane % heads == head) & (lane < live * heads)
            left.append(turned * mask.astype(F32).astype(BF16))
        acc_ref[owner] += dot(jnp.concatenate(left, axis=0), right_ref[page])

    @pl.when(step == pl.num_programs(0) - 1)
    def _():
        mine, bit = meta_ref[0], meta_ref[1]
        stored = prompt_ref.shape[0]

        def add_prompt(owner, carry):
            for slot in range(stored):

                @pl.when(meta_ref[3 + owner] == mine * stored + slot)
                def _():
                    for head in range(heads):
                        block = prompt_ref[slot, head, 0]
                        acc_ref[owner, head * HDIM : (head + 1) * HDIM, :] += (
                            block.T if cross else block
                        )

            return carry

        lax.fori_loop(0, owners, add_prompt, 0)
        for pair in range(owners // 2):
            send_ref[pair] = acc_ref[2 * pair + 1 - bit].astype(BF16)
            keep_ref[pair] = acc_ref[2 * pair + bit].astype(BF16)


def page_sums(code, meta, keys, values, prompt_state, owners, slots, after=()):
    cross = values is not None
    pool, rows, _ = keys.shape
    stored, heads = prompt_state.shape[:2]
    pages = 8
    half = (owners // 2, heads * HDIM, HDIM)
    page_spec = pl.BlockSpec((pages, rows, HDIM), lambda i, *_: (i, 0, 0))
    out_spec = pl.BlockSpec(half, lambda i, *_: (0, 0, 0))
    blocks = [keys, values] if cross else [keys]
    touch = pl.BlockSpec((16, HDIM), lambda i, *_: (0, 0))
    return pl.pallas_call(
        functools.partial(sums_kernel, heads, owners, slots, cross),
        grid_spec=pltpu.PrefetchScalarGridSpec(
            num_scalar_prefetch=2,
            grid=(pool // pages,),
            in_specs=[page_spec] * len(blocks)
            + [
                pl.BlockSpec(
                    (stored, heads, 1, HDIM, HDIM), lambda i, *_: (0, 0, int(cross), 0, 0)
                )
            ]
            + [touch] * len(after),
            out_specs=[out_spec, out_spec],
            scratch_shapes=[pltpu.VMEM((owners, heads * HDIM, HDIM), F32)],
        ),
        out_shape=[jax.ShapeDtypeStruct(half, BF16)] * 2,
        compiler_params=pltpu.CompilerParams(vmem_limit_bytes=PAGE_VMEM * 2**20),
        cost_estimate=pl.CostEstimate(
            flops=4 * pool * rows * heads * HDIM * HDIM,
            bytes_accessed=2 * len(blocks) * pool * rows * HDIM,
            transcendentals=0,
        ),
        name="cross_sums" if cross else "gram_sums",
    )(code, meta, *blocks, prompt_state, *after)


def halve_kernel(meta_ref, keep_ref, got_ref, *outs):
    for distance, out_ref in enumerate(outs):
        row = meta_ref[2] ^ distance
        total = keep_ref[row].astype(F32) + got_ref[row].astype(F32)
        out_ref[...] = total.astype(out_ref.dtype)


def halve_sums(meta, keep, got):
    count, rows, cols = keep.shape
    outs = [jax.ShapeDtypeStruct((rows, cols), F32 if i == 0 else BF16) for i in range(count)]
    whole = pl.BlockSpec(memory_space=pltpu.VMEM)
    return pl.pallas_call(
        halve_kernel,
        in_specs=[pl.BlockSpec(memory_space=pltpu.SMEM), whole, whole],
        out_specs=[whole] * count,
        out_shape=outs,
        compiler_params=pltpu.CompilerParams(vmem_limit_bytes=32 * 2**20),
        cost_estimate=pl.CostEstimate(
            flops=count * rows * cols, bytes_accessed=6 * count * rows * cols, transcendentals=0
        ),
        name="halve_sums",
    )(meta, keep, got)


def token_kernel(heads, place_ref, rate_ref, *refs):
    head_count = HEADS // heads
    blocks = refs[:head_count]
    (gain_ref, w_ref, wg_ref, taps_ref, state_ref) = refs[head_count : head_count + 5]
    (q_ref, k_ref, kt_ref, vt_ref, weight_ref, prefix_ref, rows_ref) = refs[-9:-2]
    ext_ref, gate_ref = refs[-2:]
    me = place_ref[0]
    tok_rows = blocks[0].shape[0]
    length = tok_rows * head_count
    chunks = length // CHUNK
    base = 8
    ext_ref[base - (CONV - 1) : base, :] = state_ref[0].astype(F32)
    gate_ref[...] = jnp.zeros_like(gate_ref)
    for distance, block in enumerate(blocks):
        first = pl.multiple_of((me ^ distance) * tok_rows, tok_rows)
        wide = block[...].astype(F32)
        scale = lax.rsqrt(jnp.mean(wide * wide, axis=-1, keepdims=True) + EPS_NORM)
        normed = (wide * scale * gain_ref[...]).astype(BF16)
        mixed = dot(normed, w_ref[...]).astype(BF16)
        ext_ref[pl.ds(pl.multiple_of(base + first, 8), tok_rows), :] = mixed.astype(F32)
        gate_ref[pl.ds(first, tok_rows), : 2 * HEADS] = dot(normed, wg_ref[...])

    shift = lax.rem(HDIM - 2 * heads * me, HDIM)
    logits = pltpu.roll(gate_ref[...], shift, 1)
    lane = lax.broadcasted_iota(jnp.int32, (1, HDIM), 1)
    rate = jnp.zeros((1, HDIM), F32)
    for head in range(heads):
        rate = jnp.where(lane == 2 * head + 1, rate_ref[me * heads + head], rate)
    write = jax.nn.sigmoid(logits).astype(BF16).astype(F32)
    soft = jnp.maximum(logits, 0.0) + jnp.log1p(jnp.exp(-jnp.abs(logits)))
    decay = (-rate * soft).astype(BF16)
    here = lax.broadcasted_iota(jnp.int32, (CHUNK, CHUNK), 0)
    there = lax.broadcasted_iota(jnp.int32, (CHUNK, CHUNK), 1)
    lower = (here >= there).astype(F32).astype(BF16)
    cumul = [dot(lower, decay[c * CHUNK : (c + 1) * CHUNK]) for c in range(chunks)]
    turned = [block.T for block in cumul]

    for head in range(heads):
        parts = []
        for part in range(3):
            cols = slice((3 * head + part) * HDIM, (3 * head + part + 1) * HDIM)
            total = taps_ref[CONV - 1 : CONV, cols] * ext_ref[base : base + length, cols]
            for lag in range(1, CONV):
                total = total + taps_ref[CONV - 1 - lag : CONV - lag, cols] * (
                    ext_ref[base - lag : base - lag + length, cols]
                )
            parts.append(total)
        query = unit_rows(silu(parts[0])).astype(BF16)
        key = unit_rows(silu(parts[1])).astype(BF16)
        value = parts[2].astype(BF16)
        q_ref[head] = query.T
        k_ref[head] = key
        kt_ref[head] = key.T
        vt_ref[head] = value.T
        prefix = jnp.zeros((HDIM, 2 * HDIM), F32)
        so_far = jnp.zeros((1, 1), F32)
        for c in range(chunks):
            rows = slice(c * CHUNK, (c + 1) * CHUNK)
            col = cumul[c][:, 2 * head + 1 : 2 * head + 2]
            row = turned[c][2 * head + 1 : 2 * head + 2, :]
            gate = write[rows, 2 * head : 2 * head + 1]
            spread = jnp.exp(jnp.minimum(row - col, 0.0)) * gate
            half = slice((c % 2) * CHUNK, (c % 2 + 1) * CHUNK)
            weight_ref[head, c // 2, :, half] = jnp.where(here <= there, spread, 0.0)
            rows_ref[head, c // 2, 0:1, half] = jnp.exp(row)
            rows_ref[head, c // 2, 1:2, half] = jnp.broadcast_to(jnp.exp(so_far), (1, CHUNK))
            prefix_ref[head, c, :HDIM] = prefix[:, :HDIM]
            prefix_ref[head, c, HDIM:] = prefix[:, HDIM:].T
            if c + 1 < chunks:
                whole = cumul[c][CHUNK - 1 :, 2 * head + 1 : 2 * head + 2]
                carry = jnp.exp(whole - col) * gate
                both = jnp.concatenate([key[rows], value[rows]], axis=1).astype(F32)
                prefix = prefix * jnp.exp(whole) + dot(
                    kt_ref[head, :, rows], (both * carry).astype(BF16)
                )
                so_far = so_far + whole


def token_vectors(
    place, decay_rate, blocks, norm_gain, w_qkv, w_gates, conv_weight, conv_state, after=()
):
    head_count = len(blocks)
    heads = HEADS // head_count
    width = heads * 3 * HDIM
    tok_rows, model = blocks[0].shape
    length = head_count * tok_rows
    chunks = length // CHUNK

    touch = pl.BlockSpec((16, HDIM), lambda i, *_: (0, 0))

    def full(shape):
        return pl.BlockSpec(shape, lambda i, *_: (0,) * len(shape))

    outs = [
        jax.ShapeDtypeStruct((heads, HDIM, length), BF16),
        jax.ShapeDtypeStruct((heads, length, HDIM), BF16),
        jax.ShapeDtypeStruct((heads, HDIM, length), BF16),
        jax.ShapeDtypeStruct((heads, HDIM, length), BF16),
        jax.ShapeDtypeStruct((heads, chunks // 2, CHUNK, PAIR), F32),
        jax.ShapeDtypeStruct((heads, chunks, 2 * HDIM, HDIM), F32),
        jax.ShapeDtypeStruct((heads, chunks // 2, 8, PAIR), F32),
    ]
    return pl.pallas_call(
        functools.partial(token_kernel, heads),
        grid_spec=pltpu.PrefetchScalarGridSpec(
            num_scalar_prefetch=2,
            grid=(1,),
            in_specs=[full(b.shape) for b in blocks]
            + [
                full((1, model)),
                pl.BlockSpec((model, width), lambda i, place, rate: (0, place[0])),
                full(w_gates.shape),
                pl.BlockSpec((CONV, width), lambda i, place, rate: (0, place[0])),
                pl.BlockSpec((1, CONV - 1, width), lambda i, place, rate: (0, 0, place[0])),
            ]
            + [touch] * len(after),
            out_specs=[full(o.shape) for o in outs],
            scratch_shapes=[pltpu.VMEM((8 + length, width), F32), pltpu.VMEM((length, HDIM), F32)],
        ),
        out_shape=outs,
        compiler_params=pltpu.CompilerParams(vmem_limit_bytes=TOKEN_VMEM * 2**20),
        cost_estimate=pl.CostEstimate(
            flops=2 * length * model * width,
            bytes_accessed=2 * model * (length + width) + 4 * 2**20,
            transcendentals=length * width,
        ),
        name="token_vectors",
    )(
        place,
        decay_rate,
        *blocks,
        norm_gain.reshape(1, model),
        w_qkv,
        w_gates,
        conv_weight,
        conv_state,
        *after,
    )


def read_kernel(heads, terms, ridge_ref, *refs):
    grams = refs[:terms]
    (q_ref, k_ref, kt_ref, vt_ref, weight_ref, prefix_ref, rows_ref) = refs[terms : terms + 7]
    base_ref, solved_ref, left_ref, x_ref, r_ref, d_ref = refs[-6:]
    pairs = q_ref.shape[2] // PAIR
    groups = [(head, pair) for head in range(heads) for pair in range(pairs)]
    norms = []
    for head in range(heads):
        rows = slice(head * HDIM, (head + 1) * HDIM)
        gram = grams[0][rows, :].astype(F32)
        for term in grams[1:]:
            gram = gram + term[rows, :].astype(F32)
        for pair in range(pairs):
            for side in range(2):
                c = 2 * pair + side
                half = slice(side * CHUNK, (side + 1) * CHUNK)
                scale = rows_ref[head, pair, 1:2, half]
                left_ref[head, pair, :HDIM, half] = (
                    gram * scale + prefix_ref[head, c, :HDIM]
                ).astype(BF16)
                left_ref[head, pair, HDIM:, half] = k_ref[head, c * CHUNK : (c + 1) * CHUNK]
            query = q_ref[head, :, pair * PAIR : (pair + 1) * PAIR].astype(F32)
            x_ref[head, pair] = jnp.zeros_like(query)
            r_ref[head, pair] = query
            d_ref[head, pair] = query
            norms.append(jnp.sum(query * query, axis=0, keepdims=True))

    def one_step(_, norms):
        firsts = [dot(left_ref[g], block_diag(d_ref[g].astype(BF16))) for g in groups]
        seconds = []
        for (head, pair), first in zip(groups, firsts):
            scores = (first[HDIM:] * weight_ref[head, pair]).astype(BF16)
            seconds.append(
                dot(kt_ref[head, :, pair * PAIR : (pair + 1) * PAIR], block_diag(scores))
            )
        later = []
        for (head, pair), first, second, norm in zip(groups, firsts, seconds, norms):
            direction = d_ref[head, pair]
            image = (
                rows_ref[head, pair, 0:1] * first[:HDIM] + ridge_ref[head] * direction + second
            )
            alpha = norm / jnp.sum(direction * image, axis=0, keepdims=True)
            x_ref[head, pair] += alpha * direction
            residue = r_ref[head, pair] - alpha * image
            r_ref[head, pair] = residue
            norm_next = jnp.sum(residue * residue, axis=0, keepdims=True)
            d_ref[head, pair] = residue + norm_next / norm * direction
            later.append(norm_next)
        return tuple(later)

    lax.fori_loop(0, CG_STEPS, one_step, tuple(norms))
    for head, pair in groups:
        cols = slice(head * HDIM, (head + 1) * HDIM)
        span = slice(pair * PAIR, (pair + 1) * PAIR)
        for side in range(2):
            half = slice(side * CHUNK, (side + 1) * CHUNK)
            left_ref[head, pair, :HDIM, half] = prefix_ref[head, 2 * pair + side, HDIM:].astype(BF16)
        solved = x_ref[head, pair]
        first = dot(left_ref[head, pair], block_diag(solved.astype(BF16)))
        scores = (first[HDIM:] * weight_ref[head, pair]).astype(BF16)
        carry = rows_ref[head, pair, 0:1]
        read = carry * first[:HDIM] + dot(vt_ref[head, :, span], block_diag(scores))
        base_ref[span, cols] = read.T
        solved_ref[span, cols] = (solved * (carry * rows_ref[head, pair, 1:2])).T.astype(BF16)


def ridge_reads(ridge, grams, vectors, after=()):
    heads, _, length = vectors[0].shape
    pairs = length // PAIR
    whole = pl.BlockSpec(memory_space=pltpu.VMEM)
    state = pltpu.VMEM((heads, pairs, HDIM, PAIR), F32)
    return pl.pallas_call(
        functools.partial(read_kernel, heads, len(grams)),
        in_specs=[pl.BlockSpec(memory_space=pltpu.SMEM)]
        + [whole] * (len(grams) + len(vectors))
        + [whole] * len(after),
        out_specs=[whole] * 2,
        out_shape=[
            jax.ShapeDtypeStruct((length, heads * HDIM), F32),
            jax.ShapeDtypeStruct((length, heads * HDIM), BF16),
        ],
        scratch_shapes=[pltpu.VMEM((heads, pairs, 2 * HDIM, PAIR), BF16), state, state, state],
        compiler_params=pltpu.CompilerParams(vmem_limit_bytes=32 * 2**20),
        cost_estimate=pl.CostEstimate(
            flops=CG_STEPS * heads * pairs * 6 * CHUNK**3 * 16,
            bytes_accessed=8 * 2**20,
            transcendentals=0,
        ),
        name="ridge_reads",
    )(ridge, *grams, *vectors, *after)


def cross_kernel(heads, terms, place_ref, *refs):
    crosses, (base_ref, solved_ref) = refs[:terms], refs[terms : terms + 2]
    outs, o_ref = refs[terms + 2 : -1], refs[-1]
    me = place_ref[0]
    for head in range(heads):
        cols = slice(head * HDIM, (head + 1) * HDIM)
        cross = crosses[0][cols, :].astype(F32)
        for term in crosses[1:]:
            cross = cross + term[cols, :].astype(F32)
        read = base_ref[:, cols] + dot(solved_ref[:, cols], cross.astype(BF16))
        o_ref[:, cols] = read.astype(BF16)
    tok_rows = outs[0].shape[0]
    for distance, out_ref in enumerate(outs):
        first_row = pl.multiple_of((me ^ distance) * tok_rows, tok_rows)
        out_ref[...] = o_ref[pl.ds(first_row, tok_rows), :]


def cross_reads(place, crosses, base, solved, head_count):
    length, width = base.shape
    whole = pl.BlockSpec(memory_space=pltpu.VMEM)
    return pl.pallas_call(
        functools.partial(cross_kernel, width // HDIM, len(crosses)),
        in_specs=[pl.BlockSpec(memory_space=pltpu.SMEM)] + [whole] * (len(crosses) + 2),
        out_specs=[whole] * head_count,
        out_shape=[jax.ShapeDtypeStruct((length // head_count, width), BF16)] * head_count,
        scratch_shapes=[pltpu.VMEM((length, width), BF16)],
        compiler_params=pltpu.CompilerParams(vmem_limit_bytes=24 * 2**20),
        cost_estimate=pl.CostEstimate(
            flops=2 * length * width * HDIM, bytes_accessed=8 * length * width, transcendentals=0
        ),
        name="cross_reads",
    )(place, *crosses, base, solved)


def output_kernel(place_ref, tokens_ref, w_ref, *refs):
    out_ref = refs[-1]
    me = place_ref[0]
    total = tokens_ref[...].astype(F32)
    for distance, part in enumerate(refs[:-1]):
        width = part.shape[1]
        first = pl.multiple_of((me ^ distance) * width, width)
        total = total + dot(part[...], w_ref[pl.ds(first, width), :])
    out_ref[...] = total.astype(BF16)


def output_rows(place, tokens, w_out, reads):
    whole = pl.BlockSpec(memory_space=pltpu.VMEM)
    return pl.pallas_call(
        output_kernel,
        in_specs=[pl.BlockSpec(memory_space=pltpu.SMEM)] + [whole] * (2 + len(reads)),
        out_specs=whole,
        out_shape=jax.ShapeDtypeStruct(tokens.shape, BF16),
        compiler_params=pltpu.CompilerParams(vmem_limit_bytes=24 * 2**20),
        cost_estimate=pl.CostEstimate(
            flops=2 * tokens.shape[0] * w_out.shape[0] * w_out.shape[1],
            bytes_accessed=2 * w_out.size + 6 * tokens.size,
            transcendentals=0,
        ),
        name="output_rows",
    )(place, tokens, w_out, *reads)


def shards(
    tokens,
    norm_gain,
    w_qkv,
    w_gates,
    conv_weight,
    conv_state,
    decay_rate,
    ridge,
    w_out,
    cache_keys,
    cache_values,
    page_table,
    cache_lengths,
    group_prompt,
    prompt_state,
):
    head_count = lax.axis_size("head")
    owners = lax.axis_size("grp")
    me = lax.axis_index("head").astype(jnp.int32)
    group = lax.axis_index("grp").astype(jnp.int32)
    place = me.reshape(1)
    meta = jnp.concatenate(
        [jnp.stack([group, group & 1, group >> 1]), group_prompt, cache_lengths]
    )

    blocks = {0: tokens}
    bit = head_count // 2
    while bit:
        for held in list(blocks):
            blocks[held ^ bit] = swap(blocks[held], "head", bit)
        bit //= 2
    blocks = [blocks[i] for i in range(head_count)]

    pool, page, heads, _ = cache_keys.shape
    slots = page_table.shape[1]
    ids = group * pool + jnp.arange(pool, dtype=jnp.int32)
    tag = jnp.arange(owners * slots, dtype=jnp.int32).reshape(owners, slots, 1)
    code = jnp.sum(
        jnp.where(page_table[:, :, None] == ids, tag, 0), axis=(0, 1), dtype=jnp.int32
    )
    keys = cache_keys.reshape(pool, page * heads, HDIM)
    values = cache_values.reshape(pool, page * heads, HDIM)

    def halved(parts):
        return halve_sums(meta, parts[1], swap(parts[0], "grp", 1))

    def scattered(parts):
        return [parts[0]] + [swap(parts[i], "grp", 2 * i) for i in range(1, owners // 2)]

    grams = halved(page_sums(code, meta, keys, None, prompt_state, owners, slots))
    early = [blocks[head_count // 2], blocks[1]]
    crosses = halved(page_sums(code, meta, keys, values, prompt_state, owners, slots, early))
    vectors = token_vectors(
        place, decay_rate, blocks, norm_gain, w_qkv, w_gates, conv_weight, conv_state, [grams[0]]
    )
    base, solved = ridge_reads(ridge, scattered(grams), vectors, [crosses[0]])
    reads = cross_reads(place, scattered(crosses), base, solved, head_count)
    reads = [reads[0]] + [swap(reads[i], "head", i) for i in range(1, head_count)]
    return output_rows(place, tokens, w_out, reads)


def solution(mesh):
    placed = (
        P(("grp", "head"), None),
        P(),
        P(),
        P(),
        P(),
        P("grp", None, None),
        P(),
        P("head"),
        P(),
        P("grp", None, "head", None),
        P("grp", None, "head", None),
        P(),
        P(),
        P(),
        P("grp", "head", None, None, None),
    )
    return jax.shard_map(
        shards, mesh=mesh, in_specs=placed, out_specs=P(("grp", "head"), None), check_vma=False
    )
```

```python
import functools

import jax
import jax.numpy as jnp
from jax import lax
from jax.experimental import pallas as pl
from jax.experimental.pallas import tpu as pltpu
from jax.sharding import PartitionSpec as P

HEADS = 8
HDIM = 128
CONV = 4
CG_STEPS = 8
PAGE = 128
CHUNK = 128
PAIR = 2 * CHUNK
EPS_NORM = 1e-06
PAGE_VMEM = 53
TOKEN_VMEM = 48
F32 = jnp.float32
BF16 = jnp.bfloat16


def swap(block, axis, distance):
    size = lax.axis_size(axis)
    return lax.ppermute(block, axis, [(i, i ^ distance) for i in range(size)])


def hold(block, other):
    anywhere = pl.BlockSpec(memory_space=pl.ANY)
    return pl.pallas_call(
        lambda *refs: None,
        in_specs=[anywhere, anywhere],
        out_specs=anywhere,
        out_shape=jax.ShapeDtypeStruct(block.shape, block.dtype),
        input_output_aliases={0: 0},
        name="hold",
    )(block, other)


def dot(a, b):
    return jnp.dot(a, b, preferred_element_type=F32)


def silu(a):
    return a * jax.nn.sigmoid(a)


def unit_rows(a):
    return a * lax.rsqrt(jnp.sum(a * a, axis=-1, keepdims=True) + EPS_NORM)


def block_diag(a):
    zero = jnp.zeros((a.shape[0], CHUNK), a.dtype)
    return jnp.concatenate(
        [
            jnp.concatenate([a[:, :CHUNK], zero], axis=1),
            jnp.concatenate([zero, a[:, CHUNK:]], axis=1),
        ],
        axis=0,
    )


def sums_kernel(heads, owners, slots, code_ref, meta_ref, keys_ref, values_ref, prompt_ref,
                send_gram, send_cross, keep_gram, keep_cross, acc_ref, parity_ref, stored_ref, sem):
    step = pl.program_id(0)
    pages, rows = keys_ref.shape[0], keys_ref.shape[1]
    load_prompt = pltpu.make_async_copy(prompt_ref, stored_ref, sem)
    lane = lax.broadcasted_iota(jnp.int32, (HDIM, rows), 1)

    @pl.when(step == 0)
    def _():
        load_prompt.start()
        acc_ref[...] = jnp.zeros_like(acc_ref)
        for head in range(heads):
            parity_ref[head] = (lane % heads == head).astype(F32).astype(BF16)

    def place(page):
        code = code_ref[step * pages + page]
        owner, slot = code // slots, code % slots
        return owner, jnp.clip(meta_ref[owners + owner] - slot * PAGE, 0, PAGE)

    def add(page, owner, turned):
        left = turned
        if heads > 1:
            left = jnp.concatenate([turned * parity_ref[head] for head in range(heads)], axis=0)
        right = jnp.concatenate([keys_ref[page], values_ref[page]], axis=1)
        acc_ref[owner] += dot(left, right)

    partial = jnp.int32(0)
    for page in range(pages):
        owner, live = place(page)
        add(page, jnp.where(live == PAGE, owner, owners), keys_ref[page].T)
        partial = partial | ((live > 0) & (live < PAGE)).astype(jnp.int32)

    @pl.when(partial > 0)
    def _():
        def one_page(page, carry):
            owner, live = place(page)

            @pl.when((live > 0) & (live < PAGE))
            def _():
                turned = keys_ref[page].T
                add(page, owner, jnp.where(lane < live * heads, turned, jnp.zeros_like(turned)))

            return carry

        lax.fori_loop(0, pages, one_page, 0)

    @pl.when(step == pl.num_programs(0) - 1)
    def _():
        load_prompt.wait()
        mine, bit = meta_ref[2 * owners], meta_ref[2 * owners + 1]
        stored = stored_ref.shape[0]

        def add_prompt(owner, carry):
            for slot in range(stored):

                @pl.when(meta_ref[owner] == mine * stored + slot)
                def _():
                    for head in range(heads):
                        at = slice(head * HDIM, (head + 1) * HDIM)
                        acc_ref[owner, at, :HDIM] += stored_ref[slot, head, 0]
                        acc_ref[owner, at, HDIM:] += stored_ref[slot, head, 1].T

            return carry

        lax.fori_loop(0, owners, add_prompt, 0)
        for pair in range(owners // 2):
            there, here = 2 * pair + 1 - bit, 2 * pair + bit
            send_gram[pair] = acc_ref[there, :, :HDIM].astype(BF16)
            send_cross[pair] = acc_ref[there, :, HDIM:].astype(BF16)
            keep_gram[pair] = acc_ref[here, :, :HDIM].astype(BF16)
            keep_cross[pair] = acc_ref[here, :, HDIM:].astype(BF16)


def page_sums(code, meta, keys, values, prompt_state, owners, slots):
    pool, rows, _ = keys.shape
    heads = prompt_state.shape[1]
    pages = 8
    half = (owners // 2, heads * HDIM, HDIM)
    page_spec = pl.BlockSpec((pages, rows, HDIM), lambda i, *_: (i, 0, 0))
    out_spec = pl.BlockSpec(half, lambda i, *_: (0, 0, 0))
    return pl.pallas_call(
        functools.partial(sums_kernel, heads, owners, slots),
        grid_spec=pltpu.PrefetchScalarGridSpec(
            num_scalar_prefetch=2,
            grid=(pool // pages,),
            in_specs=[page_spec, page_spec, pl.BlockSpec(memory_space=pl.ANY)],
            out_specs=[out_spec] * 4,
            scratch_shapes=[
                pltpu.VMEM((owners + 1, heads * HDIM, 2 * HDIM), F32),
                pltpu.VMEM((heads, HDIM, rows), BF16),
                pltpu.VMEM(prompt_state.shape, F32),
                pltpu.SemaphoreType.DMA,
            ],
        ),
        out_shape=[jax.ShapeDtypeStruct(half, BF16)] * 4,
        compiler_params=pltpu.CompilerParams(vmem_limit_bytes=PAGE_VMEM * 2**20),
        cost_estimate=pl.CostEstimate(
            flops=8 * pool * rows * heads * HDIM * HDIM,
            bytes_accessed=4 * pool * rows * HDIM,
            transcendentals=0,
        ),
        name="page_sums",
    )(code, meta, keys, values, prompt_state)


def halve_kernel(owners, meta_ref, keep_ref, got_ref, *outs):
    for distance, out_ref in enumerate(outs):
        row = meta_ref[2 * owners + 2] ^ distance
        total = keep_ref[row].astype(F32) + got_ref[row].astype(F32)
        out_ref[...] = total.astype(out_ref.dtype)


def halve_sums(meta, keep, got):
    count, rows, cols = keep.shape
    outs = [jax.ShapeDtypeStruct((rows, cols), F32 if i == 0 else BF16) for i in range(count)]
    whole = pl.BlockSpec(memory_space=pltpu.VMEM)
    return pl.pallas_call(
        functools.partial(halve_kernel, 2 * count),
        in_specs=[pl.BlockSpec(memory_space=pltpu.SMEM), whole, whole],
        out_specs=[whole] * count,
        out_shape=outs,
        compiler_params=pltpu.CompilerParams(vmem_limit_bytes=32 * 2**20),
        cost_estimate=pl.CostEstimate(
            flops=count * rows * cols, bytes_accessed=6 * count * rows * cols, transcendentals=0
        ),
        name="halve_sums",
    )(meta, keep, got)


def token_kernel(heads, place_ref, rate_ref, *refs):
    head_count = HEADS // heads
    blocks = refs[:head_count]
    (gain_ref, w_ref, wg_ref, taps_ref, state_ref) = refs[head_count : head_count + 5]
    (q_ref, k_ref, kt_ref, vt_ref, weight_ref, prefix_ref, rows_ref) = refs[-9:-2]
    ext_ref, gate_ref = refs[-2:]
    me = place_ref[0]
    tok_rows = blocks[0].shape[0]
    length = tok_rows * head_count
    chunks = length // CHUNK
    base = 8
    ext_ref[base - (CONV - 1) : base, :] = state_ref[0].astype(F32)
    gate_ref[...] = jnp.zeros_like(gate_ref)
    for distance, block in enumerate(blocks):
        first = pl.multiple_of((me ^ distance) * tok_rows, tok_rows)
        wide = block[...].astype(F32)
        scale = lax.rsqrt(jnp.mean(wide * wide, axis=-1, keepdims=True) + EPS_NORM)
        normed = (wide * scale * gain_ref[...]).astype(BF16)
        mixed = dot(normed, w_ref[...]).astype(BF16)
        ext_ref[pl.ds(pl.multiple_of(base + first, 8), tok_rows), :] = mixed.astype(F32)
        gate_ref[pl.ds(first, tok_rows), : 2 * HEADS] = dot(normed, wg_ref[...])

    shift = lax.rem(HDIM - 2 * heads * me, HDIM)
    logits = pltpu.roll(gate_ref[...], shift, 1)
    lane = lax.broadcasted_iota(jnp.int32, (1, HDIM), 1)
    rate = jnp.zeros((1, HDIM), F32)
    for head in range(heads):
        rate = jnp.where(lane == 2 * head + 1, rate_ref[me * heads + head], rate)
    write = jax.nn.sigmoid(logits).astype(BF16).astype(F32)
    soft = jnp.maximum(logits, 0.0) + jnp.log1p(jnp.exp(-jnp.abs(logits)))
    decay = (-rate * soft).astype(BF16)
    here = lax.broadcasted_iota(jnp.int32, (CHUNK, CHUNK), 0)
    there = lax.broadcasted_iota(jnp.int32, (CHUNK, CHUNK), 1)
    lower = (here >= there).astype(F32).astype(BF16)
    cumul = [dot(lower, decay[c * CHUNK : (c + 1) * CHUNK]) for c in range(chunks)]
    turned = [block.T for block in cumul]

    for head in range(heads):
        parts = []
        for part in range(3):
            cols = slice((3 * head + part) * HDIM, (3 * head + part + 1) * HDIM)
            total = taps_ref[CONV - 1 : CONV, cols] * ext_ref[base : base + length, cols]
            for lag in range(1, CONV):
                total = total + taps_ref[CONV - 1 - lag : CONV - lag, cols] * (
                    ext_ref[base - lag : base - lag + length, cols]
                )
            parts.append(total)
        query = unit_rows(silu(parts[0])).astype(BF16)
        key = unit_rows(silu(parts[1])).astype(BF16)
        value = parts[2].astype(BF16)
        q_ref[head] = query.T
        k_ref[head] = key
        kt_ref[head] = key.T
        vt_ref[head] = value.T
        prefix = jnp.zeros((HDIM, 2 * HDIM), F32)
        so_far = jnp.zeros((1, 1), F32)
        for c in range(chunks):
            rows = slice(c * CHUNK, (c + 1) * CHUNK)
            col = cumul[c][:, 2 * head + 1 : 2 * head + 2]
            row = turned[c][2 * head + 1 : 2 * head + 2, :]
            gate = write[rows, 2 * head : 2 * head + 1]
            spread = jnp.exp(jnp.minimum(row - col, 0.0)) * gate
            half = slice((c % 2) * CHUNK, (c % 2 + 1) * CHUNK)
            weight_ref[head, c // 2, :, half] = jnp.where(here <= there, spread, 0.0)
            rows_ref[head, c // 2, 0:1, half] = jnp.exp(row)
            rows_ref[head, c // 2, 1:2, half] = jnp.broadcast_to(jnp.exp(so_far), (1, CHUNK))
            prefix_ref[head, c, :HDIM] = prefix[:, :HDIM]
            prefix_ref[head, c, HDIM:] = prefix[:, HDIM:].T
            if c + 1 < chunks:
                whole = cumul[c][CHUNK - 1 :, 2 * head + 1 : 2 * head + 2]
                carry = jnp.exp(whole - col) * gate
                both = jnp.concatenate([key[rows], value[rows]], axis=1).astype(F32)
                prefix = prefix * jnp.exp(whole) + dot(
                    kt_ref[head, :, rows], (both * carry).astype(BF16)
                )
                so_far = so_far + whole


def token_vectors(
    place, decay_rate, blocks, norm_gain, w_qkv, w_gates, conv_weight, conv_state, held
):
    head_count = len(blocks)
    heads = HEADS // head_count
    width = heads * 3 * HDIM
    tok_rows, model = blocks[0].shape
    length = head_count * tok_rows
    chunks = length // CHUNK

    anywhere = pl.BlockSpec(memory_space=pl.ANY)

    def full(shape):
        return pl.BlockSpec(shape, lambda i, *_: (0,) * len(shape))

    outs = [
        jax.ShapeDtypeStruct((heads, HDIM, length), BF16),
        jax.ShapeDtypeStruct((heads, length, HDIM), BF16),
        jax.ShapeDtypeStruct((heads, HDIM, length), BF16),
        jax.ShapeDtypeStruct((heads, HDIM, length), BF16),
        jax.ShapeDtypeStruct((heads, chunks // 2, CHUNK, PAIR), F32),
        jax.ShapeDtypeStruct((heads, chunks, 2 * HDIM, HDIM), F32),
        jax.ShapeDtypeStruct((heads, chunks // 2, 8, PAIR), F32),
    ]
    return pl.pallas_call(
        functools.partial(token_kernel, heads),
        grid_spec=pltpu.PrefetchScalarGridSpec(
            num_scalar_prefetch=2,
            grid=(1,),
            in_specs=[full(b.shape) for b in blocks]
            + [
                full((1, model)),
                pl.BlockSpec((model, width), lambda i, place, rate: (0, place[0])),
                full(w_gates.shape),
                pl.BlockSpec((CONV, width), lambda i, place, rate: (0, place[0])),
                pl.BlockSpec((1, CONV - 1, width), lambda i, place, rate: (0, 0, place[0])),
            ]
            + [anywhere],
            out_specs=[anywhere] + [full(o.shape) for o in outs],
            scratch_shapes=[pltpu.VMEM((8 + length, width), F32), pltpu.VMEM((length, HDIM), F32)],
        ),
        out_shape=[jax.ShapeDtypeStruct(held.shape, held.dtype)] + outs,
        input_output_aliases={2 + len(blocks) + 5: 0},
        compiler_params=pltpu.CompilerParams(vmem_limit_bytes=TOKEN_VMEM * 2**20),
        cost_estimate=pl.CostEstimate(
            flops=2 * length * model * width,
            bytes_accessed=2 * model * (length + width) + 4 * 2**20,
            transcendentals=length * width,
        ),
        name="token_vectors",
    )(
        place,
        decay_rate,
        *blocks,
        norm_gain.reshape(1, model),
        w_qkv,
        w_gates,
        conv_weight,
        conv_state,
        held,
    )


def read_kernel(heads, terms, ridge_ref, *refs):
    grams = refs[:terms]
    (q_ref, k_ref, kt_ref, vt_ref, weight_ref, prefix_ref, rows_ref) = refs[terms : terms + 7]
    base_ref, solved_ref, left_ref, x_ref, r_ref, d_ref = refs[-6:]
    pairs = q_ref.shape[2] // PAIR
    groups = [(head, pair) for head in range(heads) for pair in range(pairs)]
    norms = []
    for head in range(heads):
        rows = slice(head * HDIM, (head + 1) * HDIM)
        gram = grams[0][rows, :].astype(F32)
        for term in grams[1:]:
            gram = gram + term[rows, :].astype(F32)
        for pair in range(pairs):
            for side in range(2):
                c = 2 * pair + side
                half = slice(side * CHUNK, (side + 1) * CHUNK)
                scale = rows_ref[head, pair, 1:2, half]
                left_ref[head, pair, :HDIM, half] = (
                    gram * scale + prefix_ref[head, c, :HDIM]
                ).astype(BF16)
                left_ref[head, pair, HDIM:, half] = k_ref[head, c * CHUNK : (c + 1) * CHUNK]
            query = q_ref[head, :, pair * PAIR : (pair + 1) * PAIR].astype(F32)
            x_ref[head, pair] = jnp.zeros_like(query)
            r_ref[head, pair] = query
            d_ref[head, pair] = query
            norms.append(jnp.sum(query * query, axis=0, keepdims=True))

    def one_step(_, norms):
        firsts = [dot(left_ref[g], block_diag(d_ref[g].astype(BF16))) for g in groups]
        seconds = []
        for (head, pair), first in zip(groups, firsts):
            scores = (first[HDIM:] * weight_ref[head, pair]).astype(BF16)
            seconds.append(
                dot(kt_ref[head, :, pair * PAIR : (pair + 1) * PAIR], block_diag(scores))
            )
        later = []
        for (head, pair), first, second, norm in zip(groups, firsts, seconds, norms):
            direction = d_ref[head, pair]
            image = (
                rows_ref[head, pair, 0:1] * first[:HDIM] + ridge_ref[head] * direction + second
            )
            alpha = norm / jnp.sum(direction * image, axis=0, keepdims=True)
            x_ref[head, pair] += alpha * direction
            residue = r_ref[head, pair] - alpha * image
            r_ref[head, pair] = residue
            norm_next = jnp.sum(residue * residue, axis=0, keepdims=True)
            d_ref[head, pair] = residue + norm_next / norm * direction
            later.append(norm_next)
        return tuple(later)

    lax.fori_loop(0, CG_STEPS, one_step, tuple(norms))
    for head, pair in groups:
        cols = slice(head * HDIM, (head + 1) * HDIM)
        span = slice(pair * PAIR, (pair + 1) * PAIR)
        for side in range(2):
            half = slice(side * CHUNK, (side + 1) * CHUNK)
            left_ref[head, pair, :HDIM, half] = prefix_ref[head, 2 * pair + side, HDIM:].astype(BF16)
        solved = x_ref[head, pair]
        first = dot(left_ref[head, pair], block_diag(solved.astype(BF16)))
        scores = (first[HDIM:] * weight_ref[head, pair]).astype(BF16)
        carry = rows_ref[head, pair, 0:1]
        read = carry * first[:HDIM] + dot(vt_ref[head, :, span], block_diag(scores))
        base_ref[span, cols] = read.T
        solved_ref[span, cols] = (solved * (carry * rows_ref[head, pair, 1:2])).T.astype(BF16)


def ridge_reads(ridge, grams, vectors, after=()):
    heads, _, length = vectors[0].shape
    pairs = length // PAIR
    whole = pl.BlockSpec(memory_space=pltpu.VMEM)
    state = pltpu.VMEM((heads, pairs, HDIM, PAIR), F32)
    return pl.pallas_call(
        functools.partial(read_kernel, heads, len(grams)),
        in_specs=[pl.BlockSpec(memory_space=pltpu.SMEM)]
        + [whole] * (len(grams) + len(vectors))
        + [whole] * len(after),
        out_specs=[whole] * 2,
        out_shape=[
            jax.ShapeDtypeStruct((length, heads * HDIM), F32),
            jax.ShapeDtypeStruct((length, heads * HDIM), BF16),
        ],
        scratch_shapes=[pltpu.VMEM((heads, pairs, 2 * HDIM, PAIR), BF16), state, state, state],
        compiler_params=pltpu.CompilerParams(vmem_limit_bytes=32 * 2**20),
        cost_estimate=pl.CostEstimate(
            flops=CG_STEPS * heads * pairs * 6 * CHUNK**3 * 16,
            bytes_accessed=8 * 2**20,
            transcendentals=0,
        ),
        name="ridge_reads",
    )(ridge, *grams, *vectors, *after)


def cross_kernel(heads, terms, place_ref, *refs):
    crosses, (base_ref, solved_ref) = refs[:terms], refs[terms : terms + 2]
    outs, o_ref = refs[terms + 2 : -1], refs[-1]
    me = place_ref[0]
    for head in range(heads):
        cols = slice(head * HDIM, (head + 1) * HDIM)
        cross = crosses[0][cols, :].astype(F32)
        for term in crosses[1:]:
            cross = cross + term[cols, :].astype(F32)
        read = base_ref[:, cols] + dot(solved_ref[:, cols], cross.astype(BF16))
        o_ref[:, cols] = read.astype(BF16)
    tok_rows = outs[0].shape[0]
    for distance, out_ref in enumerate(outs):
        first_row = pl.multiple_of((me ^ distance) * tok_rows, tok_rows)
        out_ref[...] = o_ref[pl.ds(first_row, tok_rows), :]


def cross_reads(place, crosses, base, solved, head_count):
    length, width = base.shape
    whole = pl.BlockSpec(memory_space=pltpu.VMEM)
    return pl.pallas_call(
        functools.partial(cross_kernel, width // HDIM, len(crosses)),
        in_specs=[pl.BlockSpec(memory_space=pltpu.SMEM)] + [whole] * (len(crosses) + 2),
        out_specs=[whole] * head_count,
        out_shape=[jax.ShapeDtypeStruct((length // head_count, width), BF16)] * head_count,
        scratch_shapes=[pltpu.VMEM((length, width), BF16)],
        compiler_params=pltpu.CompilerParams(vmem_limit_bytes=24 * 2**20),
        cost_estimate=pl.CostEstimate(
            flops=2 * length * width * HDIM, bytes_accessed=8 * length * width, transcendentals=0
        ),
        name="cross_reads",
    )(place, *crosses, base, solved)


def output_kernel(place_ref, tokens_ref, w_ref, *refs):
    out_ref = refs[-1]
    me = place_ref[0]
    total = tokens_ref[...].astype(F32)
    for distance, part in enumerate(refs[:-1]):
        width = part.shape[1]
        first = pl.multiple_of((me ^ distance) * width, width)
        total = total + dot(part[...], w_ref[pl.ds(first, width), :])
    out_ref[...] = total.astype(BF16)


def output_rows(place, tokens, w_out, reads):
    whole = pl.BlockSpec(memory_space=pltpu.VMEM)
    return pl.pallas_call(
        output_kernel,
        in_specs=[pl.BlockSpec(memory_space=pltpu.SMEM)] + [whole] * (2 + len(reads)),
        out_specs=whole,
        out_shape=jax.ShapeDtypeStruct(tokens.shape, BF16),
        compiler_params=pltpu.CompilerParams(vmem_limit_bytes=24 * 2**20),
        cost_estimate=pl.CostEstimate(
            flops=2 * tokens.shape[0] * w_out.shape[0] * w_out.shape[1],
            bytes_accessed=2 * w_out.size + 6 * tokens.size,
            transcendentals=0,
        ),
        name="output_rows",
    )(place, tokens, w_out, *reads)


def shards(
    tokens,
    norm_gain,
    w_qkv,
    w_gates,
    conv_weight,
    conv_state,
    decay_rate,
    ridge,
    w_out,
    cache_keys,
    cache_values,
    page_table,
    cache_lengths,
    group_prompt,
    prompt_state,
):
    head_count = lax.axis_size("head")
    owners = lax.axis_size("grp")
    me = lax.axis_index("head").astype(jnp.int32)
    group = lax.axis_index("grp").astype(jnp.int32)
    place = me.reshape(1)
    extra = jnp.arange(3, dtype=jnp.int32)
    own = jnp.where(extra == 0, group, jnp.where(extra == 1, group & 1, group >> 1))
    meta = (
        jnp.pad(group_prompt, (0, owners + 3))
        + jnp.pad(cache_lengths, (owners, 3))
        + jnp.pad(own, (2 * owners, 0))
    )

    bits = [head_count >> i for i in range(1, head_count.bit_length())]
    blocks = {0: tokens}
    for bit in bits:
        blocks[bit] = swap(tokens, "head", bit)

    pool, page, heads, _ = cache_keys.shape
    slots = page_table.shape[1]
    ids = group * pool + jnp.arange(pool, dtype=jnp.int32)
    tag = jnp.arange(owners * slots, dtype=jnp.int32).reshape(owners, slots, 1)
    code = jnp.sum(
        jnp.where(page_table[:, :, None] == ids, tag, 0), axis=(0, 1), dtype=jnp.int32
    )
    keys = cache_keys.reshape(pool, page * heads, HDIM)
    values = cache_values.reshape(pool, page * heads, HDIM)

    def scattered(parts):
        return [parts[0]] + [swap(parts[i], "grp", 2 * i) for i in range(1, owners // 2)]

    send_gram, send_cross, keep_gram, keep_cross = page_sums(
        code, meta, keys, values, prompt_state, owners, slots
    )
    got_gram = swap(send_gram, "grp", 1)
    for bit in bits[1:]:
        for distance in list(blocks):
            if distance and not distance & bit and distance ^ bit not in blocks:
                blocks[distance] = hold(blocks[distance], keep_gram)
                blocks[distance ^ bit] = swap(blocks[distance], "head", bit)
    blocks = [blocks[i] for i in range(head_count)]
    send_cross, *vectors = token_vectors(
        place, decay_rate, blocks, norm_gain, w_qkv, w_gates, conv_weight, conv_state, send_cross
    )
    grams = halve_sums(meta, keep_gram, got_gram)
    crosses = halve_sums(meta, keep_cross, swap(send_cross, "grp", 1))
    base, solved = ridge_reads(ridge, scattered(grams), vectors, [crosses[0]])
    reads = cross_reads(place, scattered(crosses), base, solved, head_count)
    reads = [reads[0]] + [swap(reads[i], "head", i) for i in range(1, head_count)]
    return output_rows(place, tokens, w_out, reads)


def solution(mesh):
    placed = (
        P(("grp", "head"), None),
        P(),
        P(),
        P(),
        P(),
        P("grp", None, None),
        P(),
        P("head"),
        P(),
        P("grp", None, "head", None),
        P("grp", None, "head", None),
        P(),
        P(),
        P(),
        P("grp", "head", None, None, None),
    )
    return jax.shard_map(
        shards, mesh=mesh, in_specs=placed, out_specs=P(("grp", "head"), None), check_vma=False
    )
```

```python
import functools

import jax
import jax.numpy as jnp
from jax import lax
from jax.experimental import pallas as pl
from jax.experimental.pallas import tpu as pltpu
from jax.sharding import PartitionSpec as P

HEADS = 8
HDIM = 128
CONV = 4
CG_STEPS = 8
PAGE = 128
CHUNK = 128
PAIR = 2 * CHUNK
EPS_NORM = 1e-06
PAGE_VMEM = 53
TOKEN_VMEM = 48
F32 = jnp.float32
BF16 = jnp.bfloat16


def swap(block, axis, distance):
    size = lax.axis_size(axis)
    return lax.ppermute(block, axis, [(i, i ^ distance) for i in range(size)])


def hold(block, other):
    anywhere = pl.BlockSpec(memory_space=pl.ANY)
    return pl.pallas_call(
        lambda *refs: None,
        in_specs=[anywhere, anywhere],
        out_specs=anywhere,
        out_shape=jax.ShapeDtypeStruct(block.shape, block.dtype),
        input_output_aliases={0: 0},
        compiler_params=pltpu.CompilerParams(vmem_limit_bytes=2**20),
        name="hold",
    )(block, other)


def dot(a, b):
    return jnp.dot(a, b, preferred_element_type=F32)


def silu(a):
    return a * jax.nn.sigmoid(a)


def unit_rows(a):
    return a * lax.rsqrt(jnp.sum(a * a, axis=-1, keepdims=True) + EPS_NORM)


def block_diag(a):
    zero = jnp.zeros((a.shape[0], CHUNK), a.dtype)
    return jnp.concatenate(
        [
            jnp.concatenate([a[:, :CHUNK], zero], axis=1),
            jnp.concatenate([zero, a[:, CHUNK:]], axis=1),
        ],
        axis=0,
    )


def sums_kernel(heads, owners, slots, code_ref, meta_ref, keys_ref, values_ref, prompt_ref,
                send_gram, send_cross, keep_gram, keep_cross, acc_ref, stored_ref, sem):
    step = pl.program_id(0)
    pages, rows = keys_ref.shape[0], keys_ref.shape[1]
    load_prompt = pltpu.make_async_copy(prompt_ref, stored_ref, sem)
    lane = lax.broadcasted_iota(jnp.int32, (HDIM, rows), 1)

    @pl.when(step == 0)
    def _():
        load_prompt.start()
        acc_ref[...] = jnp.zeros_like(acc_ref)

    def place(page):
        code = code_ref[step * pages + page]
        owner, slot = code // slots, code % slots
        return owner, jnp.clip(meta_ref[owners + owner] - slot * PAGE, 0, PAGE)

    def add(page, owner, turned):
        zero = jnp.zeros_like(turned)
        left = turned
        if heads > 1:
            left = jnp.concatenate(
                [jnp.where(lane % heads == head, turned, zero) for head in range(heads)], axis=0
            )
        right = jnp.concatenate([keys_ref[page], values_ref[page]], axis=1)
        acc_ref[owner] += dot(left, right)

    partial = jnp.int32(0)
    for page in range(pages):
        owner, live = place(page)
        add(page, jnp.where(live == PAGE, owner, owners), keys_ref[page].T)
        partial = partial | ((live > 0) & (live < PAGE)).astype(jnp.int32)

    @pl.when(partial > 0)
    def _():
        def one_page(page, carry):
            owner, live = place(page)

            @pl.when((live > 0) & (live < PAGE))
            def _():
                turned = keys_ref[page].T
                add(page, owner, jnp.where(lane < live * heads, turned, jnp.zeros_like(turned)))

            return carry

        lax.fori_loop(0, pages, one_page, 0)

    @pl.when(step == pl.num_programs(0) - 1)
    def _():
        load_prompt.wait()
        mine, bit = meta_ref[2 * owners], meta_ref[2 * owners + 1]
        stored = stored_ref.shape[0]

        def add_prompt(owner, carry):
            for slot in range(stored):

                @pl.when(meta_ref[owner] == mine * stored + slot)
                def _():
                    for head in range(heads):
                        at = slice(head * HDIM, (head + 1) * HDIM)
                        acc_ref[owner, at, :HDIM] += stored_ref[slot, head, 0]
                        acc_ref[owner, at, HDIM:] += stored_ref[slot, head, 1].T

            return carry

        lax.fori_loop(0, owners, add_prompt, 0)
        for pair in range(owners // 2):
            there, here = 2 * pair + 1 - bit, 2 * pair + bit
            send_gram[pair] = acc_ref[there, :, :HDIM].astype(BF16)
            send_cross[pair] = acc_ref[there, :, HDIM:].astype(BF16)
            keep_gram[pair] = acc_ref[here, :, :HDIM].astype(BF16)
            keep_cross[pair] = acc_ref[here, :, HDIM:].astype(BF16)


def page_sums(code, meta, keys, values, prompt_state, owners, slots):
    pool, rows, _ = keys.shape
    heads = prompt_state.shape[1]
    pages = 8
    half = (owners // 2, heads * HDIM, HDIM)
    page_spec = pl.BlockSpec((pages, rows, HDIM), lambda i, *_: (i, 0, 0))
    out_spec = pl.BlockSpec(half, lambda i, *_: (0, 0, 0))
    return pl.pallas_call(
        functools.partial(sums_kernel, heads, owners, slots),
        grid_spec=pltpu.PrefetchScalarGridSpec(
            num_scalar_prefetch=2,
            grid=(pool // pages,),
            in_specs=[page_spec, page_spec, pl.BlockSpec(memory_space=pl.ANY)],
            out_specs=[out_spec] * 4,
            scratch_shapes=[
                pltpu.VMEM((owners + 1, heads * HDIM, 2 * HDIM), F32),
                pltpu.VMEM(prompt_state.shape, F32),
                pltpu.SemaphoreType.DMA,
            ],
        ),
        out_shape=[jax.ShapeDtypeStruct(half, BF16)] * 4,
        compiler_params=pltpu.CompilerParams(vmem_limit_bytes=PAGE_VMEM * 2**20),
        cost_estimate=pl.CostEstimate(
            flops=8 * pool * rows * heads * HDIM * HDIM,
            bytes_accessed=4 * pool * rows * HDIM,
            transcendentals=0,
        ),
        name="page_sums",
    )(code, meta, keys, values, prompt_state)


def halve_kernel(owners, meta_ref, keep_ref, got_ref, *outs):
    for distance, out_ref in enumerate(outs):
        row = meta_ref[2 * owners + 2] ^ distance
        total = keep_ref[row].astype(F32) + got_ref[row].astype(F32)
        out_ref[...] = total.astype(out_ref.dtype)


def halve_sums(meta, keep, got):
    count, rows, cols = keep.shape
    outs = [jax.ShapeDtypeStruct((rows, cols), F32 if i == 0 else BF16) for i in range(count)]
    whole = pl.BlockSpec(memory_space=pltpu.VMEM)
    return pl.pallas_call(
        functools.partial(halve_kernel, 2 * count),
        in_specs=[pl.BlockSpec(memory_space=pltpu.SMEM), whole, whole],
        out_specs=[whole] * count,
        out_shape=outs,
        compiler_params=pltpu.CompilerParams(vmem_limit_bytes=32 * 2**20),
        cost_estimate=pl.CostEstimate(
            flops=count * rows * cols, bytes_accessed=6 * count * rows * cols, transcendentals=0
        ),
        name="halve_sums",
    )(meta, keep, got)


def token_kernel(heads, place_ref, rate_ref, *refs):
    head_count = HEADS // heads
    blocks = refs[:head_count]
    (gain_ref, w_ref, wg_ref, taps_ref, state_ref) = refs[head_count : head_count + 5]
    (q_ref, k_ref, kt_ref, vt_ref, weight_ref, prefix_ref, rows_ref) = refs[-9:-2]
    ext_ref, gate_ref = refs[-2:]
    me = place_ref[0]
    tok_rows = blocks[0].shape[0]
    length = tok_rows * head_count
    chunks = length // CHUNK
    base = 8
    ext_ref[base - (CONV - 1) : base, :] = state_ref[0].astype(F32)
    gate_ref[...] = jnp.zeros_like(gate_ref)
    for distance, block in enumerate(blocks):
        first = pl.multiple_of((me ^ distance) * tok_rows, tok_rows)
        wide = block[...].astype(F32)
        scale = lax.rsqrt(jnp.mean(wide * wide, axis=-1, keepdims=True) + EPS_NORM)
        normed = (wide * scale * gain_ref[...]).astype(BF16)
        mixed = dot(normed, w_ref[...]).astype(BF16)
        ext_ref[pl.ds(pl.multiple_of(base + first, 8), tok_rows), :] = mixed.astype(F32)
        gate_ref[pl.ds(first, tok_rows), : 2 * HEADS] = dot(normed, wg_ref[...])

    shift = lax.rem(HDIM - 2 * heads * me, HDIM)
    logits = pltpu.roll(gate_ref[...], shift, 1)
    lane = lax.broadcasted_iota(jnp.int32, (1, HDIM), 1)
    rate = jnp.zeros((1, HDIM), F32)
    for head in range(heads):
        rate = jnp.where(lane == 2 * head + 1, rate_ref[me * heads + head], rate)
    write = jax.nn.sigmoid(logits).astype(BF16).astype(F32)
    soft = jnp.maximum(logits, 0.0) + jnp.log1p(jnp.exp(-jnp.abs(logits)))
    decay = (-rate * soft).astype(BF16)
    here = lax.broadcasted_iota(jnp.int32, (CHUNK, CHUNK), 0)
    there = lax.broadcasted_iota(jnp.int32, (CHUNK, CHUNK), 1)
    lower = (here >= there).astype(F32).astype(BF16)
    cumul = [dot(lower, decay[c * CHUNK : (c + 1) * CHUNK]) for c in range(chunks)]
    turned = [block.T for block in cumul]

    for head in range(heads):
        parts = []
        for part in range(3):
            cols = slice((3 * head + part) * HDIM, (3 * head + part + 1) * HDIM)
            total = taps_ref[CONV - 1 : CONV, cols] * ext_ref[base : base + length, cols]
            for lag in range(1, CONV):
                total = total + taps_ref[CONV - 1 - lag : CONV - lag, cols] * (
                    ext_ref[base - lag : base - lag + length, cols]
                )
            parts.append(total)
        query = unit_rows(silu(parts[0])).astype(BF16)
        key = unit_rows(silu(parts[1])).astype(BF16)
        value = parts[2].astype(BF16)
        q_ref[head] = query.T
        k_ref[head] = key
        kt_ref[head] = key.T
        vt_ref[head] = value.T
        prefix = jnp.zeros((HDIM, 2 * HDIM), F32)
        so_far = jnp.zeros((1, 1), F32)
        for c in range(chunks):
            rows = slice(c * CHUNK, (c + 1) * CHUNK)
            col = cumul[c][:, 2 * head + 1 : 2 * head + 2]
            row = turned[c][2 * head + 1 : 2 * head + 2, :]
            gate = write[rows, 2 * head : 2 * head + 1]
            spread = jnp.exp(jnp.minimum(row - col, 0.0)) * gate
            half = slice((c % 2) * CHUNK, (c % 2 + 1) * CHUNK)
            weight_ref[head, c // 2, :, half] = jnp.where(here <= there, spread, 0.0)
            rows_ref[head, c // 2, 0:1, half] = jnp.exp(row)
            rows_ref[head, c // 2, 1:2, half] = jnp.broadcast_to(jnp.exp(so_far), (1, CHUNK))
            prefix_ref[head, c, :HDIM] = prefix[:, :HDIM]
            prefix_ref[head, c, HDIM:] = prefix[:, HDIM:].T
            if c + 1 < chunks:
                whole = cumul[c][CHUNK - 1 :, 2 * head + 1 : 2 * head + 2]
                carry = jnp.exp(whole - col) * gate
                both = jnp.concatenate([key[rows], value[rows]], axis=1).astype(F32)
                prefix = prefix * jnp.exp(whole) + dot(
                    kt_ref[head, :, rows], (both * carry).astype(BF16)
                )
                so_far = so_far + whole


def token_vectors(
    place, decay_rate, blocks, norm_gain, w_qkv, w_gates, conv_weight, conv_state, held
):
    head_count = len(blocks)
    heads = HEADS // head_count
    width = heads * 3 * HDIM
    tok_rows, model = blocks[0].shape
    length = head_count * tok_rows
    chunks = length // CHUNK

    anywhere = pl.BlockSpec(memory_space=pl.ANY)

    def full(shape):
        return pl.BlockSpec(shape, lambda i, *_: (0,) * len(shape))

    outs = [
        jax.ShapeDtypeStruct((heads, HDIM, length), BF16),
        jax.ShapeDtypeStruct((heads, length, HDIM), BF16),
        jax.ShapeDtypeStruct((heads, HDIM, length), BF16),
        jax.ShapeDtypeStruct((heads, HDIM, length), BF16),
        jax.ShapeDtypeStruct((heads, chunks // 2, CHUNK, PAIR), F32),
        jax.ShapeDtypeStruct((heads, chunks, 2 * HDIM, HDIM), F32),
        jax.ShapeDtypeStruct((heads, chunks // 2, 8, PAIR), F32),
    ]
    return pl.pallas_call(
        functools.partial(token_kernel, heads),
        grid_spec=pltpu.PrefetchScalarGridSpec(
            num_scalar_prefetch=2,
            grid=(1,),
            in_specs=[full(b.shape) for b in blocks]
            + [
                full((1, model)),
                pl.BlockSpec((model, width), lambda i, place, rate: (0, place[0])),
                full(w_gates.shape),
                pl.BlockSpec((CONV, width), lambda i, place, rate: (0, place[0])),
                pl.BlockSpec((1, CONV - 1, width), lambda i, place, rate: (0, 0, place[0])),
            ]
            + [anywhere],
            out_specs=[anywhere] + [full(o.shape) for o in outs],
            scratch_shapes=[pltpu.VMEM((8 + length, width), F32), pltpu.VMEM((length, HDIM), F32)],
        ),
        out_shape=[jax.ShapeDtypeStruct(held.shape, held.dtype)] + outs,
        input_output_aliases={2 + len(blocks) + 5: 0},
        compiler_params=pltpu.CompilerParams(vmem_limit_bytes=TOKEN_VMEM * 2**20),
        cost_estimate=pl.CostEstimate(
            flops=2 * length * model * width,
            bytes_accessed=2 * model * (length + width) + 4 * 2**20,
            transcendentals=length * width,
        ),
        name="token_vectors",
    )(
        place,
        decay_rate,
        *blocks,
        norm_gain.reshape(1, model),
        w_qkv,
        w_gates,
        conv_weight,
        conv_state,
        held,
    )


def read_kernel(heads, terms, ridge_ref, *refs):
    grams = refs[:terms]
    (q_ref, k_ref, kt_ref, vt_ref, weight_ref, prefix_ref, rows_ref) = refs[terms : terms + 7]
    base_ref, solved_ref, left_ref, x_ref, r_ref, d_ref = refs[-6:]
    pairs = q_ref.shape[2] // PAIR
    groups = [(head, pair) for head in range(heads) for pair in range(pairs)]
    norms = []
    for head in range(heads):
        rows = slice(head * HDIM, (head + 1) * HDIM)
        gram = grams[0][rows, :].astype(F32)
        for term in grams[1:]:
            gram = gram + term[rows, :].astype(F32)
        for pair in range(pairs):
            for side in range(2):
                c = 2 * pair + side
                half = slice(side * CHUNK, (side + 1) * CHUNK)
                scale = rows_ref[head, pair, 1:2, half]
                left_ref[head, pair, :HDIM, half] = (
                    gram * scale + prefix_ref[head, c, :HDIM]
                ).astype(BF16)
                left_ref[head, pair, HDIM:, half] = k_ref[head, c * CHUNK : (c + 1) * CHUNK]
            query = q_ref[head, :, pair * PAIR : (pair + 1) * PAIR].astype(F32)
            x_ref[head, pair] = jnp.zeros_like(query)
            r_ref[head, pair] = query
            d_ref[head, pair] = query
            norms.append(jnp.sum(query * query, axis=0, keepdims=True))

    def one_step(_, norms):
        firsts = [dot(left_ref[g], block_diag(d_ref[g].astype(BF16))) for g in groups]
        seconds = []
        for (head, pair), first in zip(groups, firsts):
            scores = (first[HDIM:] * weight_ref[head, pair]).astype(BF16)
            seconds.append(
                dot(kt_ref[head, :, pair * PAIR : (pair + 1) * PAIR], block_diag(scores))
            )
        later = []
        for (head, pair), first, second, norm in zip(groups, firsts, seconds, norms):
            direction = d_ref[head, pair]
            image = (
                rows_ref[head, pair, 0:1] * first[:HDIM] + ridge_ref[head] * direction + second
            )
            alpha = norm / jnp.sum(direction * image, axis=0, keepdims=True)
            x_ref[head, pair] += alpha * direction
            residue = r_ref[head, pair] - alpha * image
            r_ref[head, pair] = residue
            norm_next = jnp.sum(residue * residue, axis=0, keepdims=True)
            d_ref[head, pair] = residue + norm_next / norm * direction
            later.append(norm_next)
        return tuple(later)

    lax.fori_loop(0, CG_STEPS, one_step, tuple(norms), unroll=2)
    for head, pair in groups:
        cols = slice(head * HDIM, (head + 1) * HDIM)
        span = slice(pair * PAIR, (pair + 1) * PAIR)
        for side in range(2):
            half = slice(side * CHUNK, (side + 1) * CHUNK)
            left_ref[head, pair, :HDIM, half] = prefix_ref[head, 2 * pair + side, HDIM:].astype(BF16)
        solved = x_ref[head, pair]
        first = dot(left_ref[head, pair], block_diag(solved.astype(BF16)))
        scores = (first[HDIM:] * weight_ref[head, pair]).astype(BF16)
        carry = rows_ref[head, pair, 0:1]
        read = carry * first[:HDIM] + dot(vt_ref[head, :, span], block_diag(scores))
        base_ref[span, cols] = read.T
        solved_ref[span, cols] = (solved * (carry * rows_ref[head, pair, 1:2])).T.astype(BF16)


def ridge_reads(ridge, grams, vectors, after=()):
    heads, _, length = vectors[0].shape
    pairs = length // PAIR
    whole = pl.BlockSpec(memory_space=pltpu.VMEM)
    state = pltpu.VMEM((heads, pairs, HDIM, PAIR), F32)
    return pl.pallas_call(
        functools.partial(read_kernel, heads, len(grams)),
        in_specs=[pl.BlockSpec(memory_space=pltpu.SMEM)]
        + [whole] * (len(grams) + len(vectors))
        + [whole] * len(after),
        out_specs=[whole] * 2,
        out_shape=[
            jax.ShapeDtypeStruct((length, heads * HDIM), F32),
            jax.ShapeDtypeStruct((length, heads * HDIM), BF16),
        ],
        scratch_shapes=[pltpu.VMEM((heads, pairs, 2 * HDIM, PAIR), BF16), state, state, state],
        compiler_params=pltpu.CompilerParams(vmem_limit_bytes=32 * 2**20),
        cost_estimate=pl.CostEstimate(
            flops=CG_STEPS * heads * pairs * 6 * CHUNK**3 * 16,
            bytes_accessed=8 * 2**20,
            transcendentals=0,
        ),
        name="ridge_reads",
    )(ridge, *grams, *vectors, *after)


def cross_kernel(heads, terms, place_ref, *refs):
    crosses, (base_ref, solved_ref) = refs[:terms], refs[terms : terms + 2]
    outs, o_ref = refs[terms + 2 : -1], refs[-1]
    me = place_ref[0]
    for head in range(heads):
        cols = slice(head * HDIM, (head + 1) * HDIM)
        cross = crosses[0][cols, :].astype(F32)
        for term in crosses[1:]:
            cross = cross + term[cols, :].astype(F32)
        read = base_ref[:, cols] + dot(solved_ref[:, cols], cross.astype(BF16))
        o_ref[:, cols] = read.astype(BF16)
    tok_rows = outs[0].shape[0]
    for distance, out_ref in enumerate(outs):
        first_row = pl.multiple_of((me ^ distance) * tok_rows, tok_rows)
        out_ref[...] = o_ref[pl.ds(first_row, tok_rows), :]


def cross_reads(place, crosses, base, solved, head_count):
    length, width = base.shape
    whole = pl.BlockSpec(memory_space=pltpu.VMEM)
    return pl.pallas_call(
        functools.partial(cross_kernel, width // HDIM, len(crosses)),
        in_specs=[pl.BlockSpec(memory_space=pltpu.SMEM)] + [whole] * (len(crosses) + 2),
        out_specs=[whole] * head_count,
        out_shape=[jax.ShapeDtypeStruct((length // head_count, width), BF16)] * head_count,
        scratch_shapes=[pltpu.VMEM((length, width), BF16)],
        compiler_params=pltpu.CompilerParams(vmem_limit_bytes=24 * 2**20),
        cost_estimate=pl.CostEstimate(
            flops=2 * length * width * HDIM, bytes_accessed=8 * length * width, transcendentals=0
        ),
        name="cross_reads",
    )(place, *crosses, base, solved)


def output_kernel(place_ref, tokens_ref, w_ref, *refs):
    out_ref = refs[-1]
    me = place_ref[0]
    total = tokens_ref[...].astype(F32)
    for distance, part in enumerate(refs[:-1]):
        width = part.shape[1]
        first = pl.multiple_of((me ^ distance) * width, width)
        total = total + dot(part[...], w_ref[pl.ds(first, width), :])
    out_ref[...] = total.astype(BF16)


def output_rows(place, tokens, w_out, reads):
    whole = pl.BlockSpec(memory_space=pltpu.VMEM)
    return pl.pallas_call(
        output_kernel,
        in_specs=[pl.BlockSpec(memory_space=pltpu.SMEM)] + [whole] * (2 + len(reads)),
        out_specs=whole,
        out_shape=jax.ShapeDtypeStruct(tokens.shape, BF16),
        compiler_params=pltpu.CompilerParams(vmem_limit_bytes=24 * 2**20),
        cost_estimate=pl.CostEstimate(
            flops=2 * tokens.shape[0] * w_out.shape[0] * w_out.shape[1],
            bytes_accessed=2 * w_out.size + 6 * tokens.size,
            transcendentals=0,
        ),
        name="output_rows",
    )(place, tokens, w_out, *reads)


def shards(
    tokens,
    norm_gain,
    w_qkv,
    w_gates,
    conv_weight,
    conv_state,
    decay_rate,
    ridge,
    w_out,
    cache_keys,
    cache_values,
    page_table,
    cache_lengths,
    group_prompt,
    prompt_state,
):
    head_count = lax.axis_size("head")
    owners = lax.axis_size("grp")
    me = lax.axis_index("head").astype(jnp.int32)
    group = lax.axis_index("grp").astype(jnp.int32)
    place = me.reshape(1)
    extra = jnp.arange(3, dtype=jnp.int32)
    own = jnp.where(extra == 0, group, jnp.where(extra == 1, group & 1, group >> 1))
    meta = (
        jnp.pad(group_prompt, (0, owners + 3))
        + jnp.pad(cache_lengths, (owners, 3))
        + jnp.pad(own, (2 * owners, 0))
    )

    bits = [head_count >> i for i in range(1, head_count.bit_length())]
    blocks = {0: tokens}
    for bit in bits:
        blocks[bit] = swap(tokens, "head", bit)

    pool, page, heads, _ = cache_keys.shape
    slots = page_table.shape[1]
    ids = group * pool + jnp.arange(pool, dtype=jnp.int32)
    tag = jnp.arange(owners * slots, dtype=jnp.int32).reshape(owners, slots, 1)
    code = jnp.sum(
        jnp.where(page_table[:, :, None] == ids, tag, 0), axis=(0, 1), dtype=jnp.int32
    )
    keys = cache_keys.reshape(pool, page * heads, HDIM)
    values = cache_values.reshape(pool, page * heads, HDIM)

    def scattered(parts):
        return [parts[0]] + [swap(parts[i], "grp", 2 * i) for i in range(1, owners // 2)]

    send_gram, send_cross, keep_gram, keep_cross = page_sums(
        code, meta, keys, values, prompt_state, owners, slots
    )
    got_gram = swap(send_gram, "grp", 1)
    for bit in bits[1:]:
        for distance in list(blocks):
            if distance and not distance & bit and distance ^ bit not in blocks:
                blocks[distance] = hold(blocks[distance], keep_gram)
                blocks[distance ^ bit] = swap(blocks[distance], "head", bit)
    blocks = [blocks[i] for i in range(head_count)]
    send_cross, *vectors = token_vectors(
        place, decay_rate, blocks, norm_gain, w_qkv, w_gates, conv_weight, conv_state, send_cross
    )
    grams = halve_sums(meta, keep_gram, got_gram)
    crosses = halve_sums(meta, keep_cross, swap(send_cross, "grp", 1))
    base, solved = ridge_reads(ridge, scattered(grams), vectors, [crosses[0]])
    reads = cross_reads(place, scattered(crosses), base, solved, head_count)
    reads = [reads[0]] + [swap(reads[i], "head", i) for i in range(1, head_count)]
    return output_rows(place, tokens, w_out, reads)


def solution(mesh):
    placed = (
        P(("grp", "head"), None),
        P(),
        P(),
        P(),
        P(),
        P("grp", None, None),
        P(),
        P("head"),
        P(),
        P("grp", None, "head", None),
        P("grp", None, "head", None),
        P(),
        P(),
        P(),
        P("grp", "head", None, None, None),
    )
    return jax.shard_map(
        shards, mesh=mesh, in_specs=placed, out_specs=P(("grp", "head"), None), check_vma=False
    )
```

```python
import functools

import jax
import jax.numpy as jnp
from jax import lax
from jax.experimental import pallas as pl
from jax.experimental.pallas import tpu as pltpu
from jax.sharding import PartitionSpec as P

HEADS = 8
HDIM = 128
CONV = 4
CG_STEPS = 8
PAGE = 128
CHUNK = 128
PAIR = 2 * CHUNK
EPS_NORM = 1e-06
PAGE_VMEM = 53
TOKEN_VMEM = 48
F32 = jnp.float32
BF16 = jnp.bfloat16


def swap(block, axis, distance):
    size = lax.axis_size(axis)
    return lax.ppermute(block, axis, [(i, i ^ distance) for i in range(size)])


def hold(block, other):
    anywhere = pl.BlockSpec(memory_space=pl.ANY)
    return pl.pallas_call(
        lambda *refs: None,
        in_specs=[anywhere, anywhere],
        out_specs=anywhere,
        out_shape=jax.ShapeDtypeStruct(block.shape, block.dtype),
        input_output_aliases={0: 0},
        compiler_params=pltpu.CompilerParams(vmem_limit_bytes=2**20),
        name="hold",
    )(block, other)


def dot(a, b):
    return jnp.dot(a, b, preferred_element_type=F32)


def silu(a):
    return a * jax.nn.sigmoid(a)


def unit_rows(a):
    return a * lax.rsqrt(jnp.sum(a * a, axis=-1, keepdims=True) + EPS_NORM)


def block_diag(a):
    zero = jnp.zeros((a.shape[0], CHUNK), a.dtype)
    return jnp.concatenate(
        [
            jnp.concatenate([a[:, :CHUNK], zero], axis=1),
            jnp.concatenate([zero, a[:, CHUNK:]], axis=1),
        ],
        axis=0,
    )


def sums_kernel(heads, owners, pages, table_ref, keys_hbm, values_hbm,
                prompt_hbm, send_gram, send_cross, keep_gram, keep_cross,
                acc_ref, keys_ref, values_ref, stored_ref, code_ref, key_sem, value_sem, sem):
    pool, rows = keys_ref.shape[0], keys_ref.shape[1]
    blocks = pool // pages
    slots = table_ref.shape[1]
    mine = lax.axis_index("grp")

    def load(block):
        at = pl.ds(block * pages, pages)
        return (
            pltpu.make_async_copy(keys_hbm.at[at], keys_ref.at[at], key_sem.at[block]),
            pltpu.make_async_copy(values_hbm.at[at], values_ref.at[at], value_sem.at[block]),
        )

    for block in range(blocks):
        for copy in load(block):
            copy.start()
    load_prompt = pltpu.make_async_copy(prompt_hbm, stored_ref, sem)
    load_prompt.start()
    acc_ref[...] = jnp.zeros_like(acc_ref)

    first = mine * pool
    wide = 16
    for owner in range(owners):

        def note(chunk, carry):
            for i in range(wide):
                slot = chunk * wide + i
                page = table_ref[owner, slot] - first
                inside = (page >= 0) & (page < pool)
                code_ref[jnp.where(inside, page, pool)] = owner * slots + slot
            return carry

        lax.fori_loop(0, slots // wide, note, 0)

    lane = lax.broadcasted_iota(jnp.int32, (HDIM, rows), 1)

    def place(page):
        code = code_ref[page]
        owner = lax.div(code, jnp.int32(slots))
        slot = code - owner * slots
        return owner, jnp.clip(table_ref[owners, owner] - slot * PAGE, 0, PAGE)

    def add(page, owner, turned):
        zero = jnp.zeros_like(turned)
        left = turned
        if heads > 1:
            left = jnp.concatenate(
                [jnp.where(lane % heads == head, turned, zero) for head in range(heads)], axis=0
            )
        right = jnp.concatenate([keys_ref[page], values_ref[page]], axis=1)
        acc_ref[owner] += dot(left, right)

    def one_block(block, carry):
        for copy in load(block):
            copy.wait()
        partial = jnp.int32(0)
        for i in range(pages):
            page = block * pages + i
            owner, live = place(page)
            add(page, jnp.where(live == PAGE, owner, owners), keys_ref[page].T)
            partial = partial | ((live > 0) & (live < PAGE)).astype(jnp.int32)

        @pl.when(partial > 0)
        def _():
            def one_page(page, inner):
                owner, live = place(page)

                @pl.when((live > 0) & (live < PAGE))
                def _():
                    turned = keys_ref[page].T
                    add(page, owner, jnp.where(lane < live * heads, turned, jnp.zeros_like(turned)))

                return inner

            lax.fori_loop(block * pages, (block + 1) * pages, one_page, 0)

        return carry

    lax.fori_loop(0, blocks, one_block, 0)
    load_prompt.wait()
    stored = stored_ref.shape[0]

    def add_prompt(owner, carry):
        for slot in range(stored):

            @pl.when(table_ref[owners + 1, owner] == mine * stored + slot)
            def _():
                for head in range(heads):
                    at = slice(head * HDIM, (head + 1) * HDIM)
                    acc_ref[owner, at, :HDIM] += stored_ref[slot, head, 0]
                    acc_ref[owner, at, HDIM:] += stored_ref[slot, head, 1].T

        return carry

    lax.fori_loop(0, owners, add_prompt, 0)
    bit = mine & 1
    for pair in range(owners // 2):
        there, here = 2 * pair + 1 - bit, 2 * pair + bit
        send_gram[pair] = acc_ref[there, :, :HDIM].astype(BF16)
        send_cross[pair] = acc_ref[there, :, HDIM:].astype(BF16)
        keep_gram[pair] = acc_ref[here, :, :HDIM].astype(BF16)
        keep_cross[pair] = acc_ref[here, :, HDIM:].astype(BF16)


def page_sums(table, keys, values, prompt_state, owners):
    pool, rows, _ = keys.shape
    heads = prompt_state.shape[1]
    pages = 8
    half = (owners // 2, heads * HDIM, HDIM)
    small = pl.BlockSpec(memory_space=pltpu.SMEM)
    anywhere = pl.BlockSpec(memory_space=pl.ANY)
    return pl.pallas_call(
        functools.partial(sums_kernel, heads, owners, pages),
        in_specs=[small] + [anywhere] * 3,
        out_specs=[pl.BlockSpec(memory_space=pltpu.VMEM)] * 4,
        scratch_shapes=[
            pltpu.VMEM((owners + 1, heads * HDIM, 2 * HDIM), F32),
            pltpu.VMEM(keys.shape, BF16),
            pltpu.VMEM(values.shape, BF16),
            pltpu.VMEM(prompt_state.shape, F32),
            pltpu.SMEM((pool + 1,), jnp.int32),
            pltpu.SemaphoreType.DMA((pool // pages,)),
            pltpu.SemaphoreType.DMA((pool // pages,)),
            pltpu.SemaphoreType.DMA,
        ],
        out_shape=[jax.ShapeDtypeStruct(half, BF16)] * 4,
        compiler_params=pltpu.CompilerParams(vmem_limit_bytes=PAGE_VMEM * 2**20),
        cost_estimate=pl.CostEstimate(
            flops=8 * pool * rows * heads * HDIM * HDIM,
            bytes_accessed=4 * pool * rows * HDIM,
            transcendentals=0,
        ),
        name="page_sums",
    )(table, keys, values, prompt_state)


def halve_kernel(keep_ref, got_ref, *outs):
    for distance, out_ref in enumerate(outs):
        row = (lax.axis_index("grp") >> 1) ^ distance
        total = keep_ref[row].astype(F32) + got_ref[row].astype(F32)
        out_ref[...] = total.astype(out_ref.dtype)


def halve_sums(keep, got):
    count, rows, cols = keep.shape
    outs = [jax.ShapeDtypeStruct((rows, cols), F32 if i == 0 else BF16) for i in range(count)]
    whole = pl.BlockSpec(memory_space=pltpu.VMEM)
    return pl.pallas_call(
        halve_kernel,
        in_specs=[whole, whole],
        out_specs=[whole] * count,
        out_shape=outs,
        compiler_params=pltpu.CompilerParams(vmem_limit_bytes=32 * 2**20),
        cost_estimate=pl.CostEstimate(
            flops=count * rows * cols, bytes_accessed=6 * count * rows * cols, transcendentals=0
        ),
        name="halve_sums",
    )(keep, got)


def token_kernel(heads, place_ref, rate_ref, *refs):
    head_count = HEADS // heads
    blocks = refs[:head_count]
    (gain_ref, w_ref, wg_ref, taps_ref, state_ref) = refs[head_count : head_count + 5]
    (q_ref, k_ref, kt_ref, vt_ref, weight_ref, prefix_ref, rows_ref) = refs[-9:-2]
    ext_ref, gate_ref = refs[-2:]
    me = place_ref[0]
    tok_rows = blocks[0].shape[0]
    length = tok_rows * head_count
    chunks = length // CHUNK
    base = 8
    ext_ref[base - (CONV - 1) : base, :] = state_ref[0].astype(F32)
    gate_ref[...] = jnp.zeros_like(gate_ref)
    for distance, block in enumerate(blocks):
        first = pl.multiple_of((me ^ distance) * tok_rows, tok_rows)
        wide = block[...].astype(F32)
        scale = lax.rsqrt(jnp.mean(wide * wide, axis=-1, keepdims=True) + EPS_NORM)
        normed = (wide * scale * gain_ref[...]).astype(BF16)
        mixed = dot(normed, w_ref[...]).astype(BF16)
        ext_ref[pl.ds(pl.multiple_of(base + first, 8), tok_rows), :] = mixed.astype(F32)
        gate_ref[pl.ds(first, tok_rows), : 2 * HEADS] = dot(normed, wg_ref[...])

    shift = lax.rem(HDIM - 2 * heads * me, HDIM)
    logits = pltpu.roll(gate_ref[...], shift, 1)
    lane = lax.broadcasted_iota(jnp.int32, (1, HDIM), 1)
    rate = jnp.zeros((1, HDIM), F32)
    for head in range(heads):
        rate = jnp.where(lane == 2 * head + 1, rate_ref[me * heads + head], rate)
    write = jax.nn.sigmoid(logits).astype(BF16).astype(F32)
    soft = jnp.maximum(logits, 0.0) + jnp.log1p(jnp.exp(-jnp.abs(logits)))
    decay = (-rate * soft).astype(BF16)
    here = lax.broadcasted_iota(jnp.int32, (CHUNK, CHUNK), 0)
    there = lax.broadcasted_iota(jnp.int32, (CHUNK, CHUNK), 1)
    lower = (here >= there).astype(F32).astype(BF16)
    cumul = [dot(lower, decay[c * CHUNK : (c + 1) * CHUNK]) for c in range(chunks)]
    turned = [block.T for block in cumul]

    for head in range(heads):
        parts = []
        for part in range(3):
            cols = slice((3 * head + part) * HDIM, (3 * head + part + 1) * HDIM)
            total = taps_ref[CONV - 1 : CONV, cols] * ext_ref[base : base + length, cols]
            for lag in range(1, CONV):
                total = total + taps_ref[CONV - 1 - lag : CONV - lag, cols] * (
                    ext_ref[base - lag : base - lag + length, cols]
                )
            parts.append(total)
        query = unit_rows(silu(parts[0])).astype(BF16)
        key = unit_rows(silu(parts[1])).astype(BF16)
        value = parts[2].astype(BF16)
        q_ref[head] = query.T
        k_ref[head] = key
        kt_ref[head] = key.T
        vt_ref[head] = value.T
        prefix = jnp.zeros((HDIM, 2 * HDIM), F32)
        so_far = jnp.zeros((1, 1), F32)
        for c in range(chunks):
            rows = slice(c * CHUNK, (c + 1) * CHUNK)
            col = cumul[c][:, 2 * head + 1 : 2 * head + 2]
            row = turned[c][2 * head + 1 : 2 * head + 2, :]
            gate = write[rows, 2 * head : 2 * head + 1]
            spread = jnp.exp(jnp.minimum(row - col, 0.0)) * gate
            half = slice((c % 2) * CHUNK, (c % 2 + 1) * CHUNK)
            weight_ref[head, c // 2, :, half] = jnp.where(here <= there, spread, 0.0)
            rows_ref[head, c // 2, 0:1, half] = jnp.exp(row)
            rows_ref[head, c // 2, 1:2, half] = jnp.broadcast_to(jnp.exp(so_far), (1, CHUNK))
            prefix_ref[head, c, :HDIM] = prefix[:, :HDIM]
            prefix_ref[head, c, HDIM:] = prefix[:, HDIM:].T
            if c + 1 < chunks:
                whole = cumul[c][CHUNK - 1 :, 2 * head + 1 : 2 * head + 2]
                carry = jnp.exp(whole - col) * gate
                both = jnp.concatenate([key[rows], value[rows]], axis=1).astype(F32)
                prefix = prefix * jnp.exp(whole) + dot(
                    kt_ref[head, :, rows], (both * carry).astype(BF16)
                )
                so_far = so_far + whole


def token_vectors(
    place, decay_rate, blocks, norm_gain, w_qkv, w_gates, conv_weight, conv_state, held
):
    head_count = len(blocks)
    heads = HEADS // head_count
    width = heads * 3 * HDIM
    tok_rows, model = blocks[0].shape
    length = head_count * tok_rows
    chunks = length // CHUNK

    anywhere = pl.BlockSpec(memory_space=pl.ANY)

    def full(shape):
        return pl.BlockSpec(shape, lambda i, *_: (0,) * len(shape))

    outs = [
        jax.ShapeDtypeStruct((heads, HDIM, length), BF16),
        jax.ShapeDtypeStruct((heads, length, HDIM), BF16),
        jax.ShapeDtypeStruct((heads, HDIM, length), BF16),
        jax.ShapeDtypeStruct((heads, HDIM, length), BF16),
        jax.ShapeDtypeStruct((heads, chunks // 2, CHUNK, PAIR), F32),
        jax.ShapeDtypeStruct((heads, chunks, 2 * HDIM, HDIM), F32),
        jax.ShapeDtypeStruct((heads, chunks // 2, 8, PAIR), F32),
    ]
    return pl.pallas_call(
        functools.partial(token_kernel, heads),
        grid_spec=pltpu.PrefetchScalarGridSpec(
            num_scalar_prefetch=2,
            grid=(1,),
            in_specs=[full(b.shape) for b in blocks]
            + [
                full((1, model)),
                pl.BlockSpec((model, width), lambda i, place, rate: (0, place[0])),
                full(w_gates.shape),
                pl.BlockSpec((CONV, width), lambda i, place, rate: (0, place[0])),
                pl.BlockSpec((1, CONV - 1, width), lambda i, place, rate: (0, 0, place[0])),
            ]
            + [anywhere],
            out_specs=[anywhere] + [full(o.shape) for o in outs],
            scratch_shapes=[pltpu.VMEM((8 + length, width), F32), pltpu.VMEM((length, HDIM), F32)],
        ),
        out_shape=[jax.ShapeDtypeStruct(held.shape, held.dtype)] + outs,
        input_output_aliases={2 + len(blocks) + 5: 0},
        compiler_params=pltpu.CompilerParams(vmem_limit_bytes=TOKEN_VMEM * 2**20),
        cost_estimate=pl.CostEstimate(
            flops=2 * length * model * width,
            bytes_accessed=2 * model * (length + width) + 4 * 2**20,
            transcendentals=length * width,
        ),
        name="token_vectors",
    )(
        place,
        decay_rate,
        *blocks,
        norm_gain.reshape(1, model),
        w_qkv,
        w_gates,
        conv_weight,
        conv_state,
        held,
    )


def read_kernel(heads, terms, ridge_ref, *refs):
    grams = refs[:terms]
    (q_ref, k_ref, kt_ref, vt_ref, weight_ref, prefix_ref, rows_ref) = refs[terms : terms + 7]
    base_ref, solved_ref, left_ref, x_ref, r_ref, d_ref = refs[-6:]
    pairs = q_ref.shape[2] // PAIR
    groups = [(head, pair) for head in range(heads) for pair in range(pairs)]
    norms = []
    for head in range(heads):
        rows = slice(head * HDIM, (head + 1) * HDIM)
        gram = grams[0][rows, :].astype(F32)
        for term in grams[1:]:
            gram = gram + term[rows, :].astype(F32)
        for pair in range(pairs):
            for side in range(2):
                c = 2 * pair + side
                half = slice(side * CHUNK, (side + 1) * CHUNK)
                scale = rows_ref[head, pair, 1:2, half]
                left_ref[head, pair, :HDIM, half] = (
                    gram * scale + prefix_ref[head, c, :HDIM]
                ).astype(BF16)
                left_ref[head, pair, HDIM:, half] = k_ref[head, c * CHUNK : (c + 1) * CHUNK]
            query = q_ref[head, :, pair * PAIR : (pair + 1) * PAIR].astype(F32)
            x_ref[head, pair] = jnp.zeros_like(query)
            r_ref[head, pair] = query
            d_ref[head, pair] = query
            norms.append(jnp.sum(query * query, axis=0, keepdims=True))

    def one_step(_, norms):
        firsts = [dot(left_ref[g], block_diag(d_ref[g].astype(BF16))) for g in groups]
        seconds = []
        for (head, pair), first in zip(groups, firsts):
            scores = (first[HDIM:] * weight_ref[head, pair]).astype(BF16)
            seconds.append(
                dot(kt_ref[head, :, pair * PAIR : (pair + 1) * PAIR], block_diag(scores))
            )
        later = []
        for (head, pair), first, second, norm in zip(groups, firsts, seconds, norms):
            direction = d_ref[head, pair]
            image = (
                rows_ref[head, pair, 0:1] * first[:HDIM] + ridge_ref[head] * direction + second
            )
            alpha = norm / jnp.sum(direction * image, axis=0, keepdims=True)
            x_ref[head, pair] += alpha * direction
            residue = r_ref[head, pair] - alpha * image
            r_ref[head, pair] = residue
            norm_next = jnp.sum(residue * residue, axis=0, keepdims=True)
            d_ref[head, pair] = residue + norm_next / norm * direction
            later.append(norm_next)
        return tuple(later)

    lax.fori_loop(0, CG_STEPS, one_step, tuple(norms), unroll=2)
    for head, pair in groups:
        cols = slice(head * HDIM, (head + 1) * HDIM)
        span = slice(pair * PAIR, (pair + 1) * PAIR)
        for side in range(2):
            half = slice(side * CHUNK, (side + 1) * CHUNK)
            left_ref[head, pair, :HDIM, half] = prefix_ref[head, 2 * pair + side, HDIM:].astype(BF16)
        solved = x_ref[head, pair]
        first = dot(left_ref[head, pair], block_diag(solved.astype(BF16)))
        scores = (first[HDIM:] * weight_ref[head, pair]).astype(BF16)
        carry = rows_ref[head, pair, 0:1]
        read = carry * first[:HDIM] + dot(vt_ref[head, :, span], block_diag(scores))
        base_ref[span, cols] = read.T
        solved_ref[span, cols] = (solved * (carry * rows_ref[head, pair, 1:2])).T.astype(BF16)


def ridge_reads(ridge, grams, vectors, after=()):
    heads, _, length = vectors[0].shape
    pairs = length // PAIR
    whole = pl.BlockSpec(memory_space=pltpu.VMEM)
    state = pltpu.VMEM((heads, pairs, HDIM, PAIR), F32)
    return pl.pallas_call(
        functools.partial(read_kernel, heads, len(grams)),
        in_specs=[pl.BlockSpec(memory_space=pltpu.SMEM)]
        + [whole] * (len(grams) + len(vectors))
        + [whole] * len(after),
        out_specs=[whole] * 2,
        out_shape=[
            jax.ShapeDtypeStruct((length, heads * HDIM), F32),
            jax.ShapeDtypeStruct((length, heads * HDIM), BF16),
        ],
        scratch_shapes=[pltpu.VMEM((heads, pairs, 2 * HDIM, PAIR), BF16), state, state, state],
        compiler_params=pltpu.CompilerParams(vmem_limit_bytes=32 * 2**20),
        cost_estimate=pl.CostEstimate(
            flops=CG_STEPS * heads * pairs * 6 * CHUNK**3 * 16,
            bytes_accessed=8 * 2**20,
            transcendentals=0,
        ),
        name="ridge_reads",
    )(ridge, *grams, *vectors, *after)


def cross_kernel(heads, terms, place_ref, *refs):
    crosses, (base_ref, solved_ref) = refs[:terms], refs[terms : terms + 2]
    outs, o_ref = refs[terms + 2 : -1], refs[-1]
    me = place_ref[0]
    for head in range(heads):
        cols = slice(head * HDIM, (head + 1) * HDIM)
        cross = crosses[0][cols, :].astype(F32)
        for term in crosses[1:]:
            cross = cross + term[cols, :].astype(F32)
        read = base_ref[:, cols] + dot(solved_ref[:, cols], cross.astype(BF16))
        o_ref[:, cols] = read.astype(BF16)
    tok_rows = outs[0].shape[0]
    for distance, out_ref in enumerate(outs):
        first_row = pl.multiple_of((me ^ distance) * tok_rows, tok_rows)
        out_ref[...] = o_ref[pl.ds(first_row, tok_rows), :]


def cross_reads(place, crosses, base, solved, head_count):
    length, width = base.shape
    whole = pl.BlockSpec(memory_space=pltpu.VMEM)
    return pl.pallas_call(
        functools.partial(cross_kernel, width // HDIM, len(crosses)),
        in_specs=[pl.BlockSpec(memory_space=pltpu.SMEM)] + [whole] * (len(crosses) + 2),
        out_specs=[whole] * head_count,
        out_shape=[jax.ShapeDtypeStruct((length // head_count, width), BF16)] * head_count,
        scratch_shapes=[pltpu.VMEM((length, width), BF16)],
        compiler_params=pltpu.CompilerParams(vmem_limit_bytes=24 * 2**20),
        cost_estimate=pl.CostEstimate(
            flops=2 * length * width * HDIM, bytes_accessed=8 * length * width, transcendentals=0
        ),
        name="cross_reads",
    )(place, *crosses, base, solved)


def output_kernel(place_ref, tokens_ref, w_ref, *refs):
    out_ref = refs[-1]
    me = place_ref[0]
    total = tokens_ref[...].astype(F32)
    for distance, part in enumerate(refs[:-1]):
        width = part.shape[1]
        first = pl.multiple_of((me ^ distance) * width, width)
        total = total + dot(part[...], w_ref[pl.ds(first, width), :])
    out_ref[...] = total.astype(BF16)


def output_rows(place, tokens, w_out, reads):
    whole = pl.BlockSpec(memory_space=pltpu.VMEM)
    return pl.pallas_call(
        output_kernel,
        in_specs=[pl.BlockSpec(memory_space=pltpu.SMEM)] + [whole] * (2 + len(reads)),
        out_specs=whole,
        out_shape=jax.ShapeDtypeStruct(tokens.shape, BF16),
        compiler_params=pltpu.CompilerParams(vmem_limit_bytes=24 * 2**20),
        cost_estimate=pl.CostEstimate(
            flops=2 * tokens.shape[0] * w_out.shape[0] * w_out.shape[1],
            bytes_accessed=2 * w_out.size + 6 * tokens.size,
            transcendentals=0,
        ),
        name="output_rows",
    )(place, tokens, w_out, *reads)


def shards(
    tokens,
    norm_gain,
    w_qkv,
    w_gates,
    conv_weight,
    conv_state,
    decay_rate,
    ridge,
    w_out,
    cache_keys,
    cache_values,
    page_table,
    cache_lengths,
    group_prompt,
    prompt_state,
):
    head_count = lax.axis_size("head")
    owners = lax.axis_size("grp")
    me = lax.axis_index("head").astype(jnp.int32)
    place = me.reshape(1)
    bits = [head_count >> i for i in range(1, head_count.bit_length())]
    blocks = {0: tokens}
    for bit in bits:
        blocks[bit] = swap(tokens, "head", bit)

    pool, page, heads, _ = cache_keys.shape
    spare = (0, page_table.shape[1] - owners)
    rows = [jnp.pad(row, spare)[None] for row in (cache_lengths, group_prompt)]
    table = jnp.concatenate([page_table] + rows, axis=0)
    keys = cache_keys.reshape(pool, page * heads, HDIM)
    values = cache_values.reshape(pool, page * heads, HDIM)

    def scattered(parts):
        return [parts[0]] + [swap(parts[i], "grp", 2 * i) for i in range(1, owners // 2)]

    send_gram, send_cross, keep_gram, keep_cross = page_sums(
        table, keys, values, prompt_state, owners
    )
    got_gram = swap(send_gram, "grp", 1)
    for bit in bits[1:]:
        for distance in list(blocks):
            if distance and not distance & bit and distance ^ bit not in blocks:
                blocks[distance] = hold(blocks[distance], keep_gram)
                blocks[distance ^ bit] = swap(blocks[distance], "head", bit)
    blocks = [blocks[i] for i in range(head_count)]
    send_cross, *vectors = token_vectors(
        place, decay_rate, blocks, norm_gain, w_qkv, w_gates, conv_weight, conv_state, send_cross
    )
    grams = halve_sums(keep_gram, got_gram)
    crosses = halve_sums(keep_cross, swap(send_cross, "grp", 1))
    base, solved = ridge_reads(ridge, scattered(grams), vectors, [crosses[0]])
    reads = cross_reads(place, scattered(crosses), base, solved, head_count)
    reads = [reads[0]] + [swap(reads[i], "head", i) for i in range(1, head_count)]
    return output_rows(place, tokens, w_out, reads)


def solution(mesh):
    placed = (
        P(("grp", "head"), None),
        P(),
        P(),
        P(),
        P(),
        P("grp", None, None),
        P(),
        P("head"),
        P(),
        P("grp", None, "head", None),
        P("grp", None, "head", None),
        P(),
        P(),
        P(),
        P("grp", "head", None, None, None),
    )
    return jax.shard_map(
        shards, mesh=mesh, in_specs=placed, out_specs=P(("grp", "head"), None), check_vma=False
    )
```

```python
import functools

import jax
import jax.numpy as jnp
from jax import lax
from jax.experimental import pallas as pl
from jax.experimental.pallas import tpu as pltpu
from jax.sharding import PartitionSpec as P

HEADS = 8
HDIM = 128
CONV = 4
CG_STEPS = 8
PAGE = 128
CHUNK = 128
PAIR = 2 * CHUNK
EPS_NORM = 1e-06
PAGE_VMEM = 53
TOKEN_VMEM = 48
F32 = jnp.float32
BF16 = jnp.bfloat16


def swap(block, axis, distance):
    size = lax.axis_size(axis)
    return lax.ppermute(block, axis, [(i, i ^ distance) for i in range(size)])


def hold(block, other):
    anywhere = pl.BlockSpec(memory_space=pl.ANY)
    return pl.pallas_call(
        lambda *refs: None,
        in_specs=[anywhere, anywhere],
        out_specs=anywhere,
        out_shape=jax.ShapeDtypeStruct(block.shape, block.dtype),
        input_output_aliases={0: 0},
        compiler_params=pltpu.CompilerParams(vmem_limit_bytes=2**20),
        name="hold",
    )(block, other)


def dot(a, b):
    return jnp.dot(a, b, preferred_element_type=F32)


def silu(a):
    return a * jax.nn.sigmoid(a)


def unit_rows(a):
    return a * lax.rsqrt(jnp.sum(a * a, axis=-1, keepdims=True) + EPS_NORM)


def block_diag(a):
    zero = jnp.zeros((a.shape[0], CHUNK), a.dtype)
    return jnp.concatenate(
        [
            jnp.concatenate([a[:, :CHUNK], zero], axis=1),
            jnp.concatenate([zero, a[:, CHUNK:]], axis=1),
        ],
        axis=0,
    )


def sums_kernel(heads, owners, table_hbm, keys_hbm, values_hbm, prompt_hbm,
                send_gram, send_cross, keep_gram, keep_cross,
                acc_ref, keys_ref, values_ref, stored_ref, table_ref, list_ref,
                key_sem, value_sem, small_sem):
    pool, rows = keys_hbm.shape[0], keys_hbm.shape[1]
    slots = table_hbm.shape[1]
    mine = lax.axis_index("grp")
    load_table = pltpu.make_async_copy(table_hbm, table_ref, small_sem.at[0])
    load_prompt = pltpu.make_async_copy(prompt_hbm, stored_ref, small_sem.at[1])
    load_table.start()
    load_prompt.start()
    acc_ref[...] = jnp.zeros_like(acc_ref)
    load_table.wait()

    def load(item):
        page = list_ref[item] & 0xFFFF
        return (
            pltpu.make_async_copy(keys_hbm.at[page], keys_ref.at[item], key_sem.at[item]),
            pltpu.make_async_copy(values_hbm.at[page], values_ref.at[item], value_sem.at[item]),
        )

    def start(item, carry):
        for copy in load(item):
            copy.start()
        return carry

    first = mine * pool
    wide = 8
    count = jnp.int32(0)
    for owner in range(owners):

        def note(chunk, count):
            for i in range(wide):
                entry = table_ref[owner, chunk * wide + i]
                page = (entry & 0xFFFF) - first
                live = entry & 0xFF0000
                list_ref[count] = (owner << 24) | live | (page & 0xFFFF)
                inside = (page >= 0) & (page < pool) & (live > 0)
                count = count + inside.astype(jnp.int32)
            return count

        chunks = jnp.int32(0)
        for slot in range(0, slots, wide):
            chunks = chunks + ((table_ref[owner, slot] & 0xFF0000) > 0).astype(jnp.int32)
        before = count
        count = lax.fori_loop(0, chunks, note, before)
        lax.fori_loop(before, count, start, 0)

    turn = 4
    turns = (count + (turn - 1)) >> 2

    def fill(item, carry):
        list_ref[item] = jnp.int32(owners << 24)
        return start(item, carry)

    lax.fori_loop(count, turns * turn, fill, 0)

    lane = lax.broadcasted_iota(jnp.int32, (HDIM, rows), 1)

    def one_turn(step, carry):
        for i in range(turn):
            for copy in load(step * turn + i):
                copy.wait()
        for i in range(turn):
            item = step * turn + i
            code = list_ref[item]
            owner, live = code >> 24, (code >> 16) & 0xFF
            keys = keys_ref[item]
            turned = keys.T
            zero = jnp.zeros_like(turned)
            left = jnp.concatenate(
                [
                    jnp.where((lane % heads == head) & (lane < live * heads), turned, zero)
                    for head in range(heads)
                ],
                axis=0,
            )
            acc_ref[owner] += dot(left, jnp.concatenate([keys, values_ref[item]], axis=1))
        return carry

    lax.fori_loop(0, turns, one_turn, 0)
    load_prompt.wait()
    stored = stored_ref.shape[0]

    def add_prompt(owner, carry):
        for slot in range(stored):

            @pl.when((table_ref[owner, 0] >> 24) == mine * stored + slot)
            def _():
                for head in range(heads):
                    at = slice(head * HDIM, (head + 1) * HDIM)
                    acc_ref[owner, at, :HDIM] += stored_ref[slot, head, 0]
                    acc_ref[owner, at, HDIM:] += stored_ref[slot, head, 1].T

        return carry

    lax.fori_loop(0, owners, add_prompt, 0)
    bit = mine & 1
    for pair in range(owners // 2):
        there, here = 2 * pair + 1 - bit, 2 * pair + bit
        send_gram[pair] = acc_ref[there, :, :HDIM].astype(BF16)
        send_cross[pair] = acc_ref[there, :, HDIM:].astype(BF16)
        keep_gram[pair] = acc_ref[here, :, :HDIM].astype(BF16)
        keep_cross[pair] = acc_ref[here, :, HDIM:].astype(BF16)


def page_sums(table, keys, values, prompt_state, owners):
    pool, rows, _ = keys.shape
    heads = prompt_state.shape[1]
    half = (owners // 2, heads * HDIM, HDIM)
    items = pool + 4
    return pl.pallas_call(
        functools.partial(sums_kernel, heads, owners),
        in_specs=[pl.BlockSpec(memory_space=pl.ANY)] * 4,
        out_specs=[pl.BlockSpec(memory_space=pltpu.VMEM)] * 4,
        scratch_shapes=[
            pltpu.VMEM((owners + 1, heads * HDIM, 2 * HDIM), F32),
            pltpu.VMEM((items, rows, HDIM), BF16),
            pltpu.VMEM((items, rows, HDIM), BF16),
            pltpu.VMEM(prompt_state.shape, F32),
            pltpu.SMEM(table.shape, jnp.int32),
            pltpu.SMEM((items,), jnp.int32),
            pltpu.SemaphoreType.DMA((items,)),
            pltpu.SemaphoreType.DMA((items,)),
            pltpu.SemaphoreType.DMA((2,)),
        ],
        out_shape=[jax.ShapeDtypeStruct(half, BF16)] * 4,
        compiler_params=pltpu.CompilerParams(vmem_limit_bytes=PAGE_VMEM * 2**20),
        cost_estimate=pl.CostEstimate(
            flops=8 * pool * rows * heads * HDIM * HDIM,
            bytes_accessed=4 * pool * rows * HDIM,
            transcendentals=0,
        ),
        name="page_sums",
    )(table, keys, values, prompt_state)


def halve_kernel(keep_ref, got_ref, *outs):
    for distance, out_ref in enumerate(outs):
        row = (lax.axis_index("grp") >> 1) ^ distance
        total = keep_ref[row].astype(F32) + got_ref[row].astype(F32)
        out_ref[...] = total.astype(out_ref.dtype)


def halve_sums(keep, got):
    count, rows, cols = keep.shape
    outs = [jax.ShapeDtypeStruct((rows, cols), F32 if i == 0 else BF16) for i in range(count)]
    whole = pl.BlockSpec(memory_space=pltpu.VMEM)
    return pl.pallas_call(
        halve_kernel,
        in_specs=[whole, whole],
        out_specs=[whole] * count,
        out_shape=outs,
        compiler_params=pltpu.CompilerParams(vmem_limit_bytes=32 * 2**20),
        cost_estimate=pl.CostEstimate(
            flops=count * rows * cols, bytes_accessed=6 * count * rows * cols, transcendentals=0
        ),
        name="halve_sums",
    )(keep, got)


def token_kernel(heads, *refs):
    head_count = HEADS // heads
    blocks = refs[:head_count]
    (gain_ref, w_hbm, wg_ref, taps_all, state_ref, rate_ref) = refs[head_count : head_count + 6]
    (q_ref, k_ref, kt_ref, vt_ref, weight_ref, prefix_ref, rows_ref) = refs[-12:-5]
    ext_ref, gate_ref, normed_ref, w_ref, w_sem = refs[-5:]
    me = lax.axis_index("head")
    tok_rows = blocks[0].shape[0]
    width = w_ref.shape[1]
    columns = pl.ds(pl.multiple_of(me * width, HDIM), width)
    load = pltpu.make_async_copy(w_hbm.at[:, columns], w_ref, w_sem)
    load.start()
    length = tok_rows * head_count
    chunks = length // CHUNK
    base = 8
    taps_ref = taps_all[:, columns]
    ext_ref[base - (CONV - 1) : base, :] = state_ref[0, :, columns].astype(F32)
    gate_ref[...] = jnp.zeros_like(gate_ref)
    for distance, block in enumerate(blocks):
        first = pl.multiple_of((me ^ distance) * tok_rows, tok_rows)
        wide = block[...].astype(F32)
        scale = lax.rsqrt(jnp.mean(wide * wide, axis=-1, keepdims=True) + EPS_NORM)
        normed = (wide * scale * gain_ref[...]).astype(BF16)
        normed_ref[pl.ds(first, tok_rows), :] = normed
        gate_ref[pl.ds(first, tok_rows), : 2 * HEADS] = dot(normed, wg_ref[...])
    load.wait()
    for c in range(chunks):
        rows = slice(c * CHUNK, (c + 1) * CHUNK)
        mixed = dot(normed_ref[rows, :], w_ref[...]).astype(BF16)
        ext_ref[base + c * CHUNK : base + (c + 1) * CHUNK, :] = mixed.astype(F32)

    shift = lax.rem(HDIM - 2 * heads * me, HDIM)
    logits = pltpu.roll(gate_ref[...], shift, 1)
    lane = lax.broadcasted_iota(jnp.int32, (1, HDIM), 1)
    rate = jnp.zeros((1, HDIM), F32)
    for head in range(heads):
        here = lax.broadcasted_iota(jnp.int32, (1, HEADS), 1) == me * heads + head
        own = jnp.sum(jnp.where(here, rate_ref[...], 0.0), axis=1, keepdims=True)
        rate = jnp.where(lane == 2 * head + 1, own, rate)
    write = jax.nn.sigmoid(logits).astype(BF16).astype(F32)
    soft = jnp.maximum(logits, 0.0) + jnp.log1p(jnp.exp(-jnp.abs(logits)))
    decay = (-rate * soft).astype(BF16)
    here = lax.broadcasted_iota(jnp.int32, (CHUNK, CHUNK), 0)
    there = lax.broadcasted_iota(jnp.int32, (CHUNK, CHUNK), 1)
    lower = (here >= there).astype(F32).astype(BF16)
    cumul = [dot(lower, decay[c * CHUNK : (c + 1) * CHUNK]) for c in range(chunks)]
    turned = [block.T for block in cumul]

    for head in range(heads):
        parts = []
        for part in range(3):
            cols = slice((3 * head + part) * HDIM, (3 * head + part + 1) * HDIM)
            total = taps_ref[CONV - 1 : CONV, cols] * ext_ref[base : base + length, cols]
            for lag in range(1, CONV):
                total = total + taps_ref[CONV - 1 - lag : CONV - lag, cols] * (
                    ext_ref[base - lag : base - lag + length, cols]
                )
            parts.append(total)
        query = unit_rows(silu(parts[0])).astype(BF16)
        key = unit_rows(silu(parts[1])).astype(BF16)
        value = parts[2].astype(BF16)
        q_ref[head] = query.T
        k_ref[head] = key
        kt_ref[head] = key.T
        vt_ref[head] = value.T
        prefix = jnp.zeros((HDIM, 2 * HDIM), F32)
        so_far = jnp.zeros((1, 1), F32)
        for c in range(chunks):
            rows = slice(c * CHUNK, (c + 1) * CHUNK)
            col = cumul[c][:, 2 * head + 1 : 2 * head + 2]
            row = turned[c][2 * head + 1 : 2 * head + 2, :]
            gate = write[rows, 2 * head : 2 * head + 1]
            spread = jnp.exp(jnp.minimum(row - col, 0.0)) * gate
            half = slice((c % 2) * CHUNK, (c % 2 + 1) * CHUNK)
            weight_ref[head, c // 2, :, half] = jnp.where(here <= there, spread, 0.0)
            rows_ref[head, c // 2, 0:1, half] = jnp.exp(row)
            rows_ref[head, c // 2, 1:2, half] = jnp.broadcast_to(jnp.exp(so_far), (1, CHUNK))
            prefix_ref[head, c, :HDIM] = prefix[:, :HDIM]
            prefix_ref[head, c, HDIM:] = prefix[:, HDIM:].T
            if c + 1 < chunks:
                whole = cumul[c][CHUNK - 1 :, 2 * head + 1 : 2 * head + 2]
                carry = jnp.exp(whole - col) * gate
                both = jnp.concatenate([key[rows], value[rows]], axis=1).astype(F32)
                prefix = prefix * jnp.exp(whole) + dot(
                    kt_ref[head, :, rows], (both * carry).astype(BF16)
                )
                so_far = so_far + whole


def token_vectors(
    decay_rate, blocks, norm_gain, w_qkv, w_gates, conv_weight, conv_state, held
):
    head_count = len(blocks)
    heads = HEADS // head_count
    width = heads * 3 * HDIM
    tok_rows, model = blocks[0].shape
    length = head_count * tok_rows
    chunks = length // CHUNK
    whole = pl.BlockSpec(memory_space=pltpu.VMEM)
    anywhere = pl.BlockSpec(memory_space=pl.ANY)
    outs = [
        jax.ShapeDtypeStruct((heads, HDIM, length), BF16),
        jax.ShapeDtypeStruct((heads, length, HDIM), BF16),
        jax.ShapeDtypeStruct((heads, HDIM, length), BF16),
        jax.ShapeDtypeStruct((heads, HDIM, length), BF16),
        jax.ShapeDtypeStruct((heads, chunks // 2, CHUNK, PAIR), F32),
        jax.ShapeDtypeStruct((heads, chunks, 2 * HDIM, HDIM), F32),
        jax.ShapeDtypeStruct((heads, chunks // 2, 8, PAIR), F32),
    ]
    return pl.pallas_call(
        functools.partial(token_kernel, heads),
        in_specs=[whole] * head_count + [whole, anywhere] + [whole] * 4 + [anywhere],
        out_specs=[anywhere] + [whole] * len(outs),
        scratch_shapes=[
            pltpu.VMEM((8 + length, width), F32),
            pltpu.VMEM((length, HDIM), F32),
            pltpu.VMEM((length, model), BF16),
            pltpu.VMEM((model, width), BF16),
            pltpu.SemaphoreType.DMA,
        ],
        out_shape=[jax.ShapeDtypeStruct(held.shape, held.dtype)] + outs,
        input_output_aliases={head_count + 6: 0},
        compiler_params=pltpu.CompilerParams(vmem_limit_bytes=TOKEN_VMEM * 2**20),
        cost_estimate=pl.CostEstimate(
            flops=2 * length * model * width,
            bytes_accessed=2 * model * (length + width) + 4 * 2**20,
            transcendentals=length * width,
        ),
        name="token_vectors",
    )(
        *blocks,
        norm_gain.reshape(1, model),
        w_qkv,
        w_gates,
        conv_weight,
        conv_state,
        decay_rate.reshape(1, HEADS),
        held,
    )


def read_kernel(heads, terms, ridge_ref, *refs):
    grams = refs[:terms]
    (q_ref, k_ref, kt_ref, vt_ref, weight_ref, prefix_ref, rows_ref) = refs[terms : terms + 7]
    base_ref, solved_ref, left_ref, x_ref, r_ref, d_ref = refs[-6:]
    pairs = q_ref.shape[2] // PAIR
    groups = [(head, pair) for head in range(heads) for pair in range(pairs)]
    norms = []
    for head in range(heads):
        rows = slice(head * HDIM, (head + 1) * HDIM)
        gram = grams[0][rows, :].astype(F32)
        for term in grams[1:]:
            gram = gram + term[rows, :].astype(F32)
        for pair in range(pairs):
            for side in range(2):
                c = 2 * pair + side
                half = slice(side * CHUNK, (side + 1) * CHUNK)
                scale = rows_ref[head, pair, 1:2, half]
                left_ref[head, pair, :HDIM, half] = (
                    gram * scale + prefix_ref[head, c, :HDIM]
                ).astype(BF16)
                left_ref[head, pair, HDIM:, half] = k_ref[head, c * CHUNK : (c + 1) * CHUNK]
            query = q_ref[head, :, pair * PAIR : (pair + 1) * PAIR].astype(F32)
            x_ref[head, pair] = jnp.zeros_like(query)
            r_ref[head, pair] = query
            d_ref[head, pair] = query
            norms.append(jnp.sum(query * query, axis=0, keepdims=True))

    def one_step(_, norms):
        firsts = [dot(left_ref[g], block_diag(d_ref[g].astype(BF16))) for g in groups]
        seconds = []
        for (head, pair), first in zip(groups, firsts):
            scores = (first[HDIM:] * weight_ref[head, pair]).astype(BF16)
            seconds.append(
                dot(kt_ref[head, :, pair * PAIR : (pair + 1) * PAIR], block_diag(scores))
            )
        later = []
        for (head, pair), first, second, norm in zip(groups, firsts, seconds, norms):
            direction = d_ref[head, pair]
            image = (
                rows_ref[head, pair, 0:1] * first[:HDIM] + ridge_ref[:, head : head + 1] * direction + second
            )
            alpha = norm / jnp.sum(direction * image, axis=0, keepdims=True)
            x_ref[head, pair] += alpha * direction
            residue = r_ref[head, pair] - alpha * image
            r_ref[head, pair] = residue
            norm_next = jnp.sum(residue * residue, axis=0, keepdims=True)
            d_ref[head, pair] = residue + norm_next / norm * direction
            later.append(norm_next)
        return tuple(later)

    lax.fori_loop(0, CG_STEPS, one_step, tuple(norms), unroll=2)
    for head, pair in groups:
        cols = slice(head * HDIM, (head + 1) * HDIM)
        span = slice(pair * PAIR, (pair + 1) * PAIR)
        for side in range(2):
            half = slice(side * CHUNK, (side + 1) * CHUNK)
            left_ref[head, pair, :HDIM, half] = prefix_ref[head, 2 * pair + side, HDIM:].astype(BF16)
        solved = x_ref[head, pair]
        first = dot(left_ref[head, pair], block_diag(solved.astype(BF16)))
        scores = (first[HDIM:] * weight_ref[head, pair]).astype(BF16)
        carry = rows_ref[head, pair, 0:1]
        read = carry * first[:HDIM] + dot(vt_ref[head, :, span], block_diag(scores))
        base_ref[span, cols] = read.T
        solved_ref[span, cols] = (solved * (carry * rows_ref[head, pair, 1:2])).T.astype(BF16)


def ridge_reads(ridge, grams, vectors, after=()):
    heads, _, length = vectors[0].shape
    pairs = length // PAIR
    whole = pl.BlockSpec(memory_space=pltpu.VMEM)
    state = pltpu.VMEM((heads, pairs, HDIM, PAIR), F32)
    return pl.pallas_call(
        functools.partial(read_kernel, heads, len(grams)),
        in_specs=[whole] * (1 + len(grams) + len(vectors))
        + [whole] * len(after),
        out_specs=[whole] * 2,
        out_shape=[
            jax.ShapeDtypeStruct((length, heads * HDIM), F32),
            jax.ShapeDtypeStruct((length, heads * HDIM), BF16),
        ],
        scratch_shapes=[pltpu.VMEM((heads, pairs, 2 * HDIM, PAIR), BF16), state, state, state],
        compiler_params=pltpu.CompilerParams(vmem_limit_bytes=32 * 2**20),
        cost_estimate=pl.CostEstimate(
            flops=CG_STEPS * heads * pairs * 6 * CHUNK**3 * 16,
            bytes_accessed=8 * 2**20,
            transcendentals=0,
        ),
        name="ridge_reads",
    )(ridge.reshape(1, heads), *grams, *vectors, *after)


def cross_kernel(heads, terms, *refs):
    crosses, (base_ref, solved_ref) = refs[:terms], refs[terms : terms + 2]
    outs, o_ref = refs[terms + 2 : -1], refs[-1]
    me = lax.axis_index("head")
    for head in range(heads):
        cols = slice(head * HDIM, (head + 1) * HDIM)
        cross = crosses[0][cols, :].astype(F32)
        for term in crosses[1:]:
            cross = cross + term[cols, :].astype(F32)
        read = base_ref[:, cols] + dot(solved_ref[:, cols], cross.astype(BF16))
        o_ref[:, cols] = read.astype(BF16)
    tok_rows = outs[0].shape[0]
    for distance, out_ref in enumerate(outs):
        first_row = pl.multiple_of((me ^ distance) * tok_rows, tok_rows)
        out_ref[...] = o_ref[pl.ds(first_row, tok_rows), :]


def cross_reads(crosses, base, solved, head_count):
    length, width = base.shape
    whole = pl.BlockSpec(memory_space=pltpu.VMEM)
    return pl.pallas_call(
        functools.partial(cross_kernel, width // HDIM, len(crosses)),
        in_specs=[whole] * (len(crosses) + 2),
        out_specs=[whole] * head_count,
        out_shape=[jax.ShapeDtypeStruct((length // head_count, width), BF16)] * head_count,
        scratch_shapes=[pltpu.VMEM((length, width), BF16)],
        compiler_params=pltpu.CompilerParams(vmem_limit_bytes=24 * 2**20),
        cost_estimate=pl.CostEstimate(
            flops=2 * length * width * HDIM, bytes_accessed=8 * length * width, transcendentals=0
        ),
        name="cross_reads",
    )(*crosses, base, solved)


def output_kernel(tokens_ref, w_ref, *refs):
    out_ref = refs[-1]
    me = lax.axis_index("head")
    total = tokens_ref[...].astype(F32)
    for distance, part in enumerate(refs[:-1]):
        width = part.shape[1]
        first = pl.multiple_of((me ^ distance) * width, width)
        total = total + dot(part[...], w_ref[pl.ds(first, width), :])
    out_ref[...] = total.astype(BF16)


def output_rows(tokens, w_out, reads):
    whole = pl.BlockSpec(memory_space=pltpu.VMEM)
    return pl.pallas_call(
        output_kernel,
        in_specs=[whole] * (2 + len(reads)),
        out_specs=whole,
        out_shape=jax.ShapeDtypeStruct(tokens.shape, BF16),
        compiler_params=pltpu.CompilerParams(vmem_limit_bytes=24 * 2**20),
        cost_estimate=pl.CostEstimate(
            flops=2 * tokens.shape[0] * w_out.shape[0] * w_out.shape[1],
            bytes_accessed=2 * w_out.size + 6 * tokens.size,
            transcendentals=0,
        ),
        name="output_rows",
    )(tokens, w_out, *reads)


def shards(
    tokens,
    norm_gain,
    w_qkv,
    w_gates,
    conv_weight,
    conv_state,
    decay_rate,
    ridge,
    w_out,
    cache_keys,
    cache_values,
    page_table,
    cache_lengths,
    group_prompt,
    prompt_state,
):
    head_count = lax.axis_size("head")
    owners = lax.axis_size("grp")
    bits = [head_count >> i for i in range(1, head_count.bit_length())]
    blocks = {0: tokens}
    for bit in bits:
        blocks[bit] = swap(tokens, "head", bit)

    pool, page, heads, _ = cache_keys.shape
    starts = jnp.arange(page_table.shape[1], dtype=jnp.int32) * PAGE
    live = jnp.clip(cache_lengths[:, None] - starts, 0, PAGE)
    table = page_table | (live << 16) | (group_prompt[:, None] << 24)
    keys = cache_keys.reshape(pool, page * heads, HDIM)
    values = cache_values.reshape(pool, page * heads, HDIM)

    def scattered(parts):
        return [parts[0]] + [swap(parts[i], "grp", 2 * i) for i in range(1, owners // 2)]

    send_gram, send_cross, keep_gram, keep_cross = page_sums(
        table, keys, values, prompt_state, owners
    )
    got_gram = swap(send_gram, "grp", 1)
    for bit in bits[1:]:
        for distance in list(blocks):
            if distance and not distance & bit and distance ^ bit not in blocks:
                blocks[distance] = hold(blocks[distance], keep_gram)
                blocks[distance ^ bit] = swap(blocks[distance], "head", bit)
    blocks = [blocks[i] for i in range(head_count)]
    send_cross, *vectors = token_vectors(
        decay_rate, blocks, norm_gain, w_qkv, w_gates, conv_weight, conv_state, send_cross
    )
    grams = halve_sums(keep_gram, got_gram)
    crosses = halve_sums(keep_cross, swap(send_cross, "grp", 1))
    base, solved = ridge_reads(ridge, scattered(grams), vectors, [crosses[0]])
    reads = cross_reads(scattered(crosses), base, solved, head_count)
    reads = [reads[0]] + [swap(reads[i], "head", i) for i in range(1, head_count)]
    return output_rows(tokens, w_out, reads)


def solution(mesh):
    placed = (
        P(("grp", "head"), None),
        P(),
        P(),
        P(),
        P(),
        P("grp", None, None),
        P(),
        P("head"),
        P(),
        P("grp", None, "head", None),
        P("grp", None, "head", None),
        P(),
        P(),
        P(),
        P("grp", "head", None, None, None),
    )
    return jax.shard_map(
        shards, mesh=mesh, in_specs=placed, out_specs=P(("grp", "head"), None), check_vma=False
    )
```

```python
import functools

import jax
import jax.numpy as jnp
from jax import lax
from jax.experimental import pallas as pl
from jax.experimental.pallas import tpu as pltpu
from jax.sharding import PartitionSpec as P

HEADS = 8
HDIM = 128
CONV = 4
CG_STEPS = 8
PAGE = 128
CHUNK = 128
PAIR = 2 * CHUNK
EPS_NORM = 1e-06
PAGE_VMEM = 53
TOKEN_VMEM = 48
F32 = jnp.float32
BF16 = jnp.bfloat16


def swap(block, axis, distance):
    size = lax.axis_size(axis)
    return lax.ppermute(block, axis, [(i, i ^ distance) for i in range(size)])


def hold(block, other):
    anywhere = pl.BlockSpec(memory_space=pl.ANY)
    return pl.pallas_call(
        lambda *refs: None,
        in_specs=[anywhere, anywhere],
        out_specs=anywhere,
        out_shape=jax.ShapeDtypeStruct(block.shape, block.dtype),
        input_output_aliases={0: 0},
        compiler_params=pltpu.CompilerParams(vmem_limit_bytes=2**20),
        name="hold",
    )(block, other)


def dot(a, b):
    return jnp.dot(a, b, preferred_element_type=F32)


def silu(a):
    return a * jax.nn.sigmoid(a)


def unit_rows(a):
    return a * lax.rsqrt(jnp.sum(a * a, axis=-1, keepdims=True) + EPS_NORM)


def block_diag(a):
    zero = jnp.zeros((a.shape[0], CHUNK), a.dtype)
    return jnp.concatenate(
        [
            jnp.concatenate([a[:, :CHUNK], zero], axis=1),
            jnp.concatenate([zero, a[:, CHUNK:]], axis=1),
        ],
        axis=0,
    )


def sums_kernel(heads, owners, table_hbm, keys_hbm, values_hbm, prompt_hbm, tokens_hbm,
                send_gram, send_cross, keep_gram, keep_cross, tokens_ref,
                acc_ref, keys_ref, values_ref, stored_ref, table_ref, list_ref,
                key_sem, value_sem, small_sem):
    pool, rows = keys_hbm.shape[0], keys_hbm.shape[1]
    slots = table_hbm.shape[1]
    mine = lax.axis_index("grp")
    load_table = pltpu.make_async_copy(table_hbm, table_ref, small_sem.at[0])
    load_prompt = pltpu.make_async_copy(prompt_hbm, stored_ref, small_sem.at[1])
    load_tokens = pltpu.make_async_copy(tokens_hbm, tokens_ref, small_sem.at[2])
    load_table.start()
    load_prompt.start()
    load_tokens.start()
    acc_ref[...] = jnp.zeros_like(acc_ref)
    load_table.wait()

    def load(item):
        page = list_ref[item] & 0xFFFF
        return (
            pltpu.make_async_copy(keys_hbm.at[page], keys_ref.at[item], key_sem.at[item]),
            pltpu.make_async_copy(values_hbm.at[page], values_ref.at[item], value_sem.at[item]),
        )

    def start(item, carry):
        for copy in load(item):
            copy.start()
        return carry

    first = mine * pool
    wide = 8
    count = jnp.int32(0)
    for owner in range(owners):

        def note(chunk, count):
            for i in range(wide):
                entry = table_ref[owner, chunk * wide + i]
                page = (entry & 0xFFFF) - first
                live = entry & 0xFF0000
                list_ref[count] = (owner << 24) | live | (page & 0xFFFF)
                inside = (page >= 0) & (page < pool) & (live > 0)
                count = count + inside.astype(jnp.int32)
            return count

        chunks = jnp.int32(0)
        for slot in range(0, slots, wide):
            chunks = chunks + ((table_ref[owner, slot] & 0xFF0000) > 0).astype(jnp.int32)
        before = count
        count = lax.fori_loop(0, chunks, note, before)
        lax.fori_loop(before, count, start, 0)

    turn = 4
    turns = (count + (turn - 1)) >> 2

    def fill(item, carry):
        list_ref[item] = jnp.int32(owners << 24)
        return start(item, carry)

    lax.fori_loop(count, turns * turn, fill, 0)

    lane = lax.broadcasted_iota(jnp.int32, (HDIM, rows), 1)

    def one_turn(step, carry):
        for i in range(turn):
            for copy in load(step * turn + i):
                copy.wait()
        for i in range(turn):
            item = step * turn + i
            code = list_ref[item]
            owner, live = code >> 24, (code >> 16) & 0xFF
            keys = keys_ref[item]
            turned = keys.T
            zero = jnp.zeros_like(turned)
            left = jnp.concatenate(
                [
                    jnp.where((lane % heads == head) & (lane < live * heads), turned, zero)
                    for head in range(heads)
                ],
                axis=0,
            )
            acc_ref[owner] += dot(left, jnp.concatenate([keys, values_ref[item]], axis=1))
        return carry

    lax.fori_loop(0, turns, one_turn, 0)
    load_tokens.wait()
    load_prompt.wait()
    stored = stored_ref.shape[0]

    def add_prompt(owner, carry):
        for slot in range(stored):

            @pl.when((table_ref[owner, 0] >> 24) == mine * stored + slot)
            def _():
                for head in range(heads):
                    at = slice(head * HDIM, (head + 1) * HDIM)
                    acc_ref[owner, at, :HDIM] += stored_ref[slot, head, 0]
                    acc_ref[owner, at, HDIM:] += stored_ref[slot, head, 1].T

        return carry

    lax.fori_loop(0, owners, add_prompt, 0)
    bit = mine & 1
    for pair in range(owners // 2):
        there, here = 2 * pair + 1 - bit, 2 * pair + bit
        send_gram[pair] = acc_ref[there, :, :HDIM].astype(BF16)
        send_cross[pair] = acc_ref[there, :, HDIM:].astype(BF16)
        keep_gram[pair] = acc_ref[here, :, :HDIM].astype(BF16)
        keep_cross[pair] = acc_ref[here, :, HDIM:].astype(BF16)


def page_sums(table, keys, values, prompt_state, tokens, owners):
    pool, rows, _ = keys.shape
    heads = prompt_state.shape[1]
    half = (owners // 2, heads * HDIM, HDIM)
    items = pool + 4
    return pl.pallas_call(
        functools.partial(sums_kernel, heads, owners),
        in_specs=[pl.BlockSpec(memory_space=pl.ANY)] * 5,
        out_specs=[pl.BlockSpec(memory_space=pltpu.VMEM)] * 5,
        scratch_shapes=[
            pltpu.VMEM((owners + 1, heads * HDIM, 2 * HDIM), F32),
            pltpu.VMEM((items, rows, HDIM), BF16),
            pltpu.VMEM((items, rows, HDIM), BF16),
            pltpu.VMEM(prompt_state.shape, F32),
            pltpu.SMEM(table.shape, jnp.int32),
            pltpu.SMEM((items,), jnp.int32),
            pltpu.SemaphoreType.DMA((items,)),
            pltpu.SemaphoreType.DMA((items,)),
            pltpu.SemaphoreType.DMA((3,)),
        ],
        out_shape=[jax.ShapeDtypeStruct(half, BF16)] * 4
        + [jax.ShapeDtypeStruct(tokens.shape, BF16)],
        compiler_params=pltpu.CompilerParams(vmem_limit_bytes=PAGE_VMEM * 2**20),
        cost_estimate=pl.CostEstimate(
            flops=8 * pool * rows * heads * HDIM * HDIM,
            bytes_accessed=4 * pool * rows * HDIM,
            transcendentals=0,
        ),
        name="page_sums",
    )(table, keys, values, prompt_state, tokens)


def halve_kernel(keep_ref, got_ref, *refs):
    for distance, out_ref in enumerate(refs[-keep_ref.shape[0] :]):
        row = (lax.axis_index("grp") >> 1) ^ distance
        total = keep_ref[row].astype(F32) + got_ref[row].astype(F32)
        out_ref[...] = total.astype(out_ref.dtype)


def halve_sums(keep, got, after=()):
    count, rows, cols = keep.shape
    outs = [jax.ShapeDtypeStruct((rows, cols), F32 if i == 0 else BF16) for i in range(count)]
    whole = pl.BlockSpec(memory_space=pltpu.VMEM)
    return pl.pallas_call(
        halve_kernel,
        in_specs=[whole] * (2 + len(after)),
        out_specs=[whole] * count,
        out_shape=outs,
        compiler_params=pltpu.CompilerParams(vmem_limit_bytes=32 * 2**20),
        cost_estimate=pl.CostEstimate(
            flops=count * rows * cols, bytes_accessed=6 * count * rows * cols, transcendentals=0
        ),
        name="halve_sums",
    )(keep, got, *after)


def token_kernel(heads, *refs):
    head_count = HEADS // heads
    blocks = refs[:head_count]
    (gain_ref, w_hbm, wg_ref, taps_all, state_ref, rate_ref) = refs[head_count : head_count + 6]
    (q_ref, k_ref, kt_ref, vt_ref, weight_ref, prefix_ref, rows_ref) = refs[-12:-5]
    ext_ref, gate_ref, normed_ref, w_ref, w_sem = refs[-5:]
    me = lax.axis_index("head")
    tok_rows = blocks[0].shape[0]
    width = w_ref.shape[1]
    columns = pl.ds(pl.multiple_of(me * width, HDIM), width)
    load = pltpu.make_async_copy(w_hbm.at[:, columns], w_ref, w_sem)
    load.start()
    length = tok_rows * head_count
    chunks = length // CHUNK
    base = 8
    taps_ref = taps_all[:, columns]
    ext_ref[base - (CONV - 1) : base, :] = state_ref[0, :, columns].astype(F32)
    gate_ref[...] = jnp.zeros_like(gate_ref)
    for distance, block in enumerate(blocks):
        first = pl.multiple_of((me ^ distance) * tok_rows, tok_rows)
        wide = block[...].astype(F32)
        scale = lax.rsqrt(jnp.mean(wide * wide, axis=-1, keepdims=True) + EPS_NORM)
        normed = (wide * scale * gain_ref[...]).astype(BF16)
        normed_ref[pl.ds(first, tok_rows), :] = normed
        gate_ref[pl.ds(first, tok_rows), : 2 * HEADS] = dot(normed, wg_ref[...])
    load.wait()
    for c in range(chunks):
        rows = slice(c * CHUNK, (c + 1) * CHUNK)
        mixed = dot(normed_ref[rows, :], w_ref[...]).astype(BF16)
        ext_ref[base + c * CHUNK : base + (c + 1) * CHUNK, :] = mixed.astype(F32)

    shift = lax.rem(HDIM - 2 * heads * me, HDIM)
    logits = pltpu.roll(gate_ref[...], shift, 1)
    lane = lax.broadcasted_iota(jnp.int32, (1, HDIM), 1)
    rate = jnp.zeros((1, HDIM), F32)
    for head in range(heads):
        here = lax.broadcasted_iota(jnp.int32, (1, HEADS), 1) == me * heads + head
        own = jnp.sum(jnp.where(here, rate_ref[...], 0.0), axis=1, keepdims=True)
        rate = jnp.where(lane == 2 * head + 1, own, rate)
    write = jax.nn.sigmoid(logits).astype(BF16).astype(F32)
    soft = jnp.maximum(logits, 0.0) + jnp.log1p(jnp.exp(-jnp.abs(logits)))
    decay = (-rate * soft).astype(BF16)
    here = lax.broadcasted_iota(jnp.int32, (CHUNK, CHUNK), 0)
    there = lax.broadcasted_iota(jnp.int32, (CHUNK, CHUNK), 1)
    lower = (here >= there).astype(F32).astype(BF16)
    cumul = [dot(lower, decay[c * CHUNK : (c + 1) * CHUNK]) for c in range(chunks)]
    turned = [block.T for block in cumul]

    for head in range(heads):
        parts = []
        for part in range(3):
            cols = slice((3 * head + part) * HDIM, (3 * head + part + 1) * HDIM)
            total = taps_ref[CONV - 1 : CONV, cols] * ext_ref[base : base + length, cols]
            for lag in range(1, CONV):
                total = total + taps_ref[CONV - 1 - lag : CONV - lag, cols] * (
                    ext_ref[base - lag : base - lag + length, cols]
                )
            parts.append(total)
        query = unit_rows(silu(parts[0])).astype(BF16)
        key = unit_rows(silu(parts[1])).astype(BF16)
        value = parts[2].astype(BF16)
        q_ref[head] = query.T
        k_ref[head] = key
        kt_ref[head] = key.T
        vt_ref[head] = value.T
        prefix = jnp.zeros((HDIM, 2 * HDIM), F32)
        so_far = jnp.zeros((1, 1), F32)
        for c in range(chunks):
            rows = slice(c * CHUNK, (c + 1) * CHUNK)
            col = cumul[c][:, 2 * head + 1 : 2 * head + 2]
            row = turned[c][2 * head + 1 : 2 * head + 2, :]
            gate = write[rows, 2 * head : 2 * head + 1]
            spread = jnp.exp(jnp.minimum(row - col, 0.0)) * gate
            half = slice((c % 2) * CHUNK, (c % 2 + 1) * CHUNK)
            weight_ref[head, c // 2, :, half] = jnp.where(here <= there, spread, 0.0)
            rows_ref[head, c // 2, 0:1, half] = jnp.exp(row)
            rows_ref[head, c // 2, 1:2, half] = jnp.broadcast_to(jnp.exp(so_far), (1, CHUNK))
            prefix_ref[head, c, :HDIM] = prefix[:, :HDIM]
            prefix_ref[head, c, HDIM:] = prefix[:, HDIM:].T
            if c + 1 < chunks:
                whole = cumul[c][CHUNK - 1 :, 2 * head + 1 : 2 * head + 2]
                carry = jnp.exp(whole - col) * gate
                both = jnp.concatenate([key[rows], value[rows]], axis=1).astype(F32)
                prefix = prefix * jnp.exp(whole) + dot(
                    kt_ref[head, :, rows], (both * carry).astype(BF16)
                )
                so_far = so_far + whole


def token_vectors(
    decay_rate, blocks, norm_gain, w_qkv, w_gates, conv_weight, conv_state, after
):
    head_count = len(blocks)
    heads = HEADS // head_count
    width = heads * 3 * HDIM
    tok_rows, model = blocks[0].shape
    length = head_count * tok_rows
    chunks = length // CHUNK
    whole = pl.BlockSpec(memory_space=pltpu.VMEM)
    anywhere = pl.BlockSpec(memory_space=pl.ANY)
    outs = [
        jax.ShapeDtypeStruct((heads, HDIM, length), BF16),
        jax.ShapeDtypeStruct((heads, length, HDIM), BF16),
        jax.ShapeDtypeStruct((heads, HDIM, length), BF16),
        jax.ShapeDtypeStruct((heads, HDIM, length), BF16),
        jax.ShapeDtypeStruct((heads, chunks // 2, CHUNK, PAIR), F32),
        jax.ShapeDtypeStruct((heads, chunks, 2 * HDIM, HDIM), F32),
        jax.ShapeDtypeStruct((heads, chunks // 2, 8, PAIR), F32),
    ]
    return pl.pallas_call(
        functools.partial(token_kernel, heads),
        in_specs=[whole] * head_count + [whole, anywhere] + [whole] * 5,
        out_specs=[whole] * len(outs),
        scratch_shapes=[
            pltpu.VMEM((8 + length, width), F32),
            pltpu.VMEM((length, HDIM), F32),
            pltpu.VMEM((length, model), BF16),
            pltpu.VMEM((model, width), BF16),
            pltpu.SemaphoreType.DMA,
        ],
        out_shape=outs,
        compiler_params=pltpu.CompilerParams(vmem_limit_bytes=TOKEN_VMEM * 2**20),
        cost_estimate=pl.CostEstimate(
            flops=2 * length * model * width,
            bytes_accessed=2 * model * (length + width) + 4 * 2**20,
            transcendentals=length * width,
        ),
        name="token_vectors",
    )(
        *blocks,
        norm_gain.reshape(1, model),
        w_qkv,
        w_gates,
        conv_weight,
        conv_state,
        decay_rate.reshape(1, HEADS),
        after,
    )


def read_kernel(heads, terms, ridge_ref, *refs):
    grams = refs[:terms]
    (q_ref, k_ref, kt_ref, vt_ref, weight_ref, prefix_ref, rows_ref) = refs[terms : terms + 7]
    base_ref, solved_ref, left_ref, x_ref, r_ref, d_ref = refs[-6:]
    pairs = q_ref.shape[2] // PAIR
    groups = [(head, pair) for head in range(heads) for pair in range(pairs)]
    norms = []
    for head in range(heads):
        rows = slice(head * HDIM, (head + 1) * HDIM)
        gram = grams[0][rows, :].astype(F32)
        for term in grams[1:]:
            gram = gram + term[rows, :].astype(F32)
        for pair in range(pairs):
            for side in range(2):
                c = 2 * pair + side
                half = slice(side * CHUNK, (side + 1) * CHUNK)
                scale = rows_ref[head, pair, 1:2, half]
                left_ref[head, pair, :HDIM, half] = (
                    gram * scale + prefix_ref[head, c, :HDIM]
                ).astype(BF16)
                left_ref[head, pair, HDIM:, half] = k_ref[head, c * CHUNK : (c + 1) * CHUNK]
            query = q_ref[head, :, pair * PAIR : (pair + 1) * PAIR].astype(F32)
            x_ref[head, pair] = jnp.zeros_like(query)
            r_ref[head, pair] = query
            d_ref[head, pair] = query
            norms.append(jnp.sum(query * query, axis=0, keepdims=True))

    def one_step(_, norms):
        firsts = [dot(left_ref[g], block_diag(d_ref[g].astype(BF16))) for g in groups]
        seconds = []
        for (head, pair), first in zip(groups, firsts):
            scores = (first[HDIM:] * weight_ref[head, pair]).astype(BF16)
            seconds.append(
                dot(kt_ref[head, :, pair * PAIR : (pair + 1) * PAIR], block_diag(scores))
            )
        later = []
        for (head, pair), first, second, norm in zip(groups, firsts, seconds, norms):
            direction = d_ref[head, pair]
            image = (
                rows_ref[head, pair, 0:1] * first[:HDIM] + ridge_ref[:, head : head + 1] * direction + second
            )
            alpha = norm / jnp.sum(direction * image, axis=0, keepdims=True)
            x_ref[head, pair] += alpha * direction
            residue = r_ref[head, pair] - alpha * image
            r_ref[head, pair] = residue
            norm_next = jnp.sum(residue * residue, axis=0, keepdims=True)
            d_ref[head, pair] = residue + norm_next / norm * direction
            later.append(norm_next)
        return tuple(later)

    lax.fori_loop(0, CG_STEPS, one_step, tuple(norms), unroll=2)
    for head, pair in groups:
        cols = slice(head * HDIM, (head + 1) * HDIM)
        span = slice(pair * PAIR, (pair + 1) * PAIR)
        for side in range(2):
            half = slice(side * CHUNK, (side + 1) * CHUNK)
            left_ref[head, pair, :HDIM, half] = prefix_ref[head, 2 * pair + side, HDIM:].astype(BF16)
        solved = x_ref[head, pair]
        first = dot(left_ref[head, pair], block_diag(solved.astype(BF16)))
        scores = (first[HDIM:] * weight_ref[head, pair]).astype(BF16)
        carry = rows_ref[head, pair, 0:1]
        read = carry * first[:HDIM] + dot(vt_ref[head, :, span], block_diag(scores))
        base_ref[span, cols] = read.T
        solved_ref[span, cols] = (solved * (carry * rows_ref[head, pair, 1:2])).T.astype(BF16)


def ridge_reads(ridge, grams, vectors, after=()):
    heads, _, length = vectors[0].shape
    pairs = length // PAIR
    whole = pl.BlockSpec(memory_space=pltpu.VMEM)
    state = pltpu.VMEM((heads, pairs, HDIM, PAIR), F32)
    return pl.pallas_call(
        functools.partial(read_kernel, heads, len(grams)),
        in_specs=[whole] * (1 + len(grams) + len(vectors))
        + [whole] * len(after),
        out_specs=[whole] * 2,
        out_shape=[
            jax.ShapeDtypeStruct((length, heads * HDIM), F32),
            jax.ShapeDtypeStruct((length, heads * HDIM), BF16),
        ],
        scratch_shapes=[pltpu.VMEM((heads, pairs, 2 * HDIM, PAIR), BF16), state, state, state],
        compiler_params=pltpu.CompilerParams(vmem_limit_bytes=32 * 2**20),
        cost_estimate=pl.CostEstimate(
            flops=CG_STEPS * heads * pairs * 6 * CHUNK**3 * 16,
            bytes_accessed=8 * 2**20,
            transcendentals=0,
        ),
        name="ridge_reads",
    )(ridge.reshape(1, heads), *grams, *vectors, *after)


def cross_kernel(heads, terms, *refs):
    crosses, (base_ref, solved_ref) = refs[:terms], refs[terms : terms + 2]
    outs, o_ref = refs[terms + 2 : -1], refs[-1]
    me = lax.axis_index("head")
    for head in range(heads):
        cols = slice(head * HDIM, (head + 1) * HDIM)
        cross = crosses[0][cols, :].astype(F32)
        for term in crosses[1:]:
            cross = cross + term[cols, :].astype(F32)
        read = base_ref[:, cols] + dot(solved_ref[:, cols], cross.astype(BF16))
        o_ref[:, cols] = read.astype(BF16)
    tok_rows = outs[0].shape[0]
    for distance, out_ref in enumerate(outs):
        first_row = pl.multiple_of((me ^ distance) * tok_rows, tok_rows)
        out_ref[...] = o_ref[pl.ds(first_row, tok_rows), :]


def cross_reads(crosses, base, solved, head_count):
    length, width = base.shape
    whole = pl.BlockSpec(memory_space=pltpu.VMEM)
    return pl.pallas_call(
        functools.partial(cross_kernel, width // HDIM, len(crosses)),
        in_specs=[whole] * (len(crosses) + 2),
        out_specs=[whole] * head_count,
        out_shape=[jax.ShapeDtypeStruct((length // head_count, width), BF16)] * head_count,
        scratch_shapes=[pltpu.VMEM((length, width), BF16)],
        compiler_params=pltpu.CompilerParams(vmem_limit_bytes=24 * 2**20),
        cost_estimate=pl.CostEstimate(
            flops=2 * length * width * HDIM, bytes_accessed=8 * length * width, transcendentals=0
        ),
        name="cross_reads",
    )(*crosses, base, solved)


def output_kernel(tokens_ref, w_ref, *refs):
    out_ref = refs[-1]
    me = lax.axis_index("head")
    total = tokens_ref[...].astype(F32)
    for distance, part in enumerate(refs[:-1]):
        width = part.shape[1]
        first = pl.multiple_of((me ^ distance) * width, width)
        total = total + dot(part[...], w_ref[pl.ds(first, width), :])
    out_ref[...] = total.astype(BF16)


def output_rows(tokens, w_out, reads):
    whole = pl.BlockSpec(memory_space=pltpu.VMEM)
    return pl.pallas_call(
        output_kernel,
        in_specs=[whole] * (2 + len(reads)),
        out_specs=whole,
        out_shape=jax.ShapeDtypeStruct(tokens.shape, BF16),
        compiler_params=pltpu.CompilerParams(vmem_limit_bytes=24 * 2**20),
        cost_estimate=pl.CostEstimate(
            flops=2 * tokens.shape[0] * w_out.shape[0] * w_out.shape[1],
            bytes_accessed=2 * w_out.size + 6 * tokens.size,
            transcendentals=0,
        ),
        name="output_rows",
    )(tokens, w_out, *reads)


def shards(
    tokens,
    norm_gain,
    w_qkv,
    w_gates,
    conv_weight,
    conv_state,
    decay_rate,
    ridge,
    w_out,
    cache_keys,
    cache_values,
    page_table,
    cache_lengths,
    group_prompt,
    prompt_state,
):
    head_count = lax.axis_size("head")
    owners = lax.axis_size("grp")
    pool, page, heads, _ = cache_keys.shape
    starts = jnp.arange(page_table.shape[1], dtype=jnp.int32) * PAGE
    live = jnp.clip(cache_lengths[:, None] - starts, 0, PAGE)
    table = page_table | (live << 16) | (group_prompt[:, None] << 24)
    keys = cache_keys.reshape(pool, page * heads, HDIM)
    values = cache_values.reshape(pool, page * heads, HDIM)

    def scattered(parts):
        return [parts[0]] + [swap(parts[i], "grp", 2 * i) for i in range(1, owners // 2)]

    send_gram, send_cross, keep_gram, keep_cross, handed = page_sums(
        table, keys, values, prompt_state, tokens, owners
    )
    got_gram = swap(send_gram, "grp", 1)

    blocks = {0: handed}
    bit = head_count // 2
    while bit:
        for distance in list(blocks):
            blocks[distance ^ bit] = swap(blocks[distance], "head", bit)
        bit //= 2
    blocks = [blocks[i] for i in range(head_count)]

    grams = halve_sums(keep_gram, got_gram)
    got_cross = swap(hold(send_cross, grams[0]), "grp", 1)
    vectors = token_vectors(
        decay_rate, blocks, norm_gain, w_qkv, w_gates, conv_weight, conv_state, grams[0]
    )
    crosses = halve_sums(keep_cross, got_cross, vectors[-1:])
    base, solved = ridge_reads(ridge, scattered(grams), vectors, [crosses[0]])
    reads = cross_reads(scattered(crosses), base, solved, head_count)
    reads = [reads[0]] + [swap(reads[i], "head", i) for i in range(1, head_count)]
    return output_rows(handed, w_out, reads)


def solution(mesh):
    placed = (
        P(("grp", "head"), None),
        P(),
        P(),
        P(),
        P(),
        P("grp", None, None),
        P(),
        P("head"),
        P(),
        P("grp", None, "head", None),
        P("grp", None, "head", None),
        P(),
        P(),
        P(),
        P("grp", "head", None, None, None),
    )
    return jax.shard_map(
        shards, mesh=mesh, in_specs=placed, out_specs=P(("grp", "head"), None), check_vma=False
    )
```

```python
import functools

import jax
import jax.numpy as jnp
from jax import lax
from jax.experimental import pallas as pl
from jax.experimental.pallas import tpu as pltpu
from jax.sharding import PartitionSpec as P

HEADS = 8
HDIM = 128
CONV = 4
CG_STEPS = 8
PAGE = 128
CHUNK = 128
PAIR = 2 * CHUNK
EPS_NORM = 1e-06
PAGE_VMEM = 53
TOKEN_VMEM = 48
F32 = jnp.float32
BF16 = jnp.bfloat16


def swap(block, axis, distance):
    size = lax.axis_size(axis)
    return lax.ppermute(block, axis, [(i, i ^ distance) for i in range(size)])


def hold(block, other):
    anywhere = pl.BlockSpec(memory_space=pl.ANY)
    return pl.pallas_call(
        lambda *refs: None,
        in_specs=[anywhere, anywhere],
        out_specs=anywhere,
        out_shape=jax.ShapeDtypeStruct(block.shape, block.dtype),
        input_output_aliases={0: 0},
        compiler_params=pltpu.CompilerParams(vmem_limit_bytes=2**20),
        name="hold",
    )(block, other)


def dot(a, b):
    return jnp.dot(a, b, preferred_element_type=F32)


def silu(a):
    return a * jax.nn.sigmoid(a)


def unit_rows(a):
    return a * lax.rsqrt(jnp.sum(a * a, axis=-1, keepdims=True) + EPS_NORM)


def block_diag(a):
    zero = jnp.zeros((a.shape[0], CHUNK), a.dtype)
    return jnp.concatenate(
        [
            jnp.concatenate([a[:, :CHUNK], zero], axis=1),
            jnp.concatenate([zero, a[:, CHUNK:]], axis=1),
        ],
        axis=0,
    )


def sums_kernel(heads, owners, code_hbm, keys_hbm, values_hbm, prompt_hbm,
                send_gram, send_cross, keep_gram, keep_cross,
                acc_ref, keys_ref, values_ref, stored_ref, code_ref, pick_ref, list_ref,
                key_sem, value_sem, small_sem):
    pool, rows = keys_hbm.shape[0], keys_hbm.shape[1]
    mine = lax.axis_index("grp")
    load_code = pltpu.make_async_copy(code_hbm, code_ref, small_sem.at[0])
    load_prompt = pltpu.make_async_copy(prompt_hbm, stored_ref, small_sem.at[1])
    load_code.start()
    load_prompt.start()
    acc_ref[...] = jnp.zeros_like(acc_ref)
    load_code.wait()

    def load(item):
        page = list_ref[item] & 0xFFFF
        return (
            pltpu.make_async_copy(keys_hbm.at[page], keys_ref.at[item], key_sem.at[item]),
            pltpu.make_async_copy(values_hbm.at[page], values_ref.at[item], value_sem.at[item]),
        )

    def start(item, carry):
        for copy in load(item):
            copy.start()
        return carry

    wide = 8

    def note(chunk, count):
        for i in range(wide):
            page = chunk * wide + i
            code = code_ref[page]
            pick_ref[code >> 24] = code & 0xFFFF
            list_ref[count] = (code & -65536) | page
            count = count + ((code & 0xFF0000) > 0).astype(jnp.int32)
        return count

    count = lax.fori_loop(0, pool // wide, note, jnp.int32(0))
    lax.fori_loop(0, count, start, 0)

    turn = 4
    turns = (count + (turn - 1)) >> 2

    def fill(item, carry):
        list_ref[item] = jnp.int32(owners << 24)
        return start(item, carry)

    lax.fori_loop(count, turns * turn, fill, 0)

    lane = lax.broadcasted_iota(jnp.int32, (HDIM, rows), 1)

    def one_turn(step, carry):
        for i in range(turn):
            for copy in load(step * turn + i):
                copy.wait()
        for i in range(turn):
            item = step * turn + i
            code = list_ref[item]
            owner, live = code >> 24, (code >> 16) & 0xFF
            keys = keys_ref[item]
            turned = keys.T
            zero = jnp.zeros_like(turned)
            left = jnp.concatenate(
                [
                    jnp.where((lane % heads == head) & (lane < live * heads), turned, zero)
                    for head in range(heads)
                ],
                axis=0,
            )
            acc_ref[owner] += dot(left, jnp.concatenate([keys, values_ref[item]], axis=1))
        return carry

    lax.fori_loop(0, turns, one_turn, 0)
    load_prompt.wait()
    stored = stored_ref.shape[0]

    def add_prompt(owner, carry):
        for slot in range(stored):

            @pl.when(pick_ref[owner] == mine * stored + slot)
            def _():
                for head in range(heads):
                    at = slice(head * HDIM, (head + 1) * HDIM)
                    acc_ref[owner, at, :HDIM] += stored_ref[slot, head, 0]
                    acc_ref[owner, at, HDIM:] += stored_ref[slot, head, 1].T

        return carry

    lax.fori_loop(0, owners, add_prompt, 0)
    bit = mine & 1
    for pair in range(owners // 2):
        there, here = 2 * pair + 1 - bit, 2 * pair + bit
        send_gram[pair] = acc_ref[there, :, :HDIM].astype(BF16)
        send_cross[pair] = acc_ref[there, :, HDIM:].astype(BF16)
        keep_gram[pair] = acc_ref[here, :, :HDIM].astype(BF16)
        keep_cross[pair] = acc_ref[here, :, HDIM:].astype(BF16)


def page_sums(code, keys, values, prompt_state, owners):
    pool, rows, _ = keys.shape
    heads = prompt_state.shape[1]
    half = (owners // 2, heads * HDIM, HDIM)
    items = pool + 4
    return pl.pallas_call(
        functools.partial(sums_kernel, heads, owners),
        in_specs=[pl.BlockSpec(memory_space=pl.ANY)] * 4,
        out_specs=[pl.BlockSpec(memory_space=pltpu.VMEM)] * 4,
        scratch_shapes=[
            pltpu.VMEM((owners + 1, heads * HDIM, 2 * HDIM), F32),
            pltpu.VMEM((items, rows, HDIM), BF16),
            pltpu.VMEM((items, rows, HDIM), BF16),
            pltpu.VMEM(prompt_state.shape, F32),
            pltpu.SMEM(code.shape, jnp.int32),
            pltpu.SMEM((owners,), jnp.int32),
            pltpu.SMEM((items,), jnp.int32),
            pltpu.SemaphoreType.DMA((items,)),
            pltpu.SemaphoreType.DMA((items,)),
            pltpu.SemaphoreType.DMA((2,)),
        ],
        out_shape=[jax.ShapeDtypeStruct(half, BF16)] * 4,
        compiler_params=pltpu.CompilerParams(vmem_limit_bytes=PAGE_VMEM * 2**20),
        cost_estimate=pl.CostEstimate(
            flops=8 * pool * rows * heads * HDIM * HDIM,
            bytes_accessed=4 * pool * rows * HDIM,
            transcendentals=0,
        ),
        name="page_sums",
    )(code, keys, values, prompt_state)


def halve_kernel(keep_ref, got_ref, *outs):
    for distance, out_ref in enumerate(outs):
        row = (lax.axis_index("grp") >> 1) ^ distance
        total = keep_ref[row].astype(F32) + got_ref[row].astype(F32)
        out_ref[...] = total.astype(out_ref.dtype)


def halve_sums(keep, got):
    count, rows, cols = keep.shape
    outs = [jax.ShapeDtypeStruct((rows, cols), F32 if i == 0 else BF16) for i in range(count)]
    whole = pl.BlockSpec(memory_space=pltpu.VMEM)
    return pl.pallas_call(
        halve_kernel,
        in_specs=[whole, whole],
        out_specs=[whole] * count,
        out_shape=outs,
        compiler_params=pltpu.CompilerParams(vmem_limit_bytes=32 * 2**20),
        cost_estimate=pl.CostEstimate(
            flops=count * rows * cols, bytes_accessed=6 * count * rows * cols, transcendentals=0
        ),
        name="halve_sums",
    )(keep, got)


def token_kernel(heads, *refs):
    head_count = HEADS // heads
    blocks = refs[:head_count]
    (gain_ref, w_hbm, wg_ref, taps_all, state_ref, rate_ref) = refs[head_count : head_count + 6]
    (q_ref, k_ref, kt_ref, vt_ref, weight_ref, prefix_ref, rows_ref) = refs[-12:-5]
    ext_ref, gate_ref, normed_ref, w_ref, w_sem = refs[-5:]
    me = lax.axis_index("head")
    tok_rows = blocks[0].shape[0]
    width = w_ref.shape[1]
    columns = pl.ds(pl.multiple_of(me * width, HDIM), width)
    load = pltpu.make_async_copy(w_hbm.at[:, columns], w_ref, w_sem)
    load.start()
    length = tok_rows * head_count
    chunks = length // CHUNK
    base = 8
    taps_ref = taps_all[:, columns]
    ext_ref[base - (CONV - 1) : base, :] = state_ref[0, :, columns].astype(F32)
    gate_ref[...] = jnp.zeros_like(gate_ref)
    for distance, block in enumerate(blocks):
        first = pl.multiple_of((me ^ distance) * tok_rows, tok_rows)
        wide = block[...].astype(F32)
        scale = lax.rsqrt(jnp.mean(wide * wide, axis=-1, keepdims=True) + EPS_NORM)
        normed = (wide * scale * gain_ref[...]).astype(BF16)
        normed_ref[pl.ds(first, tok_rows), :] = normed
        gate_ref[pl.ds(first, tok_rows), : 2 * HEADS] = dot(normed, wg_ref[...])
    load.wait()
    for c in range(chunks):
        rows = slice(c * CHUNK, (c + 1) * CHUNK)
        mixed = dot(normed_ref[rows, :], w_ref[...]).astype(BF16)
        ext_ref[base + c * CHUNK : base + (c + 1) * CHUNK, :] = mixed.astype(F32)

    shift = lax.rem(HDIM - 2 * heads * me, HDIM)
    logits = pltpu.roll(gate_ref[...], shift, 1)
    lane = lax.broadcasted_iota(jnp.int32, (1, HDIM), 1)
    rate = jnp.zeros((1, HDIM), F32)
    for head in range(heads):
        here = lax.broadcasted_iota(jnp.int32, (1, HEADS), 1) == me * heads + head
        own = jnp.sum(jnp.where(here, rate_ref[...], 0.0), axis=1, keepdims=True)
        rate = jnp.where(lane == 2 * head + 1, own, rate)
    write = jax.nn.sigmoid(logits).astype(BF16).astype(F32)
    soft = jnp.maximum(logits, 0.0) + jnp.log1p(jnp.exp(-jnp.abs(logits)))
    decay = (-rate * soft).astype(BF16)
    here = lax.broadcasted_iota(jnp.int32, (CHUNK, CHUNK), 0)
    there = lax.broadcasted_iota(jnp.int32, (CHUNK, CHUNK), 1)
    lower = (here >= there).astype(F32).astype(BF16)
    cumul = [dot(lower, decay[c * CHUNK : (c + 1) * CHUNK]) for c in range(chunks)]
    turned = [block.T for block in cumul]

    for head in range(heads):
        parts = []
        for part in range(3):
            cols = slice((3 * head + part) * HDIM, (3 * head + part + 1) * HDIM)
            total = taps_ref[CONV - 1 : CONV, cols] * ext_ref[base : base + length, cols]
            for lag in range(1, CONV):
                total = total + taps_ref[CONV - 1 - lag : CONV - lag, cols] * (
                    ext_ref[base - lag : base - lag + length, cols]
                )
            parts.append(total)
        query = unit_rows(silu(parts[0])).astype(BF16)
        key = unit_rows(silu(parts[1])).astype(BF16)
        value = parts[2].astype(BF16)
        q_ref[head] = query.T
        k_ref[head] = key
        kt_ref[head] = key.T
        vt_ref[head] = value.T
        prefix = jnp.zeros((HDIM, 2 * HDIM), F32)
        so_far = jnp.zeros((1, 1), F32)
        for c in range(chunks):
            rows = slice(c * CHUNK, (c + 1) * CHUNK)
            col = cumul[c][:, 2 * head + 1 : 2 * head + 2]
            row = turned[c][2 * head + 1 : 2 * head + 2, :]
            gate = write[rows, 2 * head : 2 * head + 1]
            spread = jnp.exp(jnp.minimum(row - col, 0.0)) * gate
            half = slice((c % 2) * CHUNK, (c % 2 + 1) * CHUNK)
            weight_ref[head, c // 2, :, half] = jnp.where(here <= there, spread, 0.0)
            rows_ref[head, c // 2, 0:1, half] = jnp.exp(row)
            rows_ref[head, c // 2, 1:2, half] = jnp.broadcast_to(jnp.exp(so_far), (1, CHUNK))
            prefix_ref[head, c, :HDIM] = prefix[:, :HDIM]
            prefix_ref[head, c, HDIM:] = prefix[:, HDIM:].T
            if c + 1 < chunks:
                whole = cumul[c][CHUNK - 1 :, 2 * head + 1 : 2 * head + 2]
                carry = jnp.exp(whole - col) * gate
                both = jnp.concatenate([key[rows], value[rows]], axis=1).astype(F32)
                prefix = prefix * jnp.exp(whole) + dot(
                    kt_ref[head, :, rows], (both * carry).astype(BF16)
                )
                so_far = so_far + whole


def token_vectors(
    decay_rate, blocks, norm_gain, w_qkv, w_gates, conv_weight, conv_state, held
):
    head_count = len(blocks)
    heads = HEADS // head_count
    width = heads * 3 * HDIM
    tok_rows, model = blocks[0].shape
    length = head_count * tok_rows
    chunks = length // CHUNK
    whole = pl.BlockSpec(memory_space=pltpu.VMEM)
    anywhere = pl.BlockSpec(memory_space=pl.ANY)
    outs = [
        jax.ShapeDtypeStruct((heads, HDIM, length), BF16),
        jax.ShapeDtypeStruct((heads, length, HDIM), BF16),
        jax.ShapeDtypeStruct((heads, HDIM, length), BF16),
        jax.ShapeDtypeStruct((heads, HDIM, length), BF16),
        jax.ShapeDtypeStruct((heads, chunks // 2, CHUNK, PAIR), F32),
        jax.ShapeDtypeStruct((heads, chunks, 2 * HDIM, HDIM), F32),
        jax.ShapeDtypeStruct((heads, chunks // 2, 8, PAIR), F32),
    ]
    return pl.pallas_call(
        functools.partial(token_kernel, heads),
        in_specs=[whole] * head_count + [whole, anywhere] + [whole] * 4 + [anywhere],
        out_specs=[anywhere] + [whole] * len(outs),
        scratch_shapes=[
            pltpu.VMEM((8 + length, width), F32),
            pltpu.VMEM((length, HDIM), F32),
            pltpu.VMEM((length, model), BF16),
            pltpu.VMEM((model, width), BF16),
            pltpu.SemaphoreType.DMA,
        ],
        out_shape=[jax.ShapeDtypeStruct(held.shape, held.dtype)] + outs,
        input_output_aliases={head_count + 6: 0},
        compiler_params=pltpu.CompilerParams(vmem_limit_bytes=TOKEN_VMEM * 2**20),
        cost_estimate=pl.CostEstimate(
            flops=2 * length * model * width,
            bytes_accessed=2 * model * (length + width) + 4 * 2**20,
            transcendentals=length * width,
        ),
        name="token_vectors",
    )(
        *blocks,
        norm_gain.reshape(1, model),
        w_qkv,
        w_gates,
        conv_weight,
        conv_state,
        decay_rate.reshape(1, HEADS),
        held,
    )


def read_kernel(heads, terms, ridge_ref, *refs):
    grams = refs[:terms]
    (q_ref, k_ref, kt_ref, vt_ref, weight_ref, prefix_ref, rows_ref) = refs[terms : terms + 7]
    base_ref, solved_ref, left_ref, x_ref, r_ref, d_ref = refs[-6:]
    pairs = q_ref.shape[2] // PAIR
    groups = [(head, pair) for head in range(heads) for pair in range(pairs)]
    norms = []
    for head in range(heads):
        rows = slice(head * HDIM, (head + 1) * HDIM)
        gram = grams[0][rows, :].astype(F32)
        for term in grams[1:]:
            gram = gram + term[rows, :].astype(F32)
        for pair in range(pairs):
            for side in range(2):
                c = 2 * pair + side
                half = slice(side * CHUNK, (side + 1) * CHUNK)
                scale = rows_ref[head, pair, 1:2, half]
                left_ref[head, pair, :HDIM, half] = (
                    gram * scale + prefix_ref[head, c, :HDIM]
                ).astype(BF16)
                left_ref[head, pair, HDIM:, half] = k_ref[head, c * CHUNK : (c + 1) * CHUNK]
            query = q_ref[head, :, pair * PAIR : (pair + 1) * PAIR].astype(F32)
            x_ref[head, pair] = jnp.zeros_like(query)
            r_ref[head, pair] = query
            d_ref[head, pair] = query
            norms.append(jnp.sum(query * query, axis=0, keepdims=True))

    def one_step(_, norms):
        firsts = [dot(left_ref[g], block_diag(d_ref[g].astype(BF16))) for g in groups]
        seconds = []
        for (head, pair), first in zip(groups, firsts):
            scores = (first[HDIM:] * weight_ref[head, pair]).astype(BF16)
            seconds.append(
                dot(kt_ref[head, :, pair * PAIR : (pair + 1) * PAIR], block_diag(scores))
            )
        later = []
        for (head, pair), first, second, norm in zip(groups, firsts, seconds, norms):
            direction = d_ref[head, pair]
            image = (
                rows_ref[head, pair, 0:1] * first[:HDIM] + ridge_ref[:, head : head + 1] * direction + second
            )
            alpha = norm / jnp.sum(direction * image, axis=0, keepdims=True)
            x_ref[head, pair] += alpha * direction
            residue = r_ref[head, pair] - alpha * image
            r_ref[head, pair] = residue
            norm_next = jnp.sum(residue * residue, axis=0, keepdims=True)
            d_ref[head, pair] = residue + norm_next / norm * direction
            later.append(norm_next)
        return tuple(later)

    lax.fori_loop(0, CG_STEPS, one_step, tuple(norms), unroll=4)
    for head, pair in groups:
        cols = slice(head * HDIM, (head + 1) * HDIM)
        span = slice(pair * PAIR, (pair + 1) * PAIR)
        for side in range(2):
            half = slice(side * CHUNK, (side + 1) * CHUNK)
            left_ref[head, pair, :HDIM, half] = prefix_ref[head, 2 * pair + side, HDIM:].astype(BF16)
        solved = x_ref[head, pair]
        first = dot(left_ref[head, pair], block_diag(solved.astype(BF16)))
        scores = (first[HDIM:] * weight_ref[head, pair]).astype(BF16)
        carry = rows_ref[head, pair, 0:1]
        read = carry * first[:HDIM] + dot(vt_ref[head, :, span], block_diag(scores))
        base_ref[span, cols] = read.T
        solved_ref[span, cols] = (solved * (carry * rows_ref[head, pair, 1:2])).T.astype(BF16)


def ridge_reads(ridge, grams, vectors, after=()):
    heads, _, length = vectors[0].shape
    pairs = length // PAIR
    whole = pl.BlockSpec(memory_space=pltpu.VMEM)
    state = pltpu.VMEM((heads, pairs, HDIM, PAIR), F32)
    return pl.pallas_call(
        functools.partial(read_kernel, heads, len(grams)),
        in_specs=[whole] * (1 + len(grams) + len(vectors))
        + [whole] * len(after),
        out_specs=[whole] * 2,
        out_shape=[
            jax.ShapeDtypeStruct((length, heads * HDIM), F32),
            jax.ShapeDtypeStruct((length, heads * HDIM), BF16),
        ],
        scratch_shapes=[pltpu.VMEM((heads, pairs, 2 * HDIM, PAIR), BF16), state, state, state],
        compiler_params=pltpu.CompilerParams(vmem_limit_bytes=32 * 2**20),
        cost_estimate=pl.CostEstimate(
            flops=CG_STEPS * heads * pairs * 6 * CHUNK**3 * 16,
            bytes_accessed=8 * 2**20,
            transcendentals=0,
        ),
        name="ridge_reads",
    )(ridge.reshape(1, heads), *grams, *vectors, *after)


def cross_kernel(heads, terms, *refs):
    crosses, (base_ref, solved_ref) = refs[:terms], refs[terms : terms + 2]
    outs, o_ref = refs[terms + 2 : -1], refs[-1]
    me = lax.axis_index("head")
    for head in range(heads):
        cols = slice(head * HDIM, (head + 1) * HDIM)
        cross = crosses[0][cols, :].astype(F32)
        for term in crosses[1:]:
            cross = cross + term[cols, :].astype(F32)
        read = base_ref[:, cols] + dot(solved_ref[:, cols], cross.astype(BF16))
        o_ref[:, cols] = read.astype(BF16)
    tok_rows = outs[0].shape[0]
    for distance, out_ref in enumerate(outs):
        first_row = pl.multiple_of((me ^ distance) * tok_rows, tok_rows)
        out_ref[...] = o_ref[pl.ds(first_row, tok_rows), :]


def cross_reads(crosses, base, solved, head_count):
    length, width = base.shape
    whole = pl.BlockSpec(memory_space=pltpu.VMEM)
    return pl.pallas_call(
        functools.partial(cross_kernel, width // HDIM, len(crosses)),
        in_specs=[whole] * (len(crosses) + 2),
        out_specs=[whole] * head_count,
        out_shape=[jax.ShapeDtypeStruct((length // head_count, width), BF16)] * head_count,
        scratch_shapes=[pltpu.VMEM((length, width), BF16)],
        compiler_params=pltpu.CompilerParams(vmem_limit_bytes=24 * 2**20),
        cost_estimate=pl.CostEstimate(
            flops=2 * length * width * HDIM, bytes_accessed=8 * length * width, transcendentals=0
        ),
        name="cross_reads",
    )(*crosses, base, solved)


def output_kernel(tokens_ref, w_ref, *refs):
    out_ref = refs[-1]
    me = lax.axis_index("head")
    total = tokens_ref[...].astype(F32)
    for distance, part in enumerate(refs[:-1]):
        width = part.shape[1]
        first = pl.multiple_of((me ^ distance) * width, width)
        total = total + dot(part[...], w_ref[pl.ds(first, width), :])
    out_ref[...] = total.astype(BF16)


def output_rows(tokens, w_out, reads):
    whole = pl.BlockSpec(memory_space=pltpu.VMEM)
    return pl.pallas_call(
        output_kernel,
        in_specs=[whole] * (2 + len(reads)),
        out_specs=whole,
        out_shape=jax.ShapeDtypeStruct(tokens.shape, BF16),
        compiler_params=pltpu.CompilerParams(vmem_limit_bytes=24 * 2**20),
        cost_estimate=pl.CostEstimate(
            flops=2 * tokens.shape[0] * w_out.shape[0] * w_out.shape[1],
            bytes_accessed=2 * w_out.size + 6 * tokens.size,
            transcendentals=0,
        ),
        name="output_rows",
    )(tokens, w_out, *reads)


def shards(
    tokens,
    norm_gain,
    w_qkv,
    w_gates,
    conv_weight,
    conv_state,
    decay_rate,
    ridge,
    w_out,
    cache_keys,
    cache_values,
    page_table,
    cache_lengths,
    group_prompt,
    prompt_state,
):
    head_count = lax.axis_size("head")
    owners = lax.axis_size("grp")
    bits = [head_count >> i for i in range(1, head_count.bit_length())]
    blocks = {0: tokens}
    for bit in bits:
        blocks[bit] = swap(tokens, "head", bit)

    pool, page, heads, _ = cache_keys.shape
    slots = jnp.arange(page_table.shape[1], dtype=jnp.int32)
    live = jnp.clip(cache_lengths[:, None] - slots * PAGE, 0, PAGE)
    tag = (jnp.arange(owners, dtype=jnp.int32) << 24) | group_prompt
    tag = tag[:, None] | (live << 16)
    ids = lax.axis_index("grp").astype(jnp.int32) * pool + jnp.arange(pool, dtype=jnp.int32)
    code = jnp.sum(
        jnp.where(page_table[:, :, None] == ids, tag[:, :, None], 0), axis=(0, 1), dtype=jnp.int32
    )
    keys = cache_keys.reshape(pool, page * heads, HDIM)
    values = cache_values.reshape(pool, page * heads, HDIM)

    def scattered(parts):
        sent = [swap(parts[i], "grp", 2 * i) for i in reversed(range(1, owners // 2))]
        return [parts[0]] + sent

    send_gram, send_cross, keep_gram, keep_cross = page_sums(
        code, keys, values, prompt_state, owners
    )
    got_gram = swap(send_gram, "grp", 1)
    for bit in bits[1:]:
        for distance in list(blocks):
            if distance and not distance & bit and distance ^ bit not in blocks:
                blocks[distance] = hold(blocks[distance], keep_gram)
                blocks[distance ^ bit] = swap(blocks[distance], "head", bit)
    blocks = [blocks[i] for i in range(head_count)]
    send_cross, *vectors = token_vectors(
        decay_rate, blocks, norm_gain, w_qkv, w_gates, conv_weight, conv_state, send_cross
    )
    grams = halve_sums(keep_gram, got_gram)
    crosses = halve_sums(keep_cross, swap(send_cross, "grp", 1))
    base, solved = ridge_reads(ridge, scattered(grams), vectors, [crosses[0]])
    reads = cross_reads(scattered(crosses), base, solved, head_count)
    sent = {i: swap(reads[i], "head", i) for i in reversed(range(1, head_count))}
    reads = [reads[0]] + [sent[i] for i in range(1, head_count)]
    return output_rows(tokens, w_out, reads)


def solution(mesh):
    placed = (
        P(("grp", "head"), None),
        P(),
        P(),
        P(),
        P(),
        P("grp", None, None),
        P(),
        P("head"),
        P(),
        P("grp", None, "head", None),
        P("grp", None, "head", None),
        P(),
        P(),
        P(),
        P("grp", "head", None, None, None),
    )
    return jax.shard_map(
        shards, mesh=mesh, in_specs=placed, out_specs=P(("grp", "head"), None), check_vma=False
    )
```

```python
import functools

import jax
import jax.numpy as jnp
from jax import lax
from jax.experimental import pallas as pl
from jax.experimental.pallas import tpu as pltpu
from jax.sharding import PartitionSpec as P

HEADS = 8
HDIM = 128
CONV = 4
CG_STEPS = 8
PAGE = 128
CHUNK = 128
PAIR = 2 * CHUNK
EPS_NORM = 1e-06
PAGE_VMEM = 53
TOKEN_VMEM = 48
F32 = jnp.float32
BF16 = jnp.bfloat16


def swap(block, axis, distance):
    size = lax.axis_size(axis)
    return lax.ppermute(block, axis, [(i, i ^ distance) for i in range(size)])


def hold(block, other):
    anywhere = pl.BlockSpec(memory_space=pl.ANY)
    return pl.pallas_call(
        lambda *refs: None,
        in_specs=[anywhere, anywhere],
        out_specs=anywhere,
        out_shape=jax.ShapeDtypeStruct(block.shape, block.dtype),
        input_output_aliases={0: 0},
        compiler_params=pltpu.CompilerParams(vmem_limit_bytes=2**20),
        name="hold",
    )(block, other)


def dot(a, b):
    return jnp.dot(a, b, preferred_element_type=F32)


def silu(a):
    return a * jax.nn.sigmoid(a)


def unit_rows(a):
    return a * lax.rsqrt(jnp.sum(a * a, axis=-1, keepdims=True) + EPS_NORM)


def block_diag(a):
    zero = jnp.zeros((a.shape[0], CHUNK), a.dtype)
    return jnp.concatenate(
        [
            jnp.concatenate([a[:, :CHUNK], zero], axis=1),
            jnp.concatenate([zero, a[:, CHUNK:]], axis=1),
        ],
        axis=0,
    )


def sums_kernel(heads, owners, slot_bits, code_hbm, pack_hbm, keys_hbm, values_hbm, prompt_hbm,
                send_gram, send_cross, keep_gram, keep_cross,
                acc_ref, keys_ref, values_ref, stored_ref, code_ref, pack_ref, list_ref,
                key_sem, value_sem, small_sem):
    pool, rows = keys_hbm.shape[0], keys_hbm.shape[1]
    mine = lax.axis_index("grp")
    load_code = pltpu.make_async_copy(code_hbm, code_ref, small_sem.at[0])
    load_prompt = pltpu.make_async_copy(prompt_hbm, stored_ref, small_sem.at[1])
    load_pack = pltpu.make_async_copy(pack_hbm, pack_ref, small_sem.at[2])
    load_code.start()
    load_pack.start()
    load_prompt.start()
    acc_ref[...] = jnp.zeros_like(acc_ref)
    load_code.wait()
    load_pack.wait()

    def load(item):
        page = list_ref[item] & 0xFFFF
        return (
            pltpu.make_async_copy(keys_hbm.at[page], keys_ref.at[item], key_sem.at[item]),
            pltpu.make_async_copy(values_hbm.at[page], values_ref.at[item], value_sem.at[item]),
        )

    def start(item, carry):
        for copy in load(item):
            copy.start()
        return carry

    wide = 8

    def note(chunk, count):
        for i in range(wide):
            page = chunk * wide + i
            code = code_ref[page]
            owner = code >> slot_bits
            length = pack_ref[owner] & 0xFFFF
            live = length - ((code & ((1 << slot_bits) - 1)) * PAGE)
            list_ref[count] = (owner << 24) | (jnp.minimum(live, PAGE) << 16) | page
            count = count + (live > 0).astype(jnp.int32)
        return count

    count = lax.fori_loop(0, pool // wide, note, jnp.int32(0))
    lax.fori_loop(0, count, start, 0)

    turn = 4
    turns = (count + (turn - 1)) >> 2

    def fill(item, carry):
        list_ref[item] = jnp.int32(owners << 24)
        return start(item, carry)

    lax.fori_loop(count, turns * turn, fill, 0)

    lane = lax.broadcasted_iota(jnp.int32, (HDIM, rows), 1)

    def one_turn(step, carry):
        for i in range(turn):
            for copy in load(step * turn + i):
                copy.wait()
        for i in range(turn):
            item = step * turn + i
            code = list_ref[item]
            owner, live = code >> 24, (code >> 16) & 0xFF
            keys = keys_ref[item]
            turned = keys.T
            zero = jnp.zeros_like(turned)
            left = jnp.concatenate(
                [
                    jnp.where((lane % heads == head) & (lane < live * heads), turned, zero)
                    for head in range(heads)
                ],
                axis=0,
            )
            acc_ref[owner] += dot(left, jnp.concatenate([keys, values_ref[item]], axis=1))
        return carry

    lax.fori_loop(0, turns, one_turn, 0)
    load_prompt.wait()
    stored = stored_ref.shape[0]

    def add_prompt(owner, carry):
        for slot in range(stored):

            @pl.when((pack_ref[owner] >> 16) == mine * stored + slot)
            def _():
                for head in range(heads):
                    at = slice(head * HDIM, (head + 1) * HDIM)
                    acc_ref[owner, at, :HDIM] += stored_ref[slot, head, 0]
                    acc_ref[owner, at, HDIM:] += stored_ref[slot, head, 1].T

        return carry

    lax.fori_loop(0, owners, add_prompt, 0)
    bit = mine & 1
    for pair in range(owners // 2):
        there, here = 2 * pair + 1 - bit, 2 * pair + bit
        send_gram[pair] = acc_ref[there, :, :HDIM].astype(BF16)
        send_cross[pair] = acc_ref[there, :, HDIM:].astype(BF16)
        keep_gram[pair] = acc_ref[here, :, :HDIM].astype(BF16)
        keep_cross[pair] = acc_ref[here, :, HDIM:].astype(BF16)


def page_sums(code, pack, slot_bits, keys, values, prompt_state, owners):
    pool, rows, _ = keys.shape
    heads = prompt_state.shape[1]
    half = (owners // 2, heads * HDIM, HDIM)
    items = pool + 4
    return pl.pallas_call(
        functools.partial(sums_kernel, heads, owners, slot_bits),
        in_specs=[pl.BlockSpec(memory_space=pl.ANY)] * 5,
        out_specs=[pl.BlockSpec(memory_space=pltpu.VMEM)] * 4,
        scratch_shapes=[
            pltpu.VMEM((owners + 1, heads * HDIM, 2 * HDIM), F32),
            pltpu.VMEM((items, rows, HDIM), BF16),
            pltpu.VMEM((items, rows, HDIM), BF16),
            pltpu.VMEM(prompt_state.shape, F32),
            pltpu.SMEM(code.shape, jnp.int32),
            pltpu.SMEM(pack.shape, jnp.int32),
            pltpu.SMEM((items,), jnp.int32),
            pltpu.SemaphoreType.DMA((items,)),
            pltpu.SemaphoreType.DMA((items,)),
            pltpu.SemaphoreType.DMA((3,)),
        ],
        out_shape=[jax.ShapeDtypeStruct(half, BF16)] * 4,
        compiler_params=pltpu.CompilerParams(vmem_limit_bytes=PAGE_VMEM * 2**20),
        cost_estimate=pl.CostEstimate(
            flops=8 * pool * rows * heads * HDIM * HDIM,
            bytes_accessed=4 * pool * rows * HDIM,
            transcendentals=0,
        ),
        name="page_sums",
    )(code, pack, keys, values, prompt_state)


def halve_kernel(keep_ref, got_ref, *outs):
    for distance, out_ref in enumerate(outs):
        row = (lax.axis_index("grp") >> 1) ^ distance
        total = keep_ref[row].astype(F32) + got_ref[row].astype(F32)
        out_ref[...] = total.astype(out_ref.dtype)


def halve_sums(keep, got):
    count, rows, cols = keep.shape
    outs = [jax.ShapeDtypeStruct((rows, cols), F32 if i == 0 else BF16) for i in range(count)]
    whole = pl.BlockSpec(memory_space=pltpu.VMEM)
    return pl.pallas_call(
        halve_kernel,
        in_specs=[whole, whole],
        out_specs=[whole] * count,
        out_shape=outs,
        compiler_params=pltpu.CompilerParams(vmem_limit_bytes=32 * 2**20),
        cost_estimate=pl.CostEstimate(
            flops=count * rows * cols, bytes_accessed=6 * count * rows * cols, transcendentals=0
        ),
        name="halve_sums",
    )(keep, got)


def token_kernel(heads, *refs):
    head_count = HEADS // heads
    blocks = refs[:head_count]
    (gain_ref, w_hbm, wg_ref, taps_all, state_ref, rate_ref) = refs[head_count : head_count + 6]
    (q_ref, k_ref, kt_ref, vt_ref, weight_ref, prefix_ref, rows_ref) = refs[-12:-5]
    ext_ref, gate_ref, normed_ref, w_ref, w_sem = refs[-5:]
    me = lax.axis_index("head")
    tok_rows = blocks[0].shape[0]
    width = w_ref.shape[1]
    columns = pl.ds(pl.multiple_of(me * width, HDIM), width)
    load = pltpu.make_async_copy(w_hbm.at[:, columns], w_ref, w_sem)
    load.start()
    length = tok_rows * head_count
    chunks = length // CHUNK
    base = 8
    taps_ref = taps_all[:, columns]
    ext_ref[base - (CONV - 1) : base, :] = state_ref[0, :, columns].astype(F32)
    gate_ref[...] = jnp.zeros_like(gate_ref)
    for distance, block in enumerate(blocks):
        first = pl.multiple_of((me ^ distance) * tok_rows, tok_rows)
        wide = block[...].astype(F32)
        scale = lax.rsqrt(jnp.mean(wide * wide, axis=-1, keepdims=True) + EPS_NORM)
        normed = (wide * scale * gain_ref[...]).astype(BF16)
        normed_ref[pl.ds(first, tok_rows), :] = normed
        gate_ref[pl.ds(first, tok_rows), : 2 * HEADS] = dot(normed, wg_ref[...])
    load.wait()
    for c in range(chunks):
        rows = slice(c * CHUNK, (c + 1) * CHUNK)
        mixed = dot(normed_ref[rows, :], w_ref[...]).astype(BF16)
        ext_ref[base + c * CHUNK : base + (c + 1) * CHUNK, :] = mixed.astype(F32)

    shift = lax.rem(HDIM - 2 * heads * me, HDIM)
    logits = pltpu.roll(gate_ref[...], shift, 1)
    lane = lax.broadcasted_iota(jnp.int32, (1, HDIM), 1)
    rate = jnp.zeros((1, HDIM), F32)
    for head in range(heads):
        here = lax.broadcasted_iota(jnp.int32, (1, HEADS), 1) == me * heads + head
        own = jnp.sum(jnp.where(here, rate_ref[...], 0.0), axis=1, keepdims=True)
        rate = jnp.where(lane == 2 * head + 1, own, rate)
    write = jax.nn.sigmoid(logits).astype(BF16).astype(F32)
    soft = jnp.maximum(logits, 0.0) + jnp.log1p(jnp.exp(-jnp.abs(logits)))
    decay = (-rate * soft).astype(BF16)
    here = lax.broadcasted_iota(jnp.int32, (CHUNK, CHUNK), 0)
    there = lax.broadcasted_iota(jnp.int32, (CHUNK, CHUNK), 1)
    lower = (here >= there).astype(F32).astype(BF16)
    cumul = [dot(lower, decay[c * CHUNK : (c + 1) * CHUNK]) for c in range(chunks)]
    turned = [block.T for block in cumul]

    for head in range(heads):
        parts = []
        for part in range(3):
            cols = slice((3 * head + part) * HDIM, (3 * head + part + 1) * HDIM)
            total = taps_ref[CONV - 1 : CONV, cols] * ext_ref[base : base + length, cols]
            for lag in range(1, CONV):
                total = total + taps_ref[CONV - 1 - lag : CONV - lag, cols] * (
                    ext_ref[base - lag : base - lag + length, cols]
                )
            parts.append(total)
        query = unit_rows(silu(parts[0])).astype(BF16)
        key = unit_rows(silu(parts[1])).astype(BF16)
        value = parts[2].astype(BF16)
        q_ref[head] = query.T
        k_ref[head] = key
        kt_ref[head] = key.T
        vt_ref[head] = value.T
        prefix = jnp.zeros((HDIM, 2 * HDIM), F32)
        so_far = jnp.zeros((1, 1), F32)
        for c in range(chunks):
            rows = slice(c * CHUNK, (c + 1) * CHUNK)
            col = cumul[c][:, 2 * head + 1 : 2 * head + 2]
            row = turned[c][2 * head + 1 : 2 * head + 2, :]
            gate = write[rows, 2 * head : 2 * head + 1]
            spread = jnp.exp(jnp.minimum(row - col, 0.0)) * gate
            half = slice((c % 2) * CHUNK, (c % 2 + 1) * CHUNK)
            weight_ref[head, c // 2, :, half] = jnp.where(here <= there, spread, 0.0)
            rows_ref[head, c // 2, 0:1, half] = jnp.exp(row)
            rows_ref[head, c // 2, 1:2, half] = jnp.broadcast_to(jnp.exp(so_far), (1, CHUNK))
            prefix_ref[head, c, :HDIM] = prefix[:, :HDIM]
            prefix_ref[head, c, HDIM:] = prefix[:, HDIM:].T
            if c + 1 < chunks:
                whole = cumul[c][CHUNK - 1 :, 2 * head + 1 : 2 * head + 2]
                carry = jnp.exp(whole - col) * gate
                both = jnp.concatenate([key[rows], value[rows]], axis=1).astype(F32)
                prefix = prefix * jnp.exp(whole) + dot(
                    kt_ref[head, :, rows], (both * carry).astype(BF16)
                )
                so_far = so_far + whole


def token_vectors(
    decay_rate, blocks, norm_gain, w_qkv, w_gates, conv_weight, conv_state, held
):
    head_count = len(blocks)
    heads = HEADS // head_count
    width = heads * 3 * HDIM
    tok_rows, model = blocks[0].shape
    length = head_count * tok_rows
    chunks = length // CHUNK
    whole = pl.BlockSpec(memory_space=pltpu.VMEM)
    anywhere = pl.BlockSpec(memory_space=pl.ANY)
    outs = [
        jax.ShapeDtypeStruct((heads, HDIM, length), BF16),
        jax.ShapeDtypeStruct((heads, length, HDIM), BF16),
        jax.ShapeDtypeStruct((heads, HDIM, length), BF16),
        jax.ShapeDtypeStruct((heads, HDIM, length), BF16),
        jax.ShapeDtypeStruct((heads, chunks // 2, CHUNK, PAIR), F32),
        jax.ShapeDtypeStruct((heads, chunks, 2 * HDIM, HDIM), F32),
        jax.ShapeDtypeStruct((heads, chunks // 2, 8, PAIR), F32),
    ]
    return pl.pallas_call(
        functools.partial(token_kernel, heads),
        in_specs=[whole] * head_count + [whole, anywhere] + [whole] * 4 + [anywhere],
        out_specs=[anywhere] + [whole] * len(outs),
        scratch_shapes=[
            pltpu.VMEM((8 + length, width), F32),
            pltpu.VMEM((length, HDIM), F32),
            pltpu.VMEM((length, model), BF16),
            pltpu.VMEM((model, width), BF16),
            pltpu.SemaphoreType.DMA,
        ],
        out_shape=[jax.ShapeDtypeStruct(held.shape, held.dtype)] + outs,
        input_output_aliases={head_count + 6: 0},
        compiler_params=pltpu.CompilerParams(vmem_limit_bytes=TOKEN_VMEM * 2**20),
        cost_estimate=pl.CostEstimate(
            flops=2 * length * model * width,
            bytes_accessed=2 * model * (length + width) + 4 * 2**20,
            transcendentals=length * width,
        ),
        name="token_vectors",
    )(
        *blocks,
        norm_gain.reshape(1, model),
        w_qkv,
        w_gates,
        conv_weight,
        conv_state,
        decay_rate.reshape(1, HEADS),
        held,
    )


def read_kernel(heads, terms, ridge_ref, *refs):
    grams = refs[:terms]
    (q_ref, k_ref, kt_ref, vt_ref, weight_ref, prefix_ref, rows_ref) = refs[terms : terms + 7]
    base_ref, solved_ref, left_ref, x_ref, r_ref, d_ref = refs[-6:]
    pairs = q_ref.shape[2] // PAIR
    groups = [(head, pair) for head in range(heads) for pair in range(pairs)]
    norms = []
    for head in range(heads):
        rows = slice(head * HDIM, (head + 1) * HDIM)
        gram = grams[0][rows, :].astype(F32)
        for term in grams[1:]:
            gram = gram + term[rows, :].astype(F32)
        for pair in range(pairs):
            for side in range(2):
                c = 2 * pair + side
                half = slice(side * CHUNK, (side + 1) * CHUNK)
                scale = rows_ref[head, pair, 1:2, half]
                left_ref[head, pair, :HDIM, half] = (
                    gram * scale + prefix_ref[head, c, :HDIM]
                ).astype(BF16)
                left_ref[head, pair, HDIM:, half] = k_ref[head, c * CHUNK : (c + 1) * CHUNK]
            query = q_ref[head, :, pair * PAIR : (pair + 1) * PAIR].astype(F32)
            x_ref[head, pair] = jnp.zeros_like(query)
            r_ref[head, pair] = query
            d_ref[head, pair] = query
            norms.append(jnp.sum(query * query, axis=0, keepdims=True))

    def one_step(_, norms):
        firsts = [dot(left_ref[g], block_diag(d_ref[g].astype(BF16))) for g in groups]
        seconds = []
        for (head, pair), first in zip(groups, firsts):
            scores = (first[HDIM:] * weight_ref[head, pair]).astype(BF16)
            seconds.append(
                dot(kt_ref[head, :, pair * PAIR : (pair + 1) * PAIR], block_diag(scores))
            )
        later = []
        for (head, pair), first, second, norm in zip(groups, firsts, seconds, norms):
            direction = d_ref[head, pair]
            image = (
                rows_ref[head, pair, 0:1] * first[:HDIM] + ridge_ref[:, head : head + 1] * direction + second
            )
            alpha = norm / jnp.sum(direction * image, axis=0, keepdims=True)
            x_ref[head, pair] += alpha * direction
            residue = r_ref[head, pair] - alpha * image
            r_ref[head, pair] = residue
            norm_next = jnp.sum(residue * residue, axis=0, keepdims=True)
            d_ref[head, pair] = residue + norm_next / norm * direction
            later.append(norm_next)
        return tuple(later)

    lax.fori_loop(0, CG_STEPS, one_step, tuple(norms), unroll=4)
    for head, pair in groups:
        cols = slice(head * HDIM, (head + 1) * HDIM)
        span = slice(pair * PAIR, (pair + 1) * PAIR)
        for side in range(2):
            half = slice(side * CHUNK, (side + 1) * CHUNK)
            left_ref[head, pair, :HDIM, half] = prefix_ref[head, 2 * pair + side, HDIM:].astype(BF16)
        solved = x_ref[head, pair]
        first = dot(left_ref[head, pair], block_diag(solved.astype(BF16)))
        scores = (first[HDIM:] * weight_ref[head, pair]).astype(BF16)
        carry = rows_ref[head, pair, 0:1]
        read = carry * first[:HDIM] + dot(vt_ref[head, :, span], block_diag(scores))
        base_ref[span, cols] = read.T
        solved_ref[span, cols] = (solved * (carry * rows_ref[head, pair, 1:2])).T.astype(BF16)


def ridge_reads(ridge, grams, vectors, after=()):
    heads, _, length = vectors[0].shape
    pairs = length // PAIR
    whole = pl.BlockSpec(memory_space=pltpu.VMEM)
    state = pltpu.VMEM((heads, pairs, HDIM, PAIR), F32)
    return pl.pallas_call(
        functools.partial(read_kernel, heads, len(grams)),
        in_specs=[whole] * (1 + len(grams) + len(vectors))
        + [whole] * len(after),
        out_specs=[whole] * 2,
        out_shape=[
            jax.ShapeDtypeStruct((length, heads * HDIM), F32),
            jax.ShapeDtypeStruct((length, heads * HDIM), BF16),
        ],
        scratch_shapes=[pltpu.VMEM((heads, pairs, 2 * HDIM, PAIR), BF16), state, state, state],
        compiler_params=pltpu.CompilerParams(vmem_limit_bytes=32 * 2**20),
        cost_estimate=pl.CostEstimate(
            flops=CG_STEPS * heads * pairs * 6 * CHUNK**3 * 16,
            bytes_accessed=8 * 2**20,
            transcendentals=0,
        ),
        name="ridge_reads",
    )(ridge.reshape(1, heads), *grams, *vectors, *after)


def cross_kernel(heads, terms, *refs):
    crosses, (base_ref, solved_ref) = refs[:terms], refs[terms : terms + 2]
    outs, o_ref = refs[terms + 2 : -1], refs[-1]
    me = lax.axis_index("head")
    for head in range(heads):
        cols = slice(head * HDIM, (head + 1) * HDIM)
        cross = crosses[0][cols, :].astype(F32)
        for term in crosses[1:]:
            cross = cross + term[cols, :].astype(F32)
        read = base_ref[:, cols] + dot(solved_ref[:, cols], cross.astype(BF16))
        o_ref[:, cols] = read.astype(BF16)
    tok_rows = outs[0].shape[0]
    for distance, out_ref in enumerate(outs):
        first_row = pl.multiple_of((me ^ distance) * tok_rows, tok_rows)
        out_ref[...] = o_ref[pl.ds(first_row, tok_rows), :]


def cross_reads(crosses, base, solved, head_count):
    length, width = base.shape
    whole = pl.BlockSpec(memory_space=pltpu.VMEM)
    return pl.pallas_call(
        functools.partial(cross_kernel, width // HDIM, len(crosses)),
        in_specs=[whole] * (len(crosses) + 2),
        out_specs=[whole] * head_count,
        out_shape=[jax.ShapeDtypeStruct((length // head_count, width), BF16)] * head_count,
        scratch_shapes=[pltpu.VMEM((length, width), BF16)],
        compiler_params=pltpu.CompilerParams(vmem_limit_bytes=24 * 2**20),
        cost_estimate=pl.CostEstimate(
            flops=2 * length * width * HDIM, bytes_accessed=8 * length * width, transcendentals=0
        ),
        name="cross_reads",
    )(*crosses, base, solved)


def output_kernel(distances, start_ref, w_ref, *refs):
    out_ref = refs[-1]
    me = lax.axis_index("head")
    total = start_ref[...].astype(F32)
    for distance, part in zip(distances, refs[:-1]):
        width = part.shape[1]
        first = pl.multiple_of((me ^ distance) * width, width)
        total = total + dot(part[...], w_ref[pl.ds(first, width), :])
    out_ref[...] = total.astype(out_ref.dtype)


def output_rows(start, w_out, parts, distances, dtype):
    whole = pl.BlockSpec(memory_space=pltpu.VMEM)
    return pl.pallas_call(
        functools.partial(output_kernel, distances),
        in_specs=[whole] * (2 + len(parts)),
        out_specs=whole,
        out_shape=jax.ShapeDtypeStruct(start.shape, dtype),
        compiler_params=pltpu.CompilerParams(vmem_limit_bytes=24 * 2**20),
        cost_estimate=pl.CostEstimate(
            flops=2 * start.shape[0] * parts[0].shape[1] * len(parts) * w_out.shape[1],
            bytes_accessed=2 * w_out.size + 6 * start.size,
            transcendentals=0,
        ),
        name="output_rows",
    )(start, w_out, *parts)


def shards(
    tokens,
    norm_gain,
    w_qkv,
    w_gates,
    conv_weight,
    conv_state,
    decay_rate,
    ridge,
    w_out,
    cache_keys,
    cache_values,
    page_table,
    cache_lengths,
    group_prompt,
    prompt_state,
):
    head_count = lax.axis_size("head")
    owners = lax.axis_size("grp")
    bits = [head_count >> i for i in range(1, head_count.bit_length())]
    blocks = {0: tokens}
    for bit in bits:
        blocks[bit] = swap(tokens, "head", bit)

    pool, page, heads, _ = cache_keys.shape
    slots = page_table.shape[1]
    slot_bits = slots.bit_length() - 1
    assert slots == 1 << slot_bits
    tag = jnp.arange(owners * slots, dtype=jnp.int32).reshape(owners, slots)
    pack = cache_lengths | (group_prompt << 16)
    ids = lax.axis_index("grp").astype(jnp.int32) * pool + jnp.arange(pool, dtype=jnp.int32)
    code = jnp.sum(
        jnp.where(page_table[:, :, None] == ids, tag[:, :, None], 0), axis=(0, 1), dtype=jnp.int32
    )
    keys = cache_keys.reshape(pool, page * heads, HDIM)
    values = cache_values.reshape(pool, page * heads, HDIM)

    def scattered(parts):
        sent = [swap(parts[i], "grp", 2 * i) for i in reversed(range(1, owners // 2))]
        return [parts[0]] + sent

    send_gram, send_cross, keep_gram, keep_cross = page_sums(
        code, pack, slot_bits, keys, values, prompt_state, owners
    )
    got_gram = swap(send_gram, "grp", 1)
    for bit in bits[1:]:
        for distance in list(blocks):
            if distance and not distance & bit and distance ^ bit not in blocks:
                blocks[distance] = hold(blocks[distance], keep_gram)
                blocks[distance ^ bit] = swap(blocks[distance], "head", bit)
    blocks = [blocks[i] for i in range(head_count)]
    send_cross, *vectors = token_vectors(
        decay_rate, blocks, norm_gain, w_qkv, w_gates, conv_weight, conv_state, send_cross
    )
    grams = halve_sums(keep_gram, got_gram)
    crosses = halve_sums(keep_cross, swap(send_cross, "grp", 1))
    base, solved = ridge_reads(ridge, scattered(grams), vectors, [crosses[0]])
    reads = cross_reads(scattered(crosses), base, solved, head_count)
    parts = [reads[0]] + [swap(reads[i], "head", i) for i in range(1, head_count)]
    total = output_rows(tokens, w_out, parts[:2], (0, 1), F32)
    return output_rows(total, w_out, parts[2:], tuple(range(2, head_count)), BF16)


def solution(mesh):
    placed = (
        P(("grp", "head"), None),
        P(),
        P(),
        P(),
        P(),
        P("grp", None, None),
        P(),
        P("head"),
        P(),
        P("grp", None, "head", None),
        P("grp", None, "head", None),
        P(),
        P(),
        P(),
        P("grp", "head", None, None, None),
    )
    return jax.shard_map(
        shards, mesh=mesh, in_specs=placed, out_specs=P(("grp", "head"), None), check_vma=False
    )
```

```python
import functools

import jax
import jax.numpy as jnp
from jax import lax
from jax.experimental import pallas as pl
from jax.experimental.pallas import tpu as pltpu
from jax.sharding import PartitionSpec as P

HEADS = 8
HDIM = 128
CONV = 4
CG_STEPS = 8
PAGE = 128
CHUNK = 128
PAIR = 2 * CHUNK
EPS_NORM = 1e-06
BASE = 8
PAGE_VMEM = 53
TOKEN_VMEM = 48
F32 = jnp.float32
BF16 = jnp.bfloat16


def swap(block, axis, distance):
    size = lax.axis_size(axis)
    return lax.ppermute(block, axis, [(i, i ^ distance) for i in range(size)])


def hold(block, other):
    anywhere = pl.BlockSpec(memory_space=pl.ANY)
    return pl.pallas_call(
        lambda *refs: None,
        in_specs=[anywhere, anywhere],
        out_specs=anywhere,
        out_shape=jax.ShapeDtypeStruct(block.shape, block.dtype),
        input_output_aliases={0: 0},
        compiler_params=pltpu.CompilerParams(vmem_limit_bytes=2**20),
        name="hold",
    )(block, other)


def dot(a, b):
    return jnp.dot(a, b, preferred_element_type=F32)


def silu(a):
    return a * jax.nn.sigmoid(a)


def unit_rows(a):
    return a * lax.rsqrt(jnp.sum(a * a, axis=-1, keepdims=True) + EPS_NORM)


def block_diag(a):
    zero = jnp.zeros((a.shape[0], CHUNK), a.dtype)
    return jnp.concatenate(
        [
            jnp.concatenate([a[:, :CHUNK], zero], axis=1),
            jnp.concatenate([zero, a[:, CHUNK:]], axis=1),
        ],
        axis=0,
    )


def sums_kernel(heads, owners, slot_bits, code_hbm, pack_hbm, keys_hbm, values_hbm, prompt_hbm,
                send_gram, send_cross, keep_gram, keep_cross,
                acc_ref, keys_ref, values_ref, stored_ref, code_ref, pack_ref, list_ref,
                key_sem, value_sem, small_sem):
    pool, rows = keys_hbm.shape[0], keys_hbm.shape[1]
    mine = lax.axis_index("grp")
    load_code = pltpu.make_async_copy(code_hbm, code_ref, small_sem.at[0])
    load_prompt = pltpu.make_async_copy(prompt_hbm, stored_ref, small_sem.at[1])
    load_pack = pltpu.make_async_copy(pack_hbm, pack_ref, small_sem.at[2])
    load_code.start()
    load_pack.start()
    load_prompt.start()
    acc_ref[...] = jnp.zeros_like(acc_ref)
    load_code.wait()
    load_pack.wait()

    def load(item):
        page = list_ref[item] & 0xFFFF
        return (
            pltpu.make_async_copy(keys_hbm.at[page], keys_ref.at[item], key_sem.at[item]),
            pltpu.make_async_copy(values_hbm.at[page], values_ref.at[item], value_sem.at[item]),
        )

    def start(item, carry):
        for copy in load(item):
            copy.start()
        return carry

    wide = 8

    def note(chunk, count):
        for i in range(wide):
            page = chunk * wide + i
            code = code_ref[page]
            owner = code >> slot_bits
            length = pack_ref[owner] & 0xFFFF
            live = length - ((code & ((1 << slot_bits) - 1)) * PAGE)
            list_ref[count] = (owner << 24) | (jnp.minimum(live, PAGE) << 16) | page
            count = count + (live > 0).astype(jnp.int32)
        return count

    count = lax.fori_loop(0, pool // wide, note, jnp.int32(0))
    lax.fori_loop(0, count, start, 0)

    turn = 4
    turns = (count + (turn - 1)) >> 2

    def fill(item, carry):
        list_ref[item] = jnp.int32(owners << 24)
        return start(item, carry)

    lax.fori_loop(count, turns * turn, fill, 0)

    lane = lax.broadcasted_iota(jnp.int32, (HDIM, rows), 1)

    def one_turn(step, carry):
        for i in range(turn):
            for copy in load(step * turn + i):
                copy.wait()
        for i in range(turn):
            item = step * turn + i
            code = list_ref[item]
            owner, live = code >> 24, (code >> 16) & 0xFF
            keys = keys_ref[item]
            turned = keys.T
            zero = jnp.zeros_like(turned)
            left = jnp.concatenate(
                [
                    jnp.where((lane % heads == head) & (lane < live * heads), turned, zero)
                    for head in range(heads)
                ],
                axis=0,
            )
            acc_ref[owner] += dot(left, jnp.concatenate([keys, values_ref[item]], axis=1))
        return carry

    lax.fori_loop(0, turns, one_turn, 0)
    load_prompt.wait()
    stored = stored_ref.shape[0]

    def add_prompt(owner, carry):
        for slot in range(stored):

            @pl.when((pack_ref[owner] >> 16) == mine * stored + slot)
            def _():
                for head in range(heads):
                    at = slice(head * HDIM, (head + 1) * HDIM)
                    acc_ref[owner, at, :HDIM] += stored_ref[slot, head, 0]
                    acc_ref[owner, at, HDIM:] += stored_ref[slot, head, 1].T

        return carry

    lax.fori_loop(0, owners, add_prompt, 0)
    bit = mine & 1
    for pair in range(owners // 2):
        there, here = 2 * pair + 1 - bit, 2 * pair + bit
        send_gram[pair] = acc_ref[there, :, :HDIM].astype(BF16)
        send_cross[pair] = acc_ref[there, :, HDIM:].astype(BF16)
        keep_gram[pair] = acc_ref[here, :, :HDIM].astype(BF16)
        keep_cross[pair] = acc_ref[here, :, HDIM:].astype(BF16)


def page_sums(code, pack, slot_bits, keys, values, prompt_state, owners):
    pool, rows, _ = keys.shape
    heads = prompt_state.shape[1]
    half = (owners // 2, heads * HDIM, HDIM)
    items = pool + 4
    return pl.pallas_call(
        functools.partial(sums_kernel, heads, owners, slot_bits),
        in_specs=[pl.BlockSpec(memory_space=pl.ANY)] * 5,
        out_specs=[pl.BlockSpec(memory_space=pltpu.VMEM)] * 4,
        scratch_shapes=[
            pltpu.VMEM((owners + 1, heads * HDIM, 2 * HDIM), F32),
            pltpu.VMEM((items, rows, HDIM), BF16),
            pltpu.VMEM((items, rows, HDIM), BF16),
            pltpu.VMEM(prompt_state.shape, F32),
            pltpu.SMEM(code.shape, jnp.int32),
            pltpu.SMEM(pack.shape, jnp.int32),
            pltpu.SMEM((items,), jnp.int32),
            pltpu.SemaphoreType.DMA((items,)),
            pltpu.SemaphoreType.DMA((items,)),
            pltpu.SemaphoreType.DMA((3,)),
        ],
        out_shape=[jax.ShapeDtypeStruct(half, BF16)] * 4,
        compiler_params=pltpu.CompilerParams(vmem_limit_bytes=PAGE_VMEM * 2**20),
        cost_estimate=pl.CostEstimate(
            flops=8 * pool * rows * heads * HDIM * HDIM,
            bytes_accessed=4 * pool * rows * HDIM,
            transcendentals=0,
        ),
        name="page_sums",
    )(code, pack, keys, values, prompt_state)


def halve_kernel(keep_ref, got_ref, *outs):
    for distance, out_ref in enumerate(outs):
        row = (lax.axis_index("grp") >> 1) ^ distance
        total = keep_ref[row].astype(F32) + got_ref[row].astype(F32)
        out_ref[...] = total.astype(out_ref.dtype)


def halve_sums(keep, got):
    count, rows, cols = keep.shape
    outs = [jax.ShapeDtypeStruct((rows, cols), F32 if i == 0 else BF16) for i in range(count)]
    whole = pl.BlockSpec(memory_space=pltpu.VMEM)
    return pl.pallas_call(
        halve_kernel,
        in_specs=[whole, whole],
        out_specs=[whole] * count,
        out_shape=outs,
        compiler_params=pltpu.CompilerParams(vmem_limit_bytes=32 * 2**20),
        cost_estimate=pl.CostEstimate(
            flops=count * rows * cols, bytes_accessed=6 * count * rows * cols, transcendentals=0
        ),
        name="halve_sums",
    )(keep, got)


def project_kernel(heads, *refs):
    head_count = HEADS // heads
    blocks = refs[:head_count]
    (gain_ref, w_hbm, wg_ref, state_ref) = refs[head_count : head_count + 4]
    ext_ref, gate_ref, normed_ref, w_ref, w_sem = refs[-5:]
    me = lax.axis_index("head")
    tok_rows = blocks[0].shape[0]
    width = w_ref.shape[1]
    columns = pl.ds(pl.multiple_of(me * width, HDIM), width)
    load = pltpu.make_async_copy(w_hbm.at[:, columns], w_ref, w_sem)
    load.start()
    chunks = tok_rows * head_count // CHUNK
    ext_ref[BASE - (CONV - 1) : BASE, :] = state_ref[0, :, columns].astype(F32)
    gate_ref[...] = jnp.zeros_like(gate_ref)
    for distance, block in enumerate(blocks):
        first = pl.multiple_of((me ^ distance) * tok_rows, tok_rows)
        wide = block[...].astype(F32)
        scale = lax.rsqrt(jnp.mean(wide * wide, axis=-1, keepdims=True) + EPS_NORM)
        normed = (wide * scale * gain_ref[...]).astype(BF16)
        normed_ref[pl.ds(first, tok_rows), :] = normed
        gate_ref[pl.ds(first, tok_rows), : 2 * HEADS] = dot(normed, wg_ref[...])
    load.wait()
    for c in range(chunks):
        rows = slice(c * CHUNK, (c + 1) * CHUNK)
        mixed = dot(normed_ref[rows, :], w_ref[...]).astype(BF16)
        ext_ref[BASE + c * CHUNK : BASE + (c + 1) * CHUNK, :] = mixed.astype(F32)


def project(blocks, norm_gain, w_qkv, w_gates, conv_state, held):
    head_count = len(blocks)
    heads = HEADS // head_count
    width = heads * 3 * HDIM
    tok_rows, model = blocks[0].shape
    length = head_count * tok_rows
    whole = pl.BlockSpec(memory_space=pltpu.VMEM)
    anywhere = pl.BlockSpec(memory_space=pl.ANY)
    return pl.pallas_call(
        functools.partial(project_kernel, heads),
        in_specs=[whole] * head_count + [whole, anywhere] + [whole] * 2 + [anywhere],
        out_specs=[anywhere, whole, whole],
        scratch_shapes=[
            pltpu.VMEM((length, model), BF16),
            pltpu.VMEM((model, width), BF16),
            pltpu.SemaphoreType.DMA,
        ],
        out_shape=[
            jax.ShapeDtypeStruct(held.shape, held.dtype),
            jax.ShapeDtypeStruct((BASE + length, width), F32),
            jax.ShapeDtypeStruct((length, HDIM), F32),
        ],
        input_output_aliases={head_count + 4: 0},
        compiler_params=pltpu.CompilerParams(vmem_limit_bytes=TOKEN_VMEM * 2**20),
        cost_estimate=pl.CostEstimate(
            flops=2 * length * model * width,
            bytes_accessed=2 * model * (length + width) + 4 * length * width,
            transcendentals=0,
        ),
        name="project",
    )(*blocks, norm_gain.reshape(1, model), w_qkv, w_gates, conv_state, held)


def token_kernel(heads, *refs):
    ext_ref, gate_ref, taps_all, rate_ref = refs[:4]
    (q_ref, k_ref, kt_ref, vt_ref, weight_ref, prefix_ref, rows_ref) = refs[4:]
    me = lax.axis_index("head")
    width = ext_ref.shape[1]
    taps_ref = taps_all[:, pl.ds(pl.multiple_of(me * width, HDIM), width)]
    base = BASE
    length = gate_ref.shape[0]
    chunks = length // CHUNK

    shift = lax.rem(HDIM - 2 * heads * me, HDIM)
    logits = pltpu.roll(gate_ref[...], shift, 1)
    lane = lax.broadcasted_iota(jnp.int32, (1, HDIM), 1)
    rate = jnp.zeros((1, HDIM), F32)
    for head in range(heads):
        here = lax.broadcasted_iota(jnp.int32, (1, HEADS), 1) == me * heads + head
        own = jnp.sum(jnp.where(here, rate_ref[...], 0.0), axis=1, keepdims=True)
        rate = jnp.where(lane == 2 * head + 1, own, rate)
    write = jax.nn.sigmoid(logits).astype(BF16).astype(F32)
    soft = jnp.maximum(logits, 0.0) + jnp.log1p(jnp.exp(-jnp.abs(logits)))
    decay = (-rate * soft).astype(BF16)
    here = lax.broadcasted_iota(jnp.int32, (CHUNK, CHUNK), 0)
    there = lax.broadcasted_iota(jnp.int32, (CHUNK, CHUNK), 1)
    lower = (here >= there).astype(F32).astype(BF16)
    cumul = [dot(lower, decay[c * CHUNK : (c + 1) * CHUNK]) for c in range(chunks)]
    turned = [block.T for block in cumul]

    for head in range(heads):
        parts = []
        for part in range(3):
            cols = slice((3 * head + part) * HDIM, (3 * head + part + 1) * HDIM)
            total = taps_ref[CONV - 1 : CONV, cols] * ext_ref[base : base + length, cols]
            for lag in range(1, CONV):
                total = total + taps_ref[CONV - 1 - lag : CONV - lag, cols] * (
                    ext_ref[base - lag : base - lag + length, cols]
                )
            parts.append(total)
        query = unit_rows(silu(parts[0])).astype(BF16)
        key = unit_rows(silu(parts[1])).astype(BF16)
        value = parts[2].astype(BF16)
        q_ref[head] = query.T
        k_ref[head] = key
        kt_ref[head] = key.T
        vt_ref[head] = value.T
        prefix = jnp.zeros((HDIM, 2 * HDIM), F32)
        so_far = jnp.zeros((1, 1), F32)
        for c in range(chunks):
            rows = slice(c * CHUNK, (c + 1) * CHUNK)
            col = cumul[c][:, 2 * head + 1 : 2 * head + 2]
            row = turned[c][2 * head + 1 : 2 * head + 2, :]
            gate = write[rows, 2 * head : 2 * head + 1]
            spread = jnp.exp(jnp.minimum(row - col, 0.0)) * gate
            half = slice((c % 2) * CHUNK, (c % 2 + 1) * CHUNK)
            weight_ref[head, c // 2, :, half] = jnp.where(here <= there, spread, 0.0)
            rows_ref[head, c // 2, 0:1, half] = jnp.exp(row)
            rows_ref[head, c // 2, 1:2, half] = jnp.broadcast_to(jnp.exp(so_far), (1, CHUNK))
            prefix_ref[head, c, :HDIM] = prefix[:, :HDIM]
            prefix_ref[head, c, HDIM:] = prefix[:, HDIM:].T
            if c + 1 < chunks:
                whole = cumul[c][CHUNK - 1 :, 2 * head + 1 : 2 * head + 2]
                carry = jnp.exp(whole - col) * gate
                both = jnp.concatenate([key[rows], value[rows]], axis=1).astype(F32)
                prefix = prefix * jnp.exp(whole) + dot(
                    kt_ref[head, :, rows], (both * carry).astype(BF16)
                )
                so_far = so_far + whole


def token_vectors(ext, gates, conv_weight, decay_rate):
    length = gates.shape[0]
    heads = ext.shape[1] // (3 * HDIM)
    chunks = length // CHUNK
    whole = pl.BlockSpec(memory_space=pltpu.VMEM)
    outs = [
        jax.ShapeDtypeStruct((heads, HDIM, length), BF16),
        jax.ShapeDtypeStruct((heads, length, HDIM), BF16),
        jax.ShapeDtypeStruct((heads, HDIM, length), BF16),
        jax.ShapeDtypeStruct((heads, HDIM, length), BF16),
        jax.ShapeDtypeStruct((heads, chunks // 2, CHUNK, PAIR), F32),
        jax.ShapeDtypeStruct((heads, chunks, 2 * HDIM, HDIM), F32),
        jax.ShapeDtypeStruct((heads, chunks // 2, 8, PAIR), F32),
    ]
    return pl.pallas_call(
        functools.partial(token_kernel, heads),
        in_specs=[whole] * 4,
        out_specs=[whole] * len(outs),
        out_shape=outs,
        compiler_params=pltpu.CompilerParams(vmem_limit_bytes=32 * 2**20),
        cost_estimate=pl.CostEstimate(
            flops=64 * ext.size, bytes_accessed=4 * ext.size, transcendentals=ext.size
        ),
        name="token_vectors",
    )(ext, gates, conv_weight, decay_rate.reshape(1, HEADS))


def read_kernel(heads, terms, ridge_ref, *refs):
    grams = refs[:terms]
    (q_ref, k_ref, kt_ref, vt_ref, weight_ref, prefix_ref, rows_ref) = refs[terms : terms + 7]
    base_ref, solved_ref, left_ref, x_ref, r_ref, d_ref = refs[-6:]
    pairs = q_ref.shape[2] // PAIR
    groups = [(head, pair) for head in range(heads) for pair in range(pairs)]
    norms = []
    for head in range(heads):
        rows = slice(head * HDIM, (head + 1) * HDIM)
        gram = grams[0][rows, :].astype(F32)
        for term in grams[1:]:
            gram = gram + term[rows, :].astype(F32)
        for pair in range(pairs):
            for side in range(2):
                c = 2 * pair + side
                half = slice(side * CHUNK, (side + 1) * CHUNK)
                scale = rows_ref[head, pair, 1:2, half]
                left_ref[head, pair, :HDIM, half] = (
                    gram * scale + prefix_ref[head, c, :HDIM]
                ).astype(BF16)
                left_ref[head, pair, HDIM:, half] = k_ref[head, c * CHUNK : (c + 1) * CHUNK]
            query = q_ref[head, :, pair * PAIR : (pair + 1) * PAIR].astype(F32)
            x_ref[head, pair] = jnp.zeros_like(query)
            r_ref[head, pair] = query
            d_ref[head, pair] = query
            norms.append(jnp.sum(query * query, axis=0, keepdims=True))

    def one_step(_, norms):
        firsts = [dot(left_ref[g], block_diag(d_ref[g].astype(BF16))) for g in groups]
        seconds = []
        for (head, pair), first in zip(groups, firsts):
            scores = (first[HDIM:] * weight_ref[head, pair]).astype(BF16)
            seconds.append(
                dot(kt_ref[head, :, pair * PAIR : (pair + 1) * PAIR], block_diag(scores))
            )
        later = []
        for (head, pair), first, second, norm in zip(groups, firsts, seconds, norms):
            direction = d_ref[head, pair]
            image = (
                rows_ref[head, pair, 0:1] * first[:HDIM] + ridge_ref[:, head : head + 1] * direction + second
            )
            alpha = norm / jnp.sum(direction * image, axis=0, keepdims=True)
            x_ref[head, pair] += alpha * direction
            residue = r_ref[head, pair] - alpha * image
            r_ref[head, pair] = residue
            norm_next = jnp.sum(residue * residue, axis=0, keepdims=True)
            d_ref[head, pair] = residue + norm_next / norm * direction
            later.append(norm_next)
        return tuple(later)

    lax.fori_loop(0, CG_STEPS, one_step, tuple(norms), unroll=4)
    for head, pair in groups:
        cols = slice(head * HDIM, (head + 1) * HDIM)
        span = slice(pair * PAIR, (pair + 1) * PAIR)
        for side in range(2):
            half = slice(side * CHUNK, (side + 1) * CHUNK)
            left_ref[head, pair, :HDIM, half] = prefix_ref[head, 2 * pair + side, HDIM:].astype(BF16)
        solved = x_ref[head, pair]
        first = dot(left_ref[head, pair], block_diag(solved.astype(BF16)))
        scores = (first[HDIM:] * weight_ref[head, pair]).astype(BF16)
        carry = rows_ref[head, pair, 0:1]
        read = carry * first[:HDIM] + dot(vt_ref[head, :, span], block_diag(scores))
        base_ref[span, cols] = read.T
        solved_ref[span, cols] = (solved * (carry * rows_ref[head, pair, 1:2])).T.astype(BF16)


def ridge_reads(ridge, grams, vectors, after=()):
    heads, _, length = vectors[0].shape
    pairs = length // PAIR
    whole = pl.BlockSpec(memory_space=pltpu.VMEM)
    state = pltpu.VMEM((heads, pairs, HDIM, PAIR), F32)
    return pl.pallas_call(
        functools.partial(read_kernel, heads, len(grams)),
        in_specs=[whole] * (1 + len(grams) + len(vectors))
        + [whole] * len(after),
        out_specs=[whole] * 2,
        out_shape=[
            jax.ShapeDtypeStruct((length, heads * HDIM), F32),
            jax.ShapeDtypeStruct((length, heads * HDIM), BF16),
        ],
        scratch_shapes=[pltpu.VMEM((heads, pairs, 2 * HDIM, PAIR), BF16), state, state, state],
        compiler_params=pltpu.CompilerParams(vmem_limit_bytes=32 * 2**20),
        cost_estimate=pl.CostEstimate(
            flops=CG_STEPS * heads * pairs * 6 * CHUNK**3 * 16,
            bytes_accessed=8 * 2**20,
            transcendentals=0,
        ),
        name="ridge_reads",
    )(ridge.reshape(1, heads), *grams, *vectors, *after)


def cross_kernel(heads, terms, *refs):
    crosses, (base_ref, solved_ref) = refs[:terms], refs[terms : terms + 2]
    outs, o_ref = refs[terms + 2 : -1], refs[-1]
    me = lax.axis_index("head")
    for head in range(heads):
        cols = slice(head * HDIM, (head + 1) * HDIM)
        cross = crosses[0][cols, :].astype(F32)
        for term in crosses[1:]:
            cross = cross + term[cols, :].astype(F32)
        read = base_ref[:, cols] + dot(solved_ref[:, cols], cross.astype(BF16))
        o_ref[:, cols] = read.astype(BF16)
    tok_rows = outs[0].shape[0]
    for distance, out_ref in enumerate(outs):
        first_row = pl.multiple_of((me ^ distance) * tok_rows, tok_rows)
        out_ref[...] = o_ref[pl.ds(first_row, tok_rows), :]


def cross_reads(crosses, base, solved, head_count):
    length, width = base.shape
    whole = pl.BlockSpec(memory_space=pltpu.VMEM)
    return pl.pallas_call(
        functools.partial(cross_kernel, width // HDIM, len(crosses)),
        in_specs=[whole] * (len(crosses) + 2),
        out_specs=[whole] * head_count,
        out_shape=[jax.ShapeDtypeStruct((length // head_count, width), BF16)] * head_count,
        scratch_shapes=[pltpu.VMEM((length, width), BF16)],
        compiler_params=pltpu.CompilerParams(vmem_limit_bytes=24 * 2**20),
        cost_estimate=pl.CostEstimate(
            flops=2 * length * width * HDIM, bytes_accessed=8 * length * width, transcendentals=0
        ),
        name="cross_reads",
    )(*crosses, base, solved)


def output_kernel(distances, start_ref, w_ref, *refs):
    out_ref = refs[-1]
    me = lax.axis_index("head")
    total = start_ref[...].astype(F32)
    for distance, part in zip(distances, refs[:-1]):
        width = part.shape[1]
        first = pl.multiple_of((me ^ distance) * width, width)
        total = total + dot(part[...], w_ref[pl.ds(first, width), :])
    out_ref[...] = total.astype(out_ref.dtype)


def output_rows(start, w_out, parts, distances, dtype):
    whole = pl.BlockSpec(memory_space=pltpu.VMEM)
    return pl.pallas_call(
        functools.partial(output_kernel, distances),
        in_specs=[whole] * (2 + len(parts)),
        out_specs=whole,
        out_shape=jax.ShapeDtypeStruct(start.shape, dtype),
        compiler_params=pltpu.CompilerParams(vmem_limit_bytes=24 * 2**20),
        cost_estimate=pl.CostEstimate(
            flops=2 * start.shape[0] * parts[0].shape[1] * len(parts) * w_out.shape[1],
            bytes_accessed=2 * w_out.size + 6 * start.size,
            transcendentals=0,
        ),
        name="output_rows",
    )(start, w_out, *parts)


def shards(
    tokens,
    norm_gain,
    w_qkv,
    w_gates,
    conv_weight,
    conv_state,
    decay_rate,
    ridge,
    w_out,
    cache_keys,
    cache_values,
    page_table,
    cache_lengths,
    group_prompt,
    prompt_state,
):
    head_count = lax.axis_size("head")
    owners = lax.axis_size("grp")
    bits = [head_count >> i for i in range(1, head_count.bit_length())]
    blocks = {0: tokens}
    for bit in bits:
        blocks[bit] = swap(tokens, "head", bit)

    pool, page, heads, _ = cache_keys.shape
    slots = page_table.shape[1]
    slot_bits = slots.bit_length() - 1
    assert slots == 1 << slot_bits
    tag = jnp.arange(owners * slots, dtype=jnp.int32).reshape(owners, slots)
    pack = cache_lengths | (group_prompt << 16)
    ids = lax.axis_index("grp").astype(jnp.int32) * pool + jnp.arange(pool, dtype=jnp.int32)
    code = jnp.sum(
        jnp.where(page_table[:, :, None] == ids, tag[:, :, None], 0), axis=(0, 1), dtype=jnp.int32
    )
    keys = cache_keys.reshape(pool, page * heads, HDIM)
    values = cache_values.reshape(pool, page * heads, HDIM)

    def scattered(parts):
        sent = [swap(parts[i], "grp", 2 * i) for i in reversed(range(1, owners // 2))]
        return [parts[0]] + sent

    send_gram, send_cross, keep_gram, keep_cross = page_sums(
        code, pack, slot_bits, keys, values, prompt_state, owners
    )
    got_gram = swap(send_gram, "grp", 1)
    for bit in bits[1:]:
        for distance in list(blocks):
            if distance and not distance & bit and distance ^ bit not in blocks:
                blocks[distance] = hold(blocks[distance], keep_gram)
                blocks[distance ^ bit] = swap(blocks[distance], "head", bit)
    blocks = [blocks[i] for i in range(head_count)]
    send_cross, ext, gates = project(blocks, norm_gain, w_qkv, w_gates, conv_state, send_cross)
    got_cross = swap(send_cross, "grp", 1)
    vectors = token_vectors(ext, gates, conv_weight, decay_rate)
    grams = halve_sums(keep_gram, got_gram)
    crosses = halve_sums(keep_cross, got_cross)
    base, solved = ridge_reads(ridge, scattered(grams), vectors, [crosses[0]])
    reads = cross_reads(scattered(crosses), base, solved, head_count)
    far = tuple(reversed(range(1, head_count)))
    parts = [swap(reads[i], "head", i) for i in far]
    total = output_rows(tokens, w_out, reads[:1], (0,), F32)
    return output_rows(total, w_out, parts, far, BF16)


def solution(mesh):
    placed = (
        P(("grp", "head"), None),
        P(),
        P(),
        P(),
        P(),
        P("grp", None, None),
        P(),
        P("head"),
        P(),
        P("grp", None, "head", None),
        P("grp", None, "head", None),
        P(),
        P(),
        P(),
        P("grp", "head", None, None, None),
    )
    return jax.shard_map(
        shards, mesh=mesh, in_specs=placed, out_specs=P(("grp", "head"), None), check_vma=False
    )
```

```python
import functools

import jax
import jax.numpy as jnp
from jax import lax
from jax.experimental import pallas as pl
from jax.experimental.pallas import tpu as pltpu
from jax.sharding import PartitionSpec as P

HEADS = 8
HDIM = 128
CONV = 4
CG_STEPS = 8
PAGE = 128
CHUNK = 128
PAIR = 2 * CHUNK
EPS_NORM = 1e-06
BASE = 8
PAGE_VMEM = 53
TOKEN_VMEM = 48
F32 = jnp.float32
BF16 = jnp.bfloat16


def swap(block, axis, distance):
    size = lax.axis_size(axis)
    return lax.ppermute(block, axis, [(i, i ^ distance) for i in range(size)])


def hold(block, other):
    anywhere = pl.BlockSpec(memory_space=pl.ANY)
    return pl.pallas_call(
        lambda *refs: None,
        in_specs=[anywhere, anywhere],
        out_specs=anywhere,
        out_shape=jax.ShapeDtypeStruct(block.shape, block.dtype),
        input_output_aliases={0: 0},
        compiler_params=pltpu.CompilerParams(vmem_limit_bytes=2**20),
        name="hold",
    )(block, other)


def dot(a, b):
    return jnp.dot(a, b, preferred_element_type=F32)


def silu(a):
    return a * jax.nn.sigmoid(a)


def unit_rows(a):
    return a * lax.rsqrt(jnp.sum(a * a, axis=-1, keepdims=True) + EPS_NORM)


def block_diag(a):
    zero = jnp.zeros((a.shape[0], CHUNK), a.dtype)
    return jnp.concatenate(
        [
            jnp.concatenate([a[:, :CHUNK], zero], axis=1),
            jnp.concatenate([zero, a[:, CHUNK:]], axis=1),
        ],
        axis=0,
    )


def sums_kernel(heads, owners, slot_bits, code_hbm, pack_hbm, keys_hbm, values_hbm, prompt_hbm,
                send_gram, send_cross, keep_gram, keep_cross,
                acc_ref, keys_ref, values_ref, stored_ref, code_ref, pack_ref, list_ref,
                key_sem, value_sem, small_sem):
    pool, rows = keys_hbm.shape[0], keys_hbm.shape[1]
    mine = lax.axis_index("grp")
    load_code = pltpu.make_async_copy(code_hbm, code_ref, small_sem.at[0])
    load_prompt = pltpu.make_async_copy(prompt_hbm, stored_ref, small_sem.at[1])
    load_pack = pltpu.make_async_copy(pack_hbm, pack_ref, small_sem.at[2])
    load_code.start()
    load_pack.start()
    load_prompt.start()
    acc_ref[...] = jnp.zeros_like(acc_ref)
    load_code.wait()
    load_pack.wait()

    def load(item):
        page = list_ref[item] & 0xFFFF
        return (
            pltpu.make_async_copy(keys_hbm.at[page], keys_ref.at[item], key_sem.at[item]),
            pltpu.make_async_copy(values_hbm.at[page], values_ref.at[item], value_sem.at[item]),
        )

    def start(item, carry):
        for copy in load(item):
            copy.start()
        return carry

    wide = 8

    def note(chunk, count):
        for i in range(wide):
            page = chunk * wide + i
            code = code_ref[page]
            owner = code >> slot_bits
            length = pack_ref[owner] & 0xFFFF
            live = length - ((code & ((1 << slot_bits) - 1)) * PAGE)
            list_ref[count] = (owner << 24) | (jnp.minimum(live, PAGE) << 16) | page
            count = count + (live > 0).astype(jnp.int32)
        return count

    count = lax.fori_loop(0, pool // wide, note, jnp.int32(0))
    lax.fori_loop(0, count, start, 0)

    turn = 4
    turns = (count + (turn - 1)) >> 2

    def fill(item, carry):
        list_ref[item] = jnp.int32(owners << 24)
        return start(item, carry)

    lax.fori_loop(count, turns * turn, fill, 0)

    lane = lax.broadcasted_iota(jnp.int32, (HDIM, rows), 1)

    def one_turn(step, carry):
        for i in range(turn):
            for copy in load(step * turn + i):
                copy.wait()
        for i in range(turn):
            item = step * turn + i
            code = list_ref[item]
            owner, live = code >> 24, (code >> 16) & 0xFF
            keys = keys_ref[item]
            turned = keys.T
            zero = jnp.zeros_like(turned)
            left = jnp.concatenate(
                [
                    jnp.where((lane % heads == head) & (lane < live * heads), turned, zero)
                    for head in range(heads)
                ],
                axis=0,
            )
            acc_ref[owner] += dot(left, jnp.concatenate([keys, values_ref[item]], axis=1))
        return carry

    lax.fori_loop(0, turns, one_turn, 0)
    load_prompt.wait()
    stored = stored_ref.shape[0]

    def add_prompt(owner, carry):
        for slot in range(stored):

            @pl.when((pack_ref[owner] >> 16) == mine * stored + slot)
            def _():
                for head in range(heads):
                    at = slice(head * HDIM, (head + 1) * HDIM)
                    acc_ref[owner, at, :HDIM] += stored_ref[slot, head, 0]
                    acc_ref[owner, at, HDIM:] += stored_ref[slot, head, 1].T

        return carry

    lax.fori_loop(0, owners, add_prompt, 0)
    bit = mine & 1
    for pair in range(owners // 2):
        there, here = 2 * pair + 1 - bit, 2 * pair + bit
        send_gram[pair] = acc_ref[there, :, :HDIM].astype(BF16)
        send_cross[pair] = acc_ref[there, :, HDIM:].astype(BF16)
        keep_gram[pair] = acc_ref[here, :, :HDIM].astype(BF16)
        keep_cross[pair] = acc_ref[here, :, HDIM:].astype(BF16)


def page_sums(code, pack, slot_bits, keys, values, prompt_state, owners):
    pool, rows, _ = keys.shape
    heads = prompt_state.shape[1]
    half = (owners // 2, heads * HDIM, HDIM)
    items = pool + 4
    return pl.pallas_call(
        functools.partial(sums_kernel, heads, owners, slot_bits),
        in_specs=[pl.BlockSpec(memory_space=pl.ANY)] * 5,
        out_specs=[pl.BlockSpec(memory_space=pltpu.VMEM)] * 4,
        scratch_shapes=[
            pltpu.VMEM((owners + 1, heads * HDIM, 2 * HDIM), F32),
            pltpu.VMEM((items, rows, HDIM), BF16),
            pltpu.VMEM((items, rows, HDIM), BF16),
            pltpu.VMEM(prompt_state.shape, F32),
            pltpu.SMEM(code.shape, jnp.int32),
            pltpu.SMEM(pack.shape, jnp.int32),
            pltpu.SMEM((items,), jnp.int32),
            pltpu.SemaphoreType.DMA((items,)),
            pltpu.SemaphoreType.DMA((items,)),
            pltpu.SemaphoreType.DMA((3,)),
        ],
        out_shape=[jax.ShapeDtypeStruct(half, BF16)] * 4,
        compiler_params=pltpu.CompilerParams(vmem_limit_bytes=PAGE_VMEM * 2**20),
        cost_estimate=pl.CostEstimate(
            flops=8 * pool * rows * heads * HDIM * HDIM,
            bytes_accessed=4 * pool * rows * HDIM,
            transcendentals=0,
        ),
        name="page_sums",
    )(code, pack, keys, values, prompt_state)


def halve_kernel(keep_ref, got_ref, *refs):
    for distance, out_ref in enumerate(refs[-keep_ref.shape[0] :]):
        row = (lax.axis_index("grp") >> 1) ^ distance
        total = keep_ref[row].astype(F32) + got_ref[row].astype(F32)
        out_ref[...] = total.astype(out_ref.dtype)


def halve_sums(keep, got, after=()):
    count, rows, cols = keep.shape
    outs = [jax.ShapeDtypeStruct((rows, cols), F32 if i == 0 else BF16) for i in range(count)]
    whole = pl.BlockSpec(memory_space=pltpu.VMEM)
    return pl.pallas_call(
        halve_kernel,
        in_specs=[whole] * (2 + len(after)),
        out_specs=[whole] * count,
        out_shape=outs,
        compiler_params=pltpu.CompilerParams(vmem_limit_bytes=32 * 2**20),
        cost_estimate=pl.CostEstimate(
            flops=count * rows * cols, bytes_accessed=6 * count * rows * cols, transcendentals=0
        ),
        name="halve_sums",
    )(keep, got, *after)


def project_kernel(heads, *refs):
    head_count = HEADS // heads
    blocks = refs[:head_count]
    (gain_ref, w_hbm, wg_ref, state_ref) = refs[head_count : head_count + 4]
    ext_ref, gate_ref, normed_ref, w_ref, w_sem = refs[-5:]
    me = lax.axis_index("head")
    tok_rows = blocks[0].shape[0]
    width = w_ref.shape[1]
    columns = pl.ds(pl.multiple_of(me * width, HDIM), width)
    load = pltpu.make_async_copy(w_hbm.at[:, columns], w_ref, w_sem)
    load.start()
    chunks = tok_rows * head_count // CHUNK
    ext_ref[BASE - (CONV - 1) : BASE, :] = state_ref[0, :, columns].astype(F32)
    gate_ref[...] = jnp.zeros_like(gate_ref)
    for distance, block in enumerate(blocks):
        first = pl.multiple_of((me ^ distance) * tok_rows, tok_rows)
        wide = block[...].astype(F32)
        scale = lax.rsqrt(jnp.mean(wide * wide, axis=-1, keepdims=True) + EPS_NORM)
        normed = (wide * scale * gain_ref[...]).astype(BF16)
        normed_ref[pl.ds(first, tok_rows), :] = normed
        gate_ref[pl.ds(first, tok_rows), : 2 * HEADS] = dot(normed, wg_ref[...])
    load.wait()
    for c in range(chunks):
        rows = slice(c * CHUNK, (c + 1) * CHUNK)
        mixed = dot(normed_ref[rows, :], w_ref[...]).astype(BF16)
        ext_ref[BASE + c * CHUNK : BASE + (c + 1) * CHUNK, :] = mixed.astype(F32)


def project(blocks, norm_gain, w_qkv, w_gates, conv_state, held):
    head_count = len(blocks)
    heads = HEADS // head_count
    width = heads * 3 * HDIM
    tok_rows, model = blocks[0].shape
    length = head_count * tok_rows
    whole = pl.BlockSpec(memory_space=pltpu.VMEM)
    anywhere = pl.BlockSpec(memory_space=pl.ANY)
    return pl.pallas_call(
        functools.partial(project_kernel, heads),
        in_specs=[whole] * head_count + [whole, anywhere] + [whole] * 2 + [anywhere],
        out_specs=[anywhere, whole, whole],
        scratch_shapes=[
            pltpu.VMEM((length, model), BF16),
            pltpu.VMEM((model, width), BF16),
            pltpu.SemaphoreType.DMA,
        ],
        out_shape=[
            jax.ShapeDtypeStruct(held.shape, held.dtype),
            jax.ShapeDtypeStruct((BASE + length, width), F32),
            jax.ShapeDtypeStruct((length, HDIM), F32),
        ],
        input_output_aliases={head_count + 4: 0},
        compiler_params=pltpu.CompilerParams(vmem_limit_bytes=TOKEN_VMEM * 2**20),
        cost_estimate=pl.CostEstimate(
            flops=2 * length * model * width,
            bytes_accessed=2 * model * (length + width) + 4 * length * width,
            transcendentals=0,
        ),
        name="project",
    )(*blocks, norm_gain.reshape(1, model), w_qkv, w_gates, conv_state, held)


def token_kernel(heads, *refs):
    ext_ref, gate_ref, taps_all, rate_ref = refs[:4]
    (q_ref, k_ref, kt_ref, vt_ref, weight_ref, prefix_ref, rows_ref) = refs[4:]
    me = lax.axis_index("head")
    width = ext_ref.shape[1]
    taps_ref = taps_all[:, pl.ds(pl.multiple_of(me * width, HDIM), width)]
    base = BASE
    length = gate_ref.shape[0]
    chunks = length // CHUNK

    shift = lax.rem(HDIM - 2 * heads * me, HDIM)
    logits = pltpu.roll(gate_ref[...], shift, 1)
    lane = lax.broadcasted_iota(jnp.int32, (1, HDIM), 1)
    rate = jnp.zeros((1, HDIM), F32)
    for head in range(heads):
        here = lax.broadcasted_iota(jnp.int32, (1, HEADS), 1) == me * heads + head
        own = jnp.sum(jnp.where(here, rate_ref[...], 0.0), axis=1, keepdims=True)
        rate = jnp.where(lane == 2 * head + 1, own, rate)
    write = jax.nn.sigmoid(logits).astype(BF16).astype(F32)
    soft = jnp.maximum(logits, 0.0) + jnp.log1p(jnp.exp(-jnp.abs(logits)))
    decay = (-rate * soft).astype(BF16)
    here = lax.broadcasted_iota(jnp.int32, (CHUNK, CHUNK), 0)
    there = lax.broadcasted_iota(jnp.int32, (CHUNK, CHUNK), 1)
    lower = (here >= there).astype(F32).astype(BF16)
    cumul = [dot(lower, decay[c * CHUNK : (c + 1) * CHUNK]) for c in range(chunks)]
    turned = [block.T for block in cumul]

    for head in range(heads):
        parts = []
        for part in range(3):
            cols = slice((3 * head + part) * HDIM, (3 * head + part + 1) * HDIM)
            total = taps_ref[CONV - 1 : CONV, cols] * ext_ref[base : base + length, cols]
            for lag in range(1, CONV):
                total = total + taps_ref[CONV - 1 - lag : CONV - lag, cols] * (
                    ext_ref[base - lag : base - lag + length, cols]
                )
            parts.append(total)
        query = unit_rows(silu(parts[0])).astype(BF16)
        key = unit_rows(silu(parts[1])).astype(BF16)
        value = parts[2].astype(BF16)
        q_ref[head] = query.T
        k_ref[head] = key
        kt_ref[head] = key.T
        vt_ref[head] = value.T
        prefix = jnp.zeros((HDIM, 2 * HDIM), F32)
        so_far = jnp.zeros((1, 1), F32)
        for c in range(chunks):
            rows = slice(c * CHUNK, (c + 1) * CHUNK)
            col = cumul[c][:, 2 * head + 1 : 2 * head + 2]
            row = turned[c][2 * head + 1 : 2 * head + 2, :]
            gate = write[rows, 2 * head : 2 * head + 1]
            spread = jnp.exp(jnp.minimum(row - col, 0.0)) * gate
            half = slice((c % 2) * CHUNK, (c % 2 + 1) * CHUNK)
            weight_ref[head, c // 2, :, half] = jnp.where(here <= there, spread, 0.0)
            rows_ref[head, c // 2, 0:1, half] = jnp.exp(row)
            rows_ref[head, c // 2, 1:2, half] = jnp.broadcast_to(jnp.exp(so_far), (1, CHUNK))
            prefix_ref[head, c, :HDIM] = prefix[:, :HDIM]
            prefix_ref[head, c, HDIM:] = prefix[:, HDIM:].T
            if c + 1 < chunks:
                whole = cumul[c][CHUNK - 1 :, 2 * head + 1 : 2 * head + 2]
                carry = jnp.exp(whole - col) * gate
                both = jnp.concatenate([key[rows], value[rows]], axis=1).astype(F32)
                prefix = prefix * jnp.exp(whole) + dot(
                    kt_ref[head, :, rows], (both * carry).astype(BF16)
                )
                so_far = so_far + whole


def token_vectors(ext, gates, conv_weight, decay_rate):
    length = gates.shape[0]
    heads = ext.shape[1] // (3 * HDIM)
    chunks = length // CHUNK
    whole = pl.BlockSpec(memory_space=pltpu.VMEM)
    outs = [
        jax.ShapeDtypeStruct((heads, HDIM, length), BF16),
        jax.ShapeDtypeStruct((heads, length, HDIM), BF16),
        jax.ShapeDtypeStruct((heads, HDIM, length), BF16),
        jax.ShapeDtypeStruct((heads, HDIM, length), BF16),
        jax.ShapeDtypeStruct((heads, chunks // 2, CHUNK, PAIR), F32),
        jax.ShapeDtypeStruct((heads, chunks, 2 * HDIM, HDIM), F32),
        jax.ShapeDtypeStruct((heads, chunks // 2, 8, PAIR), F32),
    ]
    return pl.pallas_call(
        functools.partial(token_kernel, heads),
        in_specs=[whole] * 4,
        out_specs=[whole] * len(outs),
        out_shape=outs,
        compiler_params=pltpu.CompilerParams(vmem_limit_bytes=32 * 2**20),
        cost_estimate=pl.CostEstimate(
            flops=64 * ext.size, bytes_accessed=4 * ext.size, transcendentals=ext.size
        ),
        name="token_vectors",
    )(ext, gates, conv_weight, decay_rate.reshape(1, HEADS))


def read_kernel(heads, terms, ridge_ref, *refs):
    grams = refs[:terms]
    (q_ref, k_ref, kt_ref, vt_ref, weight_ref, prefix_ref, rows_ref) = refs[terms : terms + 7]
    base_ref, solved_ref, left_ref, x_ref, r_ref, d_ref = refs[-6:]
    pairs = q_ref.shape[2] // PAIR
    groups = [(head, pair) for head in range(heads) for pair in range(pairs)]
    norms = []
    for head in range(heads):
        rows = slice(head * HDIM, (head + 1) * HDIM)
        gram = grams[0][rows, :].astype(F32)
        for term in grams[1:]:
            gram = gram + term[rows, :].astype(F32)
        for pair in range(pairs):
            for side in range(2):
                c = 2 * pair + side
                half = slice(side * CHUNK, (side + 1) * CHUNK)
                scale = rows_ref[head, pair, 1:2, half]
                left_ref[head, pair, :HDIM, half] = (
                    gram * scale + prefix_ref[head, c, :HDIM]
                ).astype(BF16)
                left_ref[head, pair, HDIM:, half] = k_ref[head, c * CHUNK : (c + 1) * CHUNK]
            query = q_ref[head, :, pair * PAIR : (pair + 1) * PAIR].astype(F32)
            x_ref[head, pair] = jnp.zeros_like(query)
            r_ref[head, pair] = query
            d_ref[head, pair] = query
            norms.append(jnp.sum(query * query, axis=0, keepdims=True))

    def one_step(_, norms):
        firsts = [dot(left_ref[g], block_diag(d_ref[g].astype(BF16))) for g in groups]
        seconds = []
        for (head, pair), first in zip(groups, firsts):
            scores = (first[HDIM:] * weight_ref[head, pair]).astype(BF16)
            seconds.append(
                dot(kt_ref[head, :, pair * PAIR : (pair + 1) * PAIR], block_diag(scores))
            )
        later = []
        for (head, pair), first, second, norm in zip(groups, firsts, seconds, norms):
            direction = d_ref[head, pair]
            image = (
                rows_ref[head, pair, 0:1] * first[:HDIM] + ridge_ref[:, head : head + 1] * direction + second
            )
            alpha = norm / jnp.sum(direction * image, axis=0, keepdims=True)
            x_ref[head, pair] += alpha * direction
            residue = r_ref[head, pair] - alpha * image
            r_ref[head, pair] = residue
            norm_next = jnp.sum(residue * residue, axis=0, keepdims=True)
            d_ref[head, pair] = residue + norm_next / norm * direction
            later.append(norm_next)
        return tuple(later)

    lax.fori_loop(0, CG_STEPS, one_step, tuple(norms), unroll=4)
    for head, pair in groups:
        cols = slice(head * HDIM, (head + 1) * HDIM)
        span = slice(pair * PAIR, (pair + 1) * PAIR)
        for side in range(2):
            half = slice(side * CHUNK, (side + 1) * CHUNK)
            left_ref[head, pair, :HDIM, half] = prefix_ref[head, 2 * pair + side, HDIM:].astype(BF16)
        solved = x_ref[head, pair]
        first = dot(left_ref[head, pair], block_diag(solved.astype(BF16)))
        scores = (first[HDIM:] * weight_ref[head, pair]).astype(BF16)
        carry = rows_ref[head, pair, 0:1]
        read = carry * first[:HDIM] + dot(vt_ref[head, :, span], block_diag(scores))
        base_ref[span, cols] = read.T
        solved_ref[span, cols] = (solved * (carry * rows_ref[head, pair, 1:2])).T.astype(BF16)


def ridge_reads(ridge, grams, vectors, after=()):
    heads, _, length = vectors[0].shape
    pairs = length // PAIR
    whole = pl.BlockSpec(memory_space=pltpu.VMEM)
    state = pltpu.VMEM((heads, pairs, HDIM, PAIR), F32)
    return pl.pallas_call(
        functools.partial(read_kernel, heads, len(grams)),
        in_specs=[whole] * (1 + len(grams) + len(vectors))
        + [whole] * len(after),
        out_specs=[whole] * 2,
        out_shape=[
            jax.ShapeDtypeStruct((length, heads * HDIM), F32),
            jax.ShapeDtypeStruct((length, heads * HDIM), BF16),
        ],
        scratch_shapes=[pltpu.VMEM((heads, pairs, 2 * HDIM, PAIR), BF16), state, state, state],
        compiler_params=pltpu.CompilerParams(vmem_limit_bytes=32 * 2**20),
        cost_estimate=pl.CostEstimate(
            flops=CG_STEPS * heads * pairs * 6 * CHUNK**3 * 16,
            bytes_accessed=8 * 2**20,
            transcendentals=0,
        ),
        name="ridge_reads",
    )(ridge.reshape(1, heads), *grams, *vectors, *after)


def cross_kernel(heads, terms, *refs):
    crosses, (base_ref, solved_ref) = refs[:terms], refs[terms : terms + 2]
    outs, o_ref = refs[terms + 2 : -1], refs[-1]
    me = lax.axis_index("head")
    for head in range(heads):
        cols = slice(head * HDIM, (head + 1) * HDIM)
        cross = crosses[0][cols, :].astype(F32)
        for term in crosses[1:]:
            cross = cross + term[cols, :].astype(F32)
        read = base_ref[:, cols] + dot(solved_ref[:, cols], cross.astype(BF16))
        o_ref[:, cols] = read.astype(BF16)
    tok_rows = outs[0].shape[0]
    for distance, out_ref in enumerate(outs):
        first_row = pl.multiple_of((me ^ distance) * tok_rows, tok_rows)
        out_ref[...] = o_ref[pl.ds(first_row, tok_rows), :]


def cross_reads(crosses, base, solved, head_count):
    length, width = base.shape
    whole = pl.BlockSpec(memory_space=pltpu.VMEM)
    return pl.pallas_call(
        functools.partial(cross_kernel, width // HDIM, len(crosses)),
        in_specs=[whole] * (len(crosses) + 2),
        out_specs=[whole] * head_count,
        out_shape=[jax.ShapeDtypeStruct((length // head_count, width), BF16)] * head_count,
        scratch_shapes=[pltpu.VMEM((length, width), BF16)],
        compiler_params=pltpu.CompilerParams(vmem_limit_bytes=24 * 2**20),
        cost_estimate=pl.CostEstimate(
            flops=2 * length * width * HDIM, bytes_accessed=8 * length * width, transcendentals=0
        ),
        name="cross_reads",
    )(*crosses, base, solved)


def output_kernel(distances, start_ref, w_ref, *refs):
    out_ref = refs[-1]
    me = lax.axis_index("head")
    total = start_ref[...].astype(F32)
    for distance, part in zip(distances, refs[:-1]):
        width = part.shape[1]
        first = pl.multiple_of((me ^ distance) * width, width)
        total = total + dot(part[...], w_ref[pl.ds(first, width), :])
    out_ref[...] = total.astype(out_ref.dtype)


def output_rows(start, w_out, parts, distances, dtype):
    whole = pl.BlockSpec(memory_space=pltpu.VMEM)
    return pl.pallas_call(
        functools.partial(output_kernel, distances),
        in_specs=[whole] * (2 + len(parts)),
        out_specs=whole,
        out_shape=jax.ShapeDtypeStruct(start.shape, dtype),
        compiler_params=pltpu.CompilerParams(vmem_limit_bytes=24 * 2**20),
        cost_estimate=pl.CostEstimate(
            flops=2 * start.shape[0] * parts[0].shape[1] * len(parts) * w_out.shape[1],
            bytes_accessed=2 * w_out.size + 6 * start.size,
            transcendentals=0,
        ),
        name="output_rows",
    )(start, w_out, *parts)


def shards(
    tokens,
    norm_gain,
    w_qkv,
    w_gates,
    conv_weight,
    conv_state,
    decay_rate,
    ridge,
    w_out,
    cache_keys,
    cache_values,
    page_table,
    cache_lengths,
    group_prompt,
    prompt_state,
):
    head_count = lax.axis_size("head")
    owners = lax.axis_size("grp")
    bits = [head_count >> i for i in range(1, head_count.bit_length())]
    blocks = {0: tokens}
    for bit in bits:
        blocks[bit] = swap(tokens, "head", bit)

    pool, page, heads, _ = cache_keys.shape
    slots = page_table.shape[1]
    slot_bits = slots.bit_length() - 1
    assert slots == 1 << slot_bits
    tag = jnp.arange(owners * slots, dtype=jnp.int32).reshape(owners, slots)
    pack = cache_lengths | (group_prompt << 16)
    ids = lax.axis_index("grp").astype(jnp.int32) * pool + jnp.arange(pool, dtype=jnp.int32)
    code = jnp.sum(
        jnp.where(page_table[:, :, None] == ids, tag[:, :, None], 0), axis=(0, 1), dtype=jnp.int32
    )
    keys = cache_keys.reshape(pool, page * heads, HDIM)
    values = cache_values.reshape(pool, page * heads, HDIM)

    def scattered(parts):
        sent = [swap(parts[i], "grp", 2 * i) for i in reversed(range(1, owners // 2))]
        return [parts[0]] + sent

    send_gram, send_cross, keep_gram, keep_cross = page_sums(
        code, pack, slot_bits, keys, values, prompt_state, owners
    )
    got_gram = swap(send_gram, "grp", 1)
    for bit in bits[1:]:
        for distance in list(blocks):
            if distance and not distance & bit and distance ^ bit not in blocks:
                blocks[distance] = hold(blocks[distance], keep_gram)
                blocks[distance ^ bit] = swap(blocks[distance], "head", bit)
    blocks = [blocks[i] for i in range(head_count)]
    send_cross, ext, gates = project(blocks, norm_gain, w_qkv, w_gates, conv_state, send_cross)
    got_cross = swap(send_cross, "grp", 1)
    vectors = token_vectors(ext, gates, conv_weight, decay_rate)
    grams = halve_sums(keep_gram, got_gram, vectors[-1:])
    crosses = halve_sums(keep_cross, got_cross)
    base, solved = ridge_reads(ridge, scattered(grams), vectors, [crosses[0]])
    reads = cross_reads(scattered(crosses), base, solved, head_count)
    far = tuple(reversed(range(1, head_count)))
    parts = [swap(reads[i], "head", i) for i in far]
    total = output_rows(tokens, w_out, reads[:1], (0,), F32)
    return output_rows(total, w_out, parts, far, BF16)


def solution(mesh):
    placed = (
        P(("grp", "head"), None),
        P(),
        P(),
        P(),
        P(),
        P("grp", None, None),
        P(),
        P("head"),
        P(),
        P("grp", None, "head", None),
        P("grp", None, "head", None),
        P(),
        P(),
        P(),
        P("grp", "head", None, None, None),
    )
    return jax.shard_map(
        shards, mesh=mesh, in_specs=placed, out_specs=P(("grp", "head"), None), check_vma=False
    )
```

```python
import functools

import jax
import jax.numpy as jnp
from jax import lax
from jax.experimental import pallas as pl
from jax.experimental.pallas import tpu as pltpu
from jax.sharding import PartitionSpec as P

HEADS = 8
HDIM = 128
CONV = 4
CG_STEPS = 8
PAGE = 128
CHUNK = 128
PAIR = 2 * CHUNK
EPS_NORM = 1e-06
BASE = 8
PAGE_VMEM = 53
TOKEN_VMEM = 48
F32 = jnp.float32
BF16 = jnp.bfloat16


def swap(block, axis, distance):
    size = lax.axis_size(axis)
    return lax.ppermute(block, axis, [(i, i ^ distance) for i in range(size)])


def hold(block, other):
    anywhere = pl.BlockSpec(memory_space=pl.ANY)
    return pl.pallas_call(
        lambda *refs: None,
        in_specs=[anywhere, anywhere],
        out_specs=anywhere,
        out_shape=jax.ShapeDtypeStruct(block.shape, block.dtype),
        input_output_aliases={0: 0},
        compiler_params=pltpu.CompilerParams(vmem_limit_bytes=2**20),
        name="hold",
    )(block, other)


def dot(a, b):
    return jnp.dot(a, b, preferred_element_type=F32)


def silu(a):
    return a * jax.nn.sigmoid(a)


def unit_rows(a):
    return a * lax.rsqrt(jnp.sum(a * a, axis=-1, keepdims=True) + EPS_NORM)


def block_diag(a):
    zero = jnp.zeros((a.shape[0], CHUNK), a.dtype)
    return jnp.concatenate(
        [
            jnp.concatenate([a[:, :CHUNK], zero], axis=1),
            jnp.concatenate([zero, a[:, CHUNK:]], axis=1),
        ],
        axis=0,
    )


def sums_kernel(heads, owners, slot_bits, code_hbm, length_hbm, pick_hbm, keys_hbm, values_hbm, prompt_hbm,
                send_gram, send_cross, keep_gram, keep_cross,
                acc_ref, keys_ref, values_ref, stored_ref, code_ref, length_ref, pick_ref, hit_ref, list_ref,
                key_sem, value_sem, small_sem):
    pool, rows = keys_hbm.shape[0], keys_hbm.shape[1]
    mine = lax.axis_index("grp")
    load_code = pltpu.make_async_copy(code_hbm, code_ref, small_sem.at[0])
    load_prompt = pltpu.make_async_copy(prompt_hbm, stored_ref, small_sem.at[1])
    load_length = pltpu.make_async_copy(length_hbm, length_ref, small_sem.at[2])
    load_pick = pltpu.make_async_copy(pick_hbm, pick_ref, small_sem.at[3])
    load_code.start()
    load_length.start()
    load_pick.start()
    load_prompt.start()
    acc_ref[...] = jnp.zeros_like(acc_ref)
    load_code.wait()
    load_length.wait()
    load_pick.wait()

    def load(item):
        page = list_ref[item] & 0xFFFF
        return (
            pltpu.make_async_copy(keys_hbm.at[page], keys_ref.at[item], key_sem.at[item]),
            pltpu.make_async_copy(values_hbm.at[page], values_ref.at[item], value_sem.at[item]),
        )

    def start(item, carry):
        for copy in load(item):
            copy.start()
        return carry

    wide = 8

    def note(chunk, count):
        for i in range(wide):
            page = chunk * wide + i
            code = code_ref[page]
            owner = code >> slot_bits
            hit_ref[owner] = pick_ref[page]
            live = length_ref[page] - ((code & ((1 << slot_bits) - 1)) * PAGE)
            list_ref[count] = (owner << 24) | (jnp.minimum(live, PAGE) << 16) | page
            count = count + (live > 0).astype(jnp.int32)
        return count

    count = lax.fori_loop(0, pool // wide, note, jnp.int32(0))
    lax.fori_loop(0, count, start, 0)

    turn = 4
    turns = (count + (turn - 1)) >> 2

    def fill(item, carry):
        list_ref[item] = jnp.int32(owners << 24)
        return start(item, carry)

    lax.fori_loop(count, turns * turn, fill, 0)

    lane = lax.broadcasted_iota(jnp.int32, (HDIM, rows), 1)

    def one_turn(step, carry):
        for i in range(turn):
            for copy in load(step * turn + i):
                copy.wait()
        for i in range(turn):
            item = step * turn + i
            code = list_ref[item]
            owner, live = code >> 24, (code >> 16) & 0xFF
            keys = keys_ref[item]
            turned = keys.T
            zero = jnp.zeros_like(turned)
            left = jnp.concatenate(
                [
                    jnp.where((lane % heads == head) & (lane < live * heads), turned, zero)
                    for head in range(heads)
                ],
                axis=0,
            )
            acc_ref[owner] += dot(left, jnp.concatenate([keys, values_ref[item]], axis=1))
        return carry

    lax.fori_loop(0, turns, one_turn, 0)
    load_prompt.wait()
    stored = stored_ref.shape[0]

    def add_prompt(owner, carry):
        for slot in range(stored):

            @pl.when(hit_ref[owner] == mine * stored + slot)
            def _():
                for head in range(heads):
                    at = slice(head * HDIM, (head + 1) * HDIM)
                    acc_ref[owner, at, :HDIM] += stored_ref[slot, head, 0]
                    acc_ref[owner, at, HDIM:] += stored_ref[slot, head, 1].T

        return carry

    lax.fori_loop(0, owners, add_prompt, 0)
    bit = mine & 1
    for pair in range(owners // 2):
        there, here = 2 * pair + 1 - bit, 2 * pair + bit
        send_gram[pair] = acc_ref[there, :, :HDIM].astype(BF16)
        send_cross[pair] = acc_ref[there, :, HDIM:].astype(BF16)
        keep_gram[pair] = acc_ref[here, :, :HDIM].astype(BF16)
        keep_cross[pair] = acc_ref[here, :, HDIM:].astype(BF16)


def page_sums(maps, slot_bits, keys, values, prompt_state, owners):
    pool, rows, _ = keys.shape
    heads = prompt_state.shape[1]
    half = (owners // 2, heads * HDIM, HDIM)
    items = pool + 4
    return pl.pallas_call(
        functools.partial(sums_kernel, heads, owners, slot_bits),
        in_specs=[pl.BlockSpec(memory_space=pl.ANY)] * 6,
        out_specs=[pl.BlockSpec(memory_space=pltpu.VMEM)] * 4,
        scratch_shapes=[
            pltpu.VMEM((owners + 1, heads * HDIM, 2 * HDIM), F32),
            pltpu.VMEM((items, rows, HDIM), BF16),
            pltpu.VMEM((items, rows, HDIM), BF16),
            pltpu.VMEM(prompt_state.shape, F32),
            pltpu.SMEM((pool,), jnp.int32),
            pltpu.SMEM((pool,), jnp.int32),
            pltpu.SMEM((pool,), jnp.int32),
            pltpu.SMEM((owners,), jnp.int32),
            pltpu.SMEM((items,), jnp.int32),
            pltpu.SemaphoreType.DMA((items,)),
            pltpu.SemaphoreType.DMA((items,)),
            pltpu.SemaphoreType.DMA((4,)),
        ],
        out_shape=[jax.ShapeDtypeStruct(half, BF16)] * 4,
        compiler_params=pltpu.CompilerParams(vmem_limit_bytes=PAGE_VMEM * 2**20),
        cost_estimate=pl.CostEstimate(
            flops=8 * pool * rows * heads * HDIM * HDIM,
            bytes_accessed=4 * pool * rows * HDIM,
            transcendentals=0,
        ),
        name="page_sums",
    )(*maps, keys, values, prompt_state)


def halve_kernel(keep_ref, got_ref, *refs):
    for distance, out_ref in enumerate(refs[-keep_ref.shape[0] :]):
        row = (lax.axis_index("grp") >> 1) ^ distance
        total = keep_ref[row].astype(F32) + got_ref[row].astype(F32)
        out_ref[...] = total.astype(out_ref.dtype)


def halve_sums(keep, got, after=()):
    count, rows, cols = keep.shape
    outs = [jax.ShapeDtypeStruct((rows, cols), F32 if i == 0 else BF16) for i in range(count)]
    whole = pl.BlockSpec(memory_space=pltpu.VMEM)
    return pl.pallas_call(
        halve_kernel,
        in_specs=[whole] * (2 + len(after)),
        out_specs=[whole] * count,
        out_shape=outs,
        compiler_params=pltpu.CompilerParams(vmem_limit_bytes=32 * 2**20),
        cost_estimate=pl.CostEstimate(
            flops=count * rows * cols, bytes_accessed=6 * count * rows * cols, transcendentals=0
        ),
        name="halve_sums",
    )(keep, got, *after)


def project_kernel(heads, *refs):
    head_count = HEADS // heads
    blocks = refs[:head_count]
    (gain_ref, w_hbm, wg_ref, state_ref) = refs[head_count : head_count + 4]
    ext_ref, gate_ref, normed_ref, w_ref, w_sem = refs[-5:]
    me = lax.axis_index("head")
    tok_rows = blocks[0].shape[0]
    width = w_ref.shape[1]
    columns = pl.ds(pl.multiple_of(me * width, HDIM), width)
    load = pltpu.make_async_copy(w_hbm.at[:, columns], w_ref, w_sem)
    load.start()
    chunks = tok_rows * head_count // CHUNK
    ext_ref[BASE - (CONV - 1) : BASE, :] = state_ref[0, :, columns].astype(F32)
    gate_ref[...] = jnp.zeros_like(gate_ref)
    for distance, block in enumerate(blocks):
        first = pl.multiple_of((me ^ distance) * tok_rows, tok_rows)
        wide = block[...].astype(F32)
        scale = lax.rsqrt(jnp.mean(wide * wide, axis=-1, keepdims=True) + EPS_NORM)
        normed = (wide * scale * gain_ref[...]).astype(BF16)
        normed_ref[pl.ds(first, tok_rows), :] = normed
        gate_ref[pl.ds(first, tok_rows), : 2 * HEADS] = dot(normed, wg_ref[...])
    load.wait()
    for c in range(chunks):
        rows = slice(c * CHUNK, (c + 1) * CHUNK)
        mixed = dot(normed_ref[rows, :], w_ref[...]).astype(BF16)
        ext_ref[BASE + c * CHUNK : BASE + (c + 1) * CHUNK, :] = mixed.astype(F32)


def project(blocks, norm_gain, w_qkv, w_gates, conv_state, held):
    head_count = len(blocks)
    heads = HEADS // head_count
    width = heads * 3 * HDIM
    tok_rows, model = blocks[0].shape
    length = head_count * tok_rows
    whole = pl.BlockSpec(memory_space=pltpu.VMEM)
    anywhere = pl.BlockSpec(memory_space=pl.ANY)
    return pl.pallas_call(
        functools.partial(project_kernel, heads),
        in_specs=[whole] * head_count + [whole, anywhere] + [whole] * 2 + [anywhere],
        out_specs=[anywhere, whole, whole],
        scratch_shapes=[
            pltpu.VMEM((length, model), BF16),
            pltpu.VMEM((model, width), BF16),
            pltpu.SemaphoreType.DMA,
        ],
        out_shape=[
            jax.ShapeDtypeStruct(held.shape, held.dtype),
            jax.ShapeDtypeStruct((BASE + length, width), F32),
            jax.ShapeDtypeStruct((length, HDIM), F32),
        ],
        input_output_aliases={head_count + 4: 0},
        compiler_params=pltpu.CompilerParams(vmem_limit_bytes=TOKEN_VMEM * 2**20),
        cost_estimate=pl.CostEstimate(
            flops=2 * length * model * width,
            bytes_accessed=2 * model * (length + width) + 4 * length * width,
            transcendentals=0,
        ),
        name="project",
    )(*blocks, norm_gain.reshape(1, model), w_qkv, w_gates, conv_state, held)


def token_kernel(heads, *refs):
    ext_ref, gate_ref, taps_all, rate_ref = refs[:4]
    (q_ref, k_ref, kt_ref, vt_ref, weight_ref, prefix_ref, rows_ref) = refs[4:]
    me = lax.axis_index("head")
    width = ext_ref.shape[1]
    taps_ref = taps_all[:, pl.ds(pl.multiple_of(me * width, HDIM), width)]
    base = BASE
    length = gate_ref.shape[0]
    chunks = length // CHUNK

    shift = lax.rem(HDIM - 2 * heads * me, HDIM)
    logits = pltpu.roll(gate_ref[...], shift, 1)
    lane = lax.broadcasted_iota(jnp.int32, (1, HDIM), 1)
    rate = jnp.zeros((1, HDIM), F32)
    for head in range(heads):
        here = lax.broadcasted_iota(jnp.int32, (1, HEADS), 1) == me * heads + head
        own = jnp.sum(jnp.where(here, rate_ref[...], 0.0), axis=1, keepdims=True)
        rate = jnp.where(lane == 2 * head + 1, own, rate)
    write = jax.nn.sigmoid(logits).astype(BF16).astype(F32)
    soft = jnp.maximum(logits, 0.0) + jnp.log1p(jnp.exp(-jnp.abs(logits)))
    decay = (-rate * soft).astype(BF16)
    here = lax.broadcasted_iota(jnp.int32, (CHUNK, CHUNK), 0)
    there = lax.broadcasted_iota(jnp.int32, (CHUNK, CHUNK), 1)
    lower = (here >= there).astype(F32).astype(BF16)
    cumul = [dot(lower, decay[c * CHUNK : (c + 1) * CHUNK]) for c in range(chunks)]
    turned = [block.T for block in cumul]

    for head in range(heads):
        parts = []
        for part in range(3):
            cols = slice((3 * head + part) * HDIM, (3 * head + part + 1) * HDIM)
            total = taps_ref[CONV - 1 : CONV, cols] * ext_ref[base : base + length, cols]
            for lag in range(1, CONV):
                total = total + taps_ref[CONV - 1 - lag : CONV - lag, cols] * (
                    ext_ref[base - lag : base - lag + length, cols]
                )
            parts.append(total)
        query = unit_rows(silu(parts[0])).astype(BF16)
        key = unit_rows(silu(parts[1])).astype(BF16)
        value = parts[2].astype(BF16)
        q_ref[head] = query.T
        k_ref[head] = key
        kt_ref[head] = key.T
        vt_ref[head] = value.T
        prefix = jnp.zeros((HDIM, 2 * HDIM), F32)
        so_far = jnp.zeros((1, 1), F32)
        for c in range(chunks):
            rows = slice(c * CHUNK, (c + 1) * CHUNK)
            col = cumul[c][:, 2 * head + 1 : 2 * head + 2]
            row = turned[c][2 * head + 1 : 2 * head + 2, :]
            gate = write[rows, 2 * head : 2 * head + 1]
            spread = jnp.exp(jnp.minimum(row - col, 0.0)) * gate
            half = slice((c % 2) * CHUNK, (c % 2 + 1) * CHUNK)
            weight_ref[head, c // 2, :, half] = jnp.where(here <= there, spread, 0.0)
            rows_ref[head, c // 2, 0:1, half] = jnp.exp(row)
            rows_ref[head, c // 2, 1:2, half] = jnp.broadcast_to(jnp.exp(so_far), (1, CHUNK))
            prefix_ref[head, c, :HDIM] = prefix[:, :HDIM]
            prefix_ref[head, c, HDIM:] = prefix[:, HDIM:].T
            if c + 1 < chunks:
                whole = cumul[c][CHUNK - 1 :, 2 * head + 1 : 2 * head + 2]
                carry = jnp.exp(whole - col) * gate
                both = jnp.concatenate([key[rows], value[rows]], axis=1).astype(F32)
                prefix = prefix * jnp.exp(whole) + dot(
                    kt_ref[head, :, rows], (both * carry).astype(BF16)
                )
                so_far = so_far + whole


def token_vectors(ext, gates, conv_weight, decay_rate):
    length = gates.shape[0]
    heads = ext.shape[1] // (3 * HDIM)
    chunks = length // CHUNK
    whole = pl.BlockSpec(memory_space=pltpu.VMEM)
    outs = [
        jax.ShapeDtypeStruct((heads, HDIM, length), BF16),
        jax.ShapeDtypeStruct((heads, length, HDIM), BF16),
        jax.ShapeDtypeStruct((heads, HDIM, length), BF16),
        jax.ShapeDtypeStruct((heads, HDIM, length), BF16),
        jax.ShapeDtypeStruct((heads, chunks // 2, CHUNK, PAIR), F32),
        jax.ShapeDtypeStruct((heads, chunks, 2 * HDIM, HDIM), F32),
        jax.ShapeDtypeStruct((heads, chunks // 2, 8, PAIR), F32),
    ]
    return pl.pallas_call(
        functools.partial(token_kernel, heads),
        in_specs=[whole] * 4,
        out_specs=[whole] * len(outs),
        out_shape=outs,
        compiler_params=pltpu.CompilerParams(vmem_limit_bytes=32 * 2**20),
        cost_estimate=pl.CostEstimate(
            flops=64 * ext.size, bytes_accessed=4 * ext.size, transcendentals=ext.size
        ),
        name="token_vectors",
    )(ext, gates, conv_weight, decay_rate.reshape(1, HEADS))


def read_kernel(heads, terms, ridge_ref, *refs):
    grams = refs[:terms]
    (q_ref, k_ref, kt_ref, vt_ref, weight_ref, prefix_ref, rows_ref) = refs[terms : terms + 7]
    base_ref, solved_ref, left_ref, x_ref, r_ref, d_ref = refs[-6:]
    pairs = q_ref.shape[2] // PAIR
    groups = [(head, pair) for head in range(heads) for pair in range(pairs)]
    norms = []
    for head in range(heads):
        rows = slice(head * HDIM, (head + 1) * HDIM)
        gram = grams[0][rows, :].astype(F32)
        for term in grams[1:]:
            gram = gram + term[rows, :].astype(F32)
        for pair in range(pairs):
            for side in range(2):
                c = 2 * pair + side
                half = slice(side * CHUNK, (side + 1) * CHUNK)
                scale = rows_ref[head, pair, 1:2, half]
                left_ref[head, pair, :HDIM, half] = (
                    gram * scale + prefix_ref[head, c, :HDIM]
                ).astype(BF16)
                left_ref[head, pair, HDIM:, half] = k_ref[head, c * CHUNK : (c + 1) * CHUNK]
            query = q_ref[head, :, pair * PAIR : (pair + 1) * PAIR].astype(F32)
            x_ref[head, pair] = jnp.zeros_like(query)
            r_ref[head, pair] = query
            d_ref[head, pair] = query
            norms.append(jnp.sum(query * query, axis=0, keepdims=True))

    def one_step(_, norms):
        firsts = [dot(left_ref[g], block_diag(d_ref[g].astype(BF16))) for g in groups]
        seconds = []
        for (head, pair), first in zip(groups, firsts):
            scores = (first[HDIM:] * weight_ref[head, pair]).astype(BF16)
            seconds.append(
                dot(kt_ref[head, :, pair * PAIR : (pair + 1) * PAIR], block_diag(scores))
            )
        later = []
        for (head, pair), first, second, norm in zip(groups, firsts, seconds, norms):
            direction = d_ref[head, pair]
            image = (
                rows_ref[head, pair, 0:1] * first[:HDIM] + ridge_ref[:, head : head + 1] * direction + second
            )
            alpha = norm / jnp.sum(direction * image, axis=0, keepdims=True)
            x_ref[head, pair] += alpha * direction
            residue = r_ref[head, pair] - alpha * image
            r_ref[head, pair] = residue
            norm_next = jnp.sum(residue * residue, axis=0, keepdims=True)
            d_ref[head, pair] = residue + norm_next / norm * direction
            later.append(norm_next)
        return tuple(later)

    lax.fori_loop(0, CG_STEPS, one_step, tuple(norms), unroll=4)
    for head, pair in groups:
        cols = slice(head * HDIM, (head + 1) * HDIM)
        span = slice(pair * PAIR, (pair + 1) * PAIR)
        for side in range(2):
            half = slice(side * CHUNK, (side + 1) * CHUNK)
            left_ref[head, pair, :HDIM, half] = prefix_ref[head, 2 * pair + side, HDIM:].astype(BF16)
        solved = x_ref[head, pair]
        first = dot(left_ref[head, pair], block_diag(solved.astype(BF16)))
        scores = (first[HDIM:] * weight_ref[head, pair]).astype(BF16)
        carry = rows_ref[head, pair, 0:1]
        read = carry * first[:HDIM] + dot(vt_ref[head, :, span], block_diag(scores))
        base_ref[span, cols] = read.T
        solved_ref[span, cols] = (solved * (carry * rows_ref[head, pair, 1:2])).T.astype(BF16)


def ridge_reads(ridge, grams, vectors, after=()):
    heads, _, length = vectors[0].shape
    pairs = length // PAIR
    whole = pl.BlockSpec(memory_space=pltpu.VMEM)
    state = pltpu.VMEM((heads, pairs, HDIM, PAIR), F32)
    return pl.pallas_call(
        functools.partial(read_kernel, heads, len(grams)),
        in_specs=[whole] * (1 + len(grams) + len(vectors))
        + [whole] * len(after),
        out_specs=[whole] * 2,
        out_shape=[
            jax.ShapeDtypeStruct((length, heads * HDIM), F32),
            jax.ShapeDtypeStruct((length, heads * HDIM), BF16),
        ],
        scratch_shapes=[pltpu.VMEM((heads, pairs, 2 * HDIM, PAIR), BF16), state, state, state],
        compiler_params=pltpu.CompilerParams(vmem_limit_bytes=32 * 2**20),
        cost_estimate=pl.CostEstimate(
            flops=CG_STEPS * heads * pairs * 6 * CHUNK**3 * 16,
            bytes_accessed=8 * 2**20,
            transcendentals=0,
        ),
        name="ridge_reads",
    )(ridge.reshape(1, heads), *grams, *vectors, *after)


def cross_kernel(heads, terms, *refs):
    crosses, (base_ref, solved_ref) = refs[:terms], refs[terms : terms + 2]
    outs, o_ref = refs[terms + 2 : -1], refs[-1]
    me = lax.axis_index("head")
    for head in range(heads):
        cols = slice(head * HDIM, (head + 1) * HDIM)
        cross = crosses[0][cols, :].astype(F32)
        for term in crosses[1:]:
            cross = cross + term[cols, :].astype(F32)
        read = base_ref[:, cols] + dot(solved_ref[:, cols], cross.astype(BF16))
        o_ref[:, cols] = read.astype(BF16)
    tok_rows = outs[0].shape[0]
    for distance, out_ref in enumerate(outs):
        first_row = pl.multiple_of((me ^ distance) * tok_rows, tok_rows)
        out_ref[...] = o_ref[pl.ds(first_row, tok_rows), :]


def cross_reads(crosses, base, solved, head_count):
    length, width = base.shape
    whole = pl.BlockSpec(memory_space=pltpu.VMEM)
    return pl.pallas_call(
        functools.partial(cross_kernel, width // HDIM, len(crosses)),
        in_specs=[whole] * (len(crosses) + 2),
        out_specs=[whole] * head_count,
        out_shape=[jax.ShapeDtypeStruct((length // head_count, width), BF16)] * head_count,
        scratch_shapes=[pltpu.VMEM((length, width), BF16)],
        compiler_params=pltpu.CompilerParams(vmem_limit_bytes=24 * 2**20),
        cost_estimate=pl.CostEstimate(
            flops=2 * length * width * HDIM, bytes_accessed=8 * length * width, transcendentals=0
        ),
        name="cross_reads",
    )(*crosses, base, solved)


def output_kernel(distances, start_ref, w_ref, *refs):
    out_ref = refs[-1]
    me = lax.axis_index("head")
    total = start_ref[...].astype(F32)
    for distance, part in zip(distances, refs[:-1]):
        width = part.shape[1]
        first = pl.multiple_of((me ^ distance) * width, width)
        total = total + dot(part[...], w_ref[pl.ds(first, width), :])
    out_ref[...] = total.astype(out_ref.dtype)


def output_rows(start, w_out, parts, distances, dtype):
    whole = pl.BlockSpec(memory_space=pltpu.VMEM)
    return pl.pallas_call(
        functools.partial(output_kernel, distances),
        in_specs=[whole] * (2 + len(parts)),
        out_specs=whole,
        out_shape=jax.ShapeDtypeStruct(start.shape, dtype),
        compiler_params=pltpu.CompilerParams(vmem_limit_bytes=24 * 2**20),
        cost_estimate=pl.CostEstimate(
            flops=2 * start.shape[0] * parts[0].shape[1] * len(parts) * w_out.shape[1],
            bytes_accessed=2 * w_out.size + 6 * start.size,
            transcendentals=0,
        ),
        name="output_rows",
    )(start, w_out, *parts)


def shards(
    tokens,
    norm_gain,
    w_qkv,
    w_gates,
    conv_weight,
    conv_state,
    decay_rate,
    ridge,
    w_out,
    cache_keys,
    cache_values,
    page_table,
    cache_lengths,
    group_prompt,
    prompt_state,
):
    head_count = lax.axis_size("head")
    owners = lax.axis_size("grp")
    bits = [head_count >> i for i in range(1, head_count.bit_length())]
    blocks = {0: tokens}
    for bit in bits:
        blocks[bit] = swap(tokens, "head", bit)

    pool, page, heads, _ = cache_keys.shape
    slots = page_table.shape[1]
    slot_bits = slots.bit_length() - 1
    assert slots == 1 << slot_bits
    tag = jnp.arange(owners * slots, dtype=jnp.int32).reshape(owners, slots, 1)
    ids = lax.axis_index("grp").astype(jnp.int32) * pool + jnp.arange(pool, dtype=jnp.int32)
    match = page_table[:, :, None] == ids
    maps = [
        jnp.sum(jnp.where(match, what, 0), axis=(0, 1), dtype=jnp.int32)
        for what in (tag, cache_lengths[:, None, None], group_prompt[:, None, None])
    ]
    keys = cache_keys.reshape(pool, page * heads, HDIM)
    values = cache_values.reshape(pool, page * heads, HDIM)

    def scattered(parts):
        sent = [swap(parts[i], "grp", 2 * i) for i in reversed(range(1, owners // 2))]
        return [parts[0]] + sent

    send_gram, send_cross, keep_gram, keep_cross = page_sums(
        maps, slot_bits, keys, values, prompt_state, owners
    )
    got_gram = swap(send_gram, "grp", 1)
    for bit in bits[1:]:
        for distance in list(blocks):
            if distance and not distance & bit and distance ^ bit not in blocks:
                blocks[distance] = hold(blocks[distance], keep_gram)
                blocks[distance ^ bit] = swap(blocks[distance], "head", bit)
    blocks = [blocks[i] for i in range(head_count)]
    send_cross, ext, gates = project(blocks, norm_gain, w_qkv, w_gates, conv_state, send_cross)
    got_cross = swap(send_cross, "grp", 1)
    vectors = token_vectors(ext, gates, conv_weight, decay_rate)
    grams = halve_sums(keep_gram, got_gram, vectors[-1:])
    crosses = halve_sums(keep_cross, got_cross)
    base, solved = ridge_reads(ridge, scattered(grams), vectors, [crosses[0]])
    reads = cross_reads(scattered(crosses), base, solved, head_count)
    far = tuple(reversed(range(1, head_count)))
    parts = [swap(reads[i], "head", i) for i in far]
    total = output_rows(tokens, w_out, reads[:1], (0,), F32)
    return output_rows(total, w_out, parts, far, BF16)


def solution(mesh):
    placed = (
        P(("grp", "head"), None),
        P(),
        P(),
        P(),
        P(),
        P("grp", None, None),
        P(),
        P("head"),
        P(),
        P("grp", None, "head", None),
        P("grp", None, "head", None),
        P(),
        P(),
        P(),
        P("grp", "head", None, None, None),
    )
    return jax.shard_map(
        shards, mesh=mesh, in_specs=placed, out_specs=P(("grp", "head"), None), check_vma=False
    )
```

```python
import functools

import jax
import jax.numpy as jnp
from jax import lax
from jax.experimental import pallas as pl
from jax.experimental.pallas import tpu as pltpu
from jax.sharding import PartitionSpec as P

HEADS = 8
HDIM = 128
CONV = 4
CG_STEPS = 8
PAGE = 128
CHUNK = 128
PAIR = 2 * CHUNK
EPS_NORM = 1e-06
PAGE_VMEM = 53
TOKEN_VMEM = 48
F32 = jnp.float32
BF16 = jnp.bfloat16


def swap(block, axis, distance):
    size = lax.axis_size(axis)
    return lax.ppermute(block, axis, [(i, i ^ distance) for i in range(size)])


def hold(block, other):
    anywhere = pl.BlockSpec(memory_space=pl.ANY)
    return pl.pallas_call(
        lambda *refs: None,
        in_specs=[anywhere, anywhere],
        out_specs=anywhere,
        out_shape=jax.ShapeDtypeStruct(block.shape, block.dtype),
        input_output_aliases={0: 0},
        compiler_params=pltpu.CompilerParams(vmem_limit_bytes=2**20),
        name="hold",
    )(block, other)


def dot(a, b):
    return jnp.dot(a, b, preferred_element_type=F32)


def silu(a):
    return a * jax.nn.sigmoid(a)


def unit_rows(a):
    return a * lax.rsqrt(jnp.sum(a * a, axis=-1, keepdims=True) + EPS_NORM)


def block_diag(a):
    zero = jnp.zeros((a.shape[0], CHUNK), a.dtype)
    return jnp.concatenate(
        [
            jnp.concatenate([a[:, :CHUNK], zero], axis=1),
            jnp.concatenate([zero, a[:, CHUNK:]], axis=1),
        ],
        axis=0,
    )


def sums_kernel(heads, owners, slot_bits, code_hbm, length_hbm, pick_hbm, keys_hbm, values_hbm, prompt_hbm,
                send_gram, send_cross, keep_gram, keep_cross,
                acc_ref, keys_ref, values_ref, stored_ref, code_ref, length_ref, pick_ref, hit_ref, list_ref,
                key_sem, value_sem, small_sem):
    pool, rows = keys_hbm.shape[0], keys_hbm.shape[1]
    mine = lax.axis_index("grp")
    load_code = pltpu.make_async_copy(code_hbm, code_ref, small_sem.at[0])
    load_prompt = pltpu.make_async_copy(prompt_hbm, stored_ref, small_sem.at[1])
    load_length = pltpu.make_async_copy(length_hbm, length_ref, small_sem.at[2])
    load_pick = pltpu.make_async_copy(pick_hbm, pick_ref, small_sem.at[3])
    load_code.start()
    load_length.start()
    load_pick.start()
    load_prompt.start()
    acc_ref[...] = jnp.zeros_like(acc_ref)
    load_code.wait()
    load_length.wait()
    load_pick.wait()

    def load(item):
        page = list_ref[item] & 0xFFFF
        return (
            pltpu.make_async_copy(keys_hbm.at[page], keys_ref.at[item], key_sem.at[item]),
            pltpu.make_async_copy(values_hbm.at[page], values_ref.at[item], value_sem.at[item]),
        )

    def start(item, carry):
        for copy in load(item):
            copy.start()
        return carry

    wide = 8

    def note(chunk, count):
        for i in range(wide):
            page = chunk * wide + i
            code = code_ref[page]
            owner = code >> slot_bits
            hit_ref[owner] = pick_ref[page]
            live = length_ref[page] - ((code & ((1 << slot_bits) - 1)) * PAGE)
            list_ref[count] = (owner << 24) | (jnp.minimum(live, PAGE) << 16) | page
            count = count + (live > 0).astype(jnp.int32)
        return count

    count = lax.fori_loop(0, pool // wide, note, jnp.int32(0))
    lax.fori_loop(0, count, start, 0)

    turn = 4
    turns = (count + (turn - 1)) >> 2

    def fill(item, carry):
        list_ref[item] = jnp.int32(owners << 24)
        return start(item, carry)

    lax.fori_loop(count, turns * turn, fill, 0)

    lane = lax.broadcasted_iota(jnp.int32, (HDIM, rows), 1)

    def one_turn(step, carry):
        for i in range(turn):
            for copy in load(step * turn + i):
                copy.wait()
        for i in range(turn):
            item = step * turn + i
            code = list_ref[item]
            owner, live = code >> 24, (code >> 16) & 0xFF
            keys = keys_ref[item]
            turned = keys.T
            zero = jnp.zeros_like(turned)
            left = jnp.concatenate(
                [
                    jnp.where((lane % heads == head) & (lane < live * heads), turned, zero)
                    for head in range(heads)
                ],
                axis=0,
            )
            acc_ref[owner] += dot(left, jnp.concatenate([keys, values_ref[item]], axis=1))
        return carry

    lax.fori_loop(0, turns, one_turn, 0)
    load_prompt.wait()
    stored = stored_ref.shape[0]

    def add_prompt(owner, carry):
        for slot in range(stored):

            @pl.when(hit_ref[owner] == mine * stored + slot)
            def _():
                for head in range(heads):
                    at = slice(head * HDIM, (head + 1) * HDIM)
                    acc_ref[owner, at, :HDIM] += stored_ref[slot, head, 0]
                    acc_ref[owner, at, HDIM:] += stored_ref[slot, head, 1].T

        return carry

    lax.fori_loop(0, owners, add_prompt, 0)
    bit = mine & 1
    for pair in range(owners // 2):
        there, here = 2 * pair + 1 - bit, 2 * pair + bit
        send_gram[pair] = acc_ref[there, :, :HDIM].astype(BF16)
        send_cross[pair] = acc_ref[there, :, HDIM:].astype(BF16)
        keep_gram[pair] = acc_ref[here, :, :HDIM].astype(BF16)
        keep_cross[pair] = acc_ref[here, :, HDIM:].astype(BF16)


def page_sums(maps, slot_bits, keys, values, prompt_state, owners):
    pool, rows, _ = keys.shape
    heads = prompt_state.shape[1]
    half = (owners // 2, heads * HDIM, HDIM)
    items = pool + 4
    return pl.pallas_call(
        functools.partial(sums_kernel, heads, owners, slot_bits),
        in_specs=[pl.BlockSpec(memory_space=pl.ANY)] * 6,
        out_specs=[pl.BlockSpec(memory_space=pltpu.VMEM)] * 4,
        scratch_shapes=[
            pltpu.VMEM((owners + 1, heads * HDIM, 2 * HDIM), F32),
            pltpu.VMEM((items, rows, HDIM), BF16),
            pltpu.VMEM((items, rows, HDIM), BF16),
            pltpu.VMEM(prompt_state.shape, F32),
            pltpu.SMEM((pool,), jnp.int32),
            pltpu.SMEM((pool,), jnp.int32),
            pltpu.SMEM((pool,), jnp.int32),
            pltpu.SMEM((owners,), jnp.int32),
            pltpu.SMEM((items,), jnp.int32),
            pltpu.SemaphoreType.DMA((items,)),
            pltpu.SemaphoreType.DMA((items,)),
            pltpu.SemaphoreType.DMA((4,)),
        ],
        out_shape=[jax.ShapeDtypeStruct(half, BF16)] * 4,
        compiler_params=pltpu.CompilerParams(vmem_limit_bytes=PAGE_VMEM * 2**20),
        cost_estimate=pl.CostEstimate(
            flops=8 * pool * rows * heads * HDIM * HDIM,
            bytes_accessed=4 * pool * rows * HDIM,
            transcendentals=0,
        ),
        name="page_sums",
    )(*maps, keys, values, prompt_state)


def halve_kernel(keep_ref, got_ref, *outs):
    for distance, out_ref in enumerate(outs):
        row = (lax.axis_index("grp") >> 1) ^ distance
        total = keep_ref[row].astype(F32) + got_ref[row].astype(F32)
        out_ref[...] = total.astype(out_ref.dtype)


def halve_sums(keep, got):
    count, rows, cols = keep.shape
    outs = [jax.ShapeDtypeStruct((rows, cols), F32 if i == 0 else BF16) for i in range(count)]
    whole = pl.BlockSpec(memory_space=pltpu.VMEM)
    return pl.pallas_call(
        halve_kernel,
        in_specs=[whole, whole],
        out_specs=[whole] * count,
        out_shape=outs,
        compiler_params=pltpu.CompilerParams(vmem_limit_bytes=32 * 2**20),
        cost_estimate=pl.CostEstimate(
            flops=count * rows * cols, bytes_accessed=6 * count * rows * cols, transcendentals=0
        ),
        name="halve_sums",
    )(keep, got)


def token_kernel(heads, *refs):
    head_count = HEADS // heads
    blocks = refs[:head_count]
    (gain_ref, w_hbm, wg_ref, taps_all, state_ref, rate_ref) = refs[head_count : head_count + 6]
    (q_ref, k_ref, kt_ref, vt_ref, weight_ref, prefix_ref, rows_ref) = refs[-12:-5]
    ext_ref, gate_ref, normed_ref, w_ref, w_sem = refs[-5:]
    me = lax.axis_index("head")
    tok_rows = blocks[0].shape[0]
    width = w_ref.shape[1]
    columns = pl.ds(pl.multiple_of(me * width, HDIM), width)
    load = pltpu.make_async_copy(w_hbm.at[:, columns], w_ref, w_sem)
    load.start()
    length = tok_rows * head_count
    chunks = length // CHUNK
    base = 8
    taps_ref = taps_all[:, columns]
    ext_ref[base - (CONV - 1) : base, :] = state_ref[0, :, columns].astype(F32)
    gate_ref[...] = jnp.zeros_like(gate_ref)
    for distance, block in enumerate(blocks):
        first = pl.multiple_of((me ^ distance) * tok_rows, tok_rows)
        wide = block[...].astype(F32)
        scale = lax.rsqrt(jnp.mean(wide * wide, axis=-1, keepdims=True) + EPS_NORM)
        normed = (wide * scale * gain_ref[...]).astype(BF16)
        normed_ref[pl.ds(first, tok_rows), :] = normed
        gate_ref[pl.ds(first, tok_rows), : 2 * HEADS] = dot(normed, wg_ref[...])
    load.wait()
    for c in range(chunks):
        rows = slice(c * CHUNK, (c + 1) * CHUNK)
        mixed = dot(normed_ref[rows, :], w_ref[...]).astype(BF16)
        ext_ref[base + c * CHUNK : base + (c + 1) * CHUNK, :] = mixed.astype(F32)

    shift = lax.rem(HDIM - 2 * heads * me, HDIM)
    logits = pltpu.roll(gate_ref[...], shift, 1)
    lane = lax.broadcasted_iota(jnp.int32, (1, HDIM), 1)
    rate = jnp.zeros((1, HDIM), F32)
    for head in range(heads):
        here = lax.broadcasted_iota(jnp.int32, (1, HEADS), 1) == me * heads + head
        own = jnp.sum(jnp.where(here, rate_ref[...], 0.0), axis=1, keepdims=True)
        rate = jnp.where(lane == 2 * head + 1, own, rate)
    write = jax.nn.sigmoid(logits).astype(BF16).astype(F32)
    soft = jnp.maximum(logits, 0.0) + jnp.log1p(jnp.exp(-jnp.abs(logits)))
    decay = (-rate * soft).astype(BF16)
    here = lax.broadcasted_iota(jnp.int32, (CHUNK, CHUNK), 0)
    there = lax.broadcasted_iota(jnp.int32, (CHUNK, CHUNK), 1)
    lower = (here >= there).astype(F32).astype(BF16)
    cumul = [dot(lower, decay[c * CHUNK : (c + 1) * CHUNK]) for c in range(chunks)]
    turned = [block.T for block in cumul]

    for head in range(heads):
        parts = []
        for part in range(3):
            cols = slice((3 * head + part) * HDIM, (3 * head + part + 1) * HDIM)
            total = taps_ref[CONV - 1 : CONV, cols] * ext_ref[base : base + length, cols]
            for lag in range(1, CONV):
                total = total + taps_ref[CONV - 1 - lag : CONV - lag, cols] * (
                    ext_ref[base - lag : base - lag + length, cols]
                )
            parts.append(total)
        query = unit_rows(silu(parts[0])).astype(BF16)
        key = unit_rows(silu(parts[1])).astype(BF16)
        value = parts[2].astype(BF16)
        q_ref[head] = query.T
        k_ref[head] = key
        kt_ref[head] = key.T
        vt_ref[head] = value.T
        prefix = jnp.zeros((HDIM, 2 * HDIM), F32)
        so_far = jnp.zeros((1, 1), F32)
        for c in range(chunks):
            rows = slice(c * CHUNK, (c + 1) * CHUNK)
            col = cumul[c][:, 2 * head + 1 : 2 * head + 2]
            row = turned[c][2 * head + 1 : 2 * head + 2, :]
            gate = write[rows, 2 * head : 2 * head + 1]
            spread = jnp.exp(jnp.minimum(row - col, 0.0)) * gate
            half = slice((c % 2) * CHUNK, (c % 2 + 1) * CHUNK)
            weight_ref[head, c // 2, :, half] = jnp.where(here <= there, spread, 0.0)
            rows_ref[head, c // 2, 0:1, half] = jnp.exp(row)
            rows_ref[head, c // 2, 1:2, half] = jnp.broadcast_to(jnp.exp(so_far), (1, CHUNK))
            prefix_ref[head, c, :HDIM] = prefix[:, :HDIM]
            prefix_ref[head, c, HDIM:] = prefix[:, HDIM:].T
            if c + 1 < chunks:
                whole = cumul[c][CHUNK - 1 :, 2 * head + 1 : 2 * head + 2]
                carry = jnp.exp(whole - col) * gate
                both = jnp.concatenate([key[rows], value[rows]], axis=1).astype(F32)
                prefix = prefix * jnp.exp(whole) + dot(
                    kt_ref[head, :, rows], (both * carry).astype(BF16)
                )
                so_far = so_far + whole


def token_vectors(
    decay_rate, blocks, norm_gain, w_qkv, w_gates, conv_weight, conv_state, held
):
    head_count = len(blocks)
    heads = HEADS // head_count
    width = heads * 3 * HDIM
    tok_rows, model = blocks[0].shape
    length = head_count * tok_rows
    chunks = length // CHUNK
    whole = pl.BlockSpec(memory_space=pltpu.VMEM)
    anywhere = pl.BlockSpec(memory_space=pl.ANY)
    outs = [
        jax.ShapeDtypeStruct((heads, HDIM, length), BF16),
        jax.ShapeDtypeStruct((heads, length, HDIM), BF16),
        jax.ShapeDtypeStruct((heads, HDIM, length), BF16),
        jax.ShapeDtypeStruct((heads, HDIM, length), BF16),
        jax.ShapeDtypeStruct((heads, chunks // 2, CHUNK, PAIR), F32),
        jax.ShapeDtypeStruct((heads, chunks, 2 * HDIM, HDIM), F32),
        jax.ShapeDtypeStruct((heads, chunks // 2, 8, PAIR), F32),
    ]
    return pl.pallas_call(
        functools.partial(token_kernel, heads),
        in_specs=[whole] * head_count + [whole, anywhere] + [whole] * 4 + [anywhere],
        out_specs=[anywhere] + [whole] * len(outs),
        scratch_shapes=[
            pltpu.VMEM((8 + length, width), F32),
            pltpu.VMEM((length, HDIM), F32),
            pltpu.VMEM((length, model), BF16),
            pltpu.VMEM((model, width), BF16),
            pltpu.SemaphoreType.DMA,
        ],
        out_shape=[jax.ShapeDtypeStruct(held.shape, held.dtype)] + outs,
        input_output_aliases={head_count + 6: 0},
        compiler_params=pltpu.CompilerParams(vmem_limit_bytes=TOKEN_VMEM * 2**20),
        cost_estimate=pl.CostEstimate(
            flops=2 * length * model * width,
            bytes_accessed=2 * model * (length + width) + 4 * 2**20,
            transcendentals=length * width,
        ),
        name="token_vectors",
    )(
        *blocks,
        norm_gain.reshape(1, model),
        w_qkv,
        w_gates,
        conv_weight,
        conv_state,
        decay_rate.reshape(1, HEADS),
        held,
    )


def read_kernel(heads, terms, ridge_ref, *refs):
    grams = refs[:terms]
    (q_ref, k_ref, kt_ref, vt_ref, weight_ref, prefix_ref, rows_ref) = refs[terms : terms + 7]
    base_ref, solved_ref, left_ref, x_ref, r_ref, d_ref = refs[-6:]
    pairs = q_ref.shape[2] // PAIR
    groups = [(head, pair) for head in range(heads) for pair in range(pairs)]
    norms = []
    for head in range(heads):
        rows = slice(head * HDIM, (head + 1) * HDIM)
        gram = grams[0][rows, :].astype(F32)
        for term in grams[1:]:
            gram = gram + term[rows, :].astype(F32)
        for pair in range(pairs):
            for side in range(2):
                c = 2 * pair + side
                half = slice(side * CHUNK, (side + 1) * CHUNK)
                scale = rows_ref[head, pair, 1:2, half]
                left_ref[head, pair, :HDIM, half] = (
                    gram * scale + prefix_ref[head, c, :HDIM]
                ).astype(BF16)
                left_ref[head, pair, HDIM:, half] = k_ref[head, c * CHUNK : (c + 1) * CHUNK]
            query = q_ref[head, :, pair * PAIR : (pair + 1) * PAIR].astype(F32)
            x_ref[head, pair] = jnp.zeros_like(query)
            r_ref[head, pair] = query
            d_ref[head, pair] = query
            norms.append(jnp.sum(query * query, axis=0, keepdims=True))

    def one_step(_, norms):
        firsts = [dot(left_ref[g], block_diag(d_ref[g].astype(BF16))) for g in groups]
        seconds = []
        for (head, pair), first in zip(groups, firsts):
            scores = (first[HDIM:] * weight_ref[head, pair]).astype(BF16)
            seconds.append(
                dot(kt_ref[head, :, pair * PAIR : (pair + 1) * PAIR], block_diag(scores))
            )
        later = []
        for (head, pair), first, second, norm in zip(groups, firsts, seconds, norms):
            direction = d_ref[head, pair]
            image = (
                rows_ref[head, pair, 0:1] * first[:HDIM] + ridge_ref[:, head : head + 1] * direction + second
            )
            alpha = norm / jnp.sum(direction * image, axis=0, keepdims=True)
            x_ref[head, pair] += alpha * direction
            residue = r_ref[head, pair] - alpha * image
            r_ref[head, pair] = residue
            norm_next = jnp.sum(residue * residue, axis=0, keepdims=True)
            d_ref[head, pair] = residue + norm_next / norm * direction
            later.append(norm_next)
        return tuple(later)

    lax.fori_loop(0, CG_STEPS, one_step, tuple(norms), unroll=4)
    for head, pair in groups:
        cols = slice(head * HDIM, (head + 1) * HDIM)
        span = slice(pair * PAIR, (pair + 1) * PAIR)
        for side in range(2):
            half = slice(side * CHUNK, (side + 1) * CHUNK)
            left_ref[head, pair, :HDIM, half] = prefix_ref[head, 2 * pair + side, HDIM:].astype(BF16)
        solved = x_ref[head, pair]
        first = dot(left_ref[head, pair], block_diag(solved.astype(BF16)))
        scores = (first[HDIM:] * weight_ref[head, pair]).astype(BF16)
        carry = rows_ref[head, pair, 0:1]
        read = carry * first[:HDIM] + dot(vt_ref[head, :, span], block_diag(scores))
        base_ref[span, cols] = read.T
        solved_ref[span, cols] = (solved * (carry * rows_ref[head, pair, 1:2])).T.astype(BF16)


def ridge_reads(ridge, grams, vectors, after=()):
    heads, _, length = vectors[0].shape
    pairs = length // PAIR
    whole = pl.BlockSpec(memory_space=pltpu.VMEM)
    state = pltpu.VMEM((heads, pairs, HDIM, PAIR), F32)
    return pl.pallas_call(
        functools.partial(read_kernel, heads, len(grams)),
        in_specs=[whole] * (1 + len(grams) + len(vectors))
        + [whole] * len(after),
        out_specs=[whole] * 2,
        out_shape=[
            jax.ShapeDtypeStruct((length, heads * HDIM), F32),
            jax.ShapeDtypeStruct((length, heads * HDIM), BF16),
        ],
        scratch_shapes=[pltpu.VMEM((heads, pairs, 2 * HDIM, PAIR), BF16), state, state, state],
        compiler_params=pltpu.CompilerParams(vmem_limit_bytes=32 * 2**20),
        cost_estimate=pl.CostEstimate(
            flops=CG_STEPS * heads * pairs * 6 * CHUNK**3 * 16,
            bytes_accessed=8 * 2**20,
            transcendentals=0,
        ),
        name="ridge_reads",
    )(ridge.reshape(1, heads), *grams, *vectors, *after)


def cross_kernel(heads, terms, *refs):
    crosses, (base_ref, solved_ref) = refs[:terms], refs[terms : terms + 2]
    outs, o_ref = refs[terms + 2 : -1], refs[-1]
    me = lax.axis_index("head")
    for head in range(heads):
        cols = slice(head * HDIM, (head + 1) * HDIM)
        cross = crosses[0][cols, :].astype(F32)
        for term in crosses[1:]:
            cross = cross + term[cols, :].astype(F32)
        read = base_ref[:, cols] + dot(solved_ref[:, cols], cross.astype(BF16))
        o_ref[:, cols] = read.astype(BF16)
    tok_rows = outs[0].shape[0]
    for distance, out_ref in enumerate(outs):
        first_row = pl.multiple_of((me ^ distance) * tok_rows, tok_rows)
        out_ref[...] = o_ref[pl.ds(first_row, tok_rows), :]


def cross_reads(crosses, base, solved, head_count):
    length, width = base.shape
    whole = pl.BlockSpec(memory_space=pltpu.VMEM)
    return pl.pallas_call(
        functools.partial(cross_kernel, width // HDIM, len(crosses)),
        in_specs=[whole] * (len(crosses) + 2),
        out_specs=[whole] * head_count,
        out_shape=[jax.ShapeDtypeStruct((length // head_count, width), BF16)] * head_count,
        scratch_shapes=[pltpu.VMEM((length, width), BF16)],
        compiler_params=pltpu.CompilerParams(vmem_limit_bytes=24 * 2**20),
        cost_estimate=pl.CostEstimate(
            flops=2 * length * width * HDIM, bytes_accessed=8 * length * width, transcendentals=0
        ),
        name="cross_reads",
    )(*crosses, base, solved)


def output_kernel(distances, start_ref, w_ref, *refs):
    out_ref = refs[-1]
    me = lax.axis_index("head")
    total = start_ref[...].astype(F32)
    for distance, part in zip(distances, refs[:-1]):
        width = part.shape[1]
        first = pl.multiple_of((me ^ distance) * width, width)
        total = total + dot(part[...], w_ref[pl.ds(first, width), :])
    out_ref[...] = total.astype(out_ref.dtype)


def output_rows(start, w_out, parts, distances, dtype):
    whole = pl.BlockSpec(memory_space=pltpu.VMEM)
    return pl.pallas_call(
        functools.partial(output_kernel, distances),
        in_specs=[whole] * (2 + len(parts)),
        out_specs=whole,
        out_shape=jax.ShapeDtypeStruct(start.shape, dtype),
        compiler_params=pltpu.CompilerParams(vmem_limit_bytes=24 * 2**20),
        cost_estimate=pl.CostEstimate(
            flops=2 * start.shape[0] * parts[0].shape[1] * len(parts) * w_out.shape[1],
            bytes_accessed=2 * w_out.size + 6 * start.size,
            transcendentals=0,
        ),
        name="output_rows",
    )(start, w_out, *parts)


def shards(
    tokens,
    norm_gain,
    w_qkv,
    w_gates,
    conv_weight,
    conv_state,
    decay_rate,
    ridge,
    w_out,
    cache_keys,
    cache_values,
    page_table,
    cache_lengths,
    group_prompt,
    prompt_state,
):
    head_count = lax.axis_size("head")
    owners = lax.axis_size("grp")
    bits = [head_count >> i for i in range(1, head_count.bit_length())]
    blocks = {0: tokens}
    for bit in bits:
        blocks[bit] = swap(tokens, "head", bit)

    pool, page, heads, _ = cache_keys.shape
    slots = page_table.shape[1]
    slot_bits = slots.bit_length() - 1
    assert slots == 1 << slot_bits
    tag = jnp.arange(owners * slots, dtype=jnp.int32).reshape(owners, slots, 1)
    ids = lax.axis_index("grp").astype(jnp.int32) * pool + jnp.arange(pool, dtype=jnp.int32)
    match = page_table[:, :, None] == ids
    maps = [
        jnp.sum(jnp.where(match, what, 0), axis=(0, 1), dtype=jnp.int32)
        for what in (tag, cache_lengths[:, None, None], group_prompt[:, None, None])
    ]
    keys = cache_keys.reshape(pool, page * heads, HDIM)
    values = cache_values.reshape(pool, page * heads, HDIM)

    def scattered(parts):
        sent = [swap(parts[i], "grp", 2 * i) for i in reversed(range(1, owners // 2))]
        return [parts[0]] + sent

    send_gram, send_cross, keep_gram, keep_cross = page_sums(
        maps, slot_bits, keys, values, prompt_state, owners
    )
    got_gram = swap(send_gram, "grp", 1)
    for bit in bits[1:]:
        for distance in list(blocks):
            if distance and not distance & bit and distance ^ bit not in blocks:
                blocks[distance] = hold(blocks[distance], keep_gram)
                blocks[distance ^ bit] = swap(blocks[distance], "head", bit)
    blocks = [blocks[i] for i in range(head_count)]
    send_cross, *vectors = token_vectors(
        decay_rate, blocks, norm_gain, w_qkv, w_gates, conv_weight, conv_state, send_cross
    )
    grams = halve_sums(keep_gram, got_gram)
    crosses = halve_sums(keep_cross, swap(send_cross, "grp", 1))
    base, solved = ridge_reads(ridge, scattered(grams), vectors, [crosses[0]])
    reads = cross_reads(scattered(crosses), base, solved, head_count)
    far = tuple(reversed(range(1, head_count)))
    parts = [swap(reads[i], "head", i) for i in far]
    total = output_rows(tokens, w_out, reads[:1], (0,), F32)
    return output_rows(total, w_out, parts, far, BF16)


def solution(mesh):
    placed = (
        P(("grp", "head"), None),
        P(),
        P(),
        P(),
        P(),
        P("grp", None, None),
        P(),
        P("head"),
        P(),
        P("grp", None, "head", None),
        P("grp", None, "head", None),
        P(),
        P(),
        P(),
        P("grp", "head", None, None, None),
    )
    return jax.shard_map(
        shards, mesh=mesh, in_specs=placed, out_specs=P(("grp", "head"), None), check_vma=False
    )
```
